32 devices in a mesh: dp: 4 (over y, x), seq: 8 (over z, core).
Axes of the slice: x: 2, y: 2, z: 4, core: 2. Of those that a mesh axis runs over, the one named last changes fastest.
Arguments:
- tokens: bfloat16 [2, 4, 4096, 768], P(None, 'dp', 'seq'), may hold values from -6 to 6
- cotangent: bfloat16 [2, 4, 4096, 768], P(None, 'dp', 'seq'), may hold values from -6 to 6
- lengths: int32 [2, 4, 4], P(None, 'dp'), may hold values from 1 to 3840, as said below
- att_key: bfloat16 [768, 768], P('dp'), may hold values from -0.21875 to 0.21875
- att_value: bfloat16 [768, 768], P('dp'), may hold values from -0.21875 to 0.21875
- att_recept: bfloat16 [768, 768], P('dp'), may hold values from -0.21875 to 0.21875
- att_out: bfloat16 [768, 768], P('dp'), may hold values from -0.875 to 0.875
- ffn_key: bfloat16 [768, 3072], P('dp'), may hold values from -0.21875 to 0.21875
- ffn_value: bfloat16 [3072, 768], P('dp'), may hold values from -0.109375 to 0.109375
- ffn_recept: bfloat16 [768, 768], P('dp'), may hold values from -0.21875 to 0.21875
- params: bfloat16 [768, 11], P('dp'), may hold values from -16 to 1.5, as said below
Outputs:
- mixed: bfloat16 [2, 4, 4096, 768], P(None, 'dp', 'seq')
- tokens_grad: float32 [2, 4, 4096, 768], P(None, 'dp', 'seq')
- att_key_grad: float32 [768, 768], P(('dp', 'seq'))
- att_value_grad: float32 [768, 768], P(('dp', 'seq'))
- att_recept_grad: float32 [768, 768], P(('dp', 'seq'))
- att_out_grad: float32 [768, 768], P(('dp', 'seq'))
- ffn_key_grad: float32 [768, 3072], P(('dp', 'seq'))
- ffn_value_grad: float32 [3072, 768], P(('dp', 'seq'))
- ffn_recept_grad: float32 [768, 768], P(('dp', 'seq'))
- params_grad: float32 [768, 11], P(('dp', 'seq'))
The draws below stay inside these ranges and needn't reach their ends.
Inputs may be any that keep to these rules, and one draw needn't show every extreme that they name: `lengths`: in each micro-batch and group the 4 sequences lie end to end from position 0; one of them is 3840 long, the others at most 64; positions after the last are padding. `params`: mix columns lie in 0 to 1.
All inputs are finite; a program needn't handle non-finite values.
Results may differ from the reference program's by a relative error of at most 0.008.
Values may be sent and summed in bfloat16 or wider, within the bound.
No kernel may reach another device: no remote copies, remote signals or barrier semaphores. Data moves between devices by JAX's collectives and lax.ppermute only.
A program may use at most 256 MiB of HBM per device.

```python
import jax
import jax.numpy as jnp
from jax import lax

EMBED_SIZE = 768
FF = 3072
SPAN = 512
MB = 2
SEQS = 4
GROUP = 4096
N_DP = 4
N_SEQ = 8


def draw_lengths(key, part):
    key = jax.random.fold_in(key, 3)
    short_key, place_key = jax.random.split(key)
    count = MB * N_DP
    shorts = jax.random.randint(short_key, (count, SEQS - 1), 1, SPAN // 8 + 1)
    longest = jnp.full((count, 1), N_SEQ * SPAN - SPAN // 2, jnp.int32)
    rows = jnp.concatenate([longest, shorts.astype(jnp.int32)], axis=1)
    scores = jax.random.randint(place_key, (count, SEQS), 0, 1 << 20) * SEQS + jnp.arange(SEQS, dtype=jnp.int32)
    order = jnp.argsort(scores, axis=1)
    rows = jnp.take_along_axis(rows, order, axis=1)
    return rows.reshape(MB, N_DP, SEQS).astype(jnp.int32)


def draw_params(key, part):
    key = jax.random.fold_in(key, 7)
    lookup_projection = jax.random.split(key, 9)
    slow_share = 0.5
    initial_scaling = jax.random.uniform(lookup_projection[0], (EMBED_SIZE,), jnp.float32, 0.5, 1.5)
    initial_offset = jax.random.uniform(lookup_projection[1], (EMBED_SIZE,), jnp.float32, -0.5, 0.5)
    blend_coefficients = jax.random.uniform(lookup_projection[2], (5, EMBED_SIZE), jnp.float32, 0.05, 0.95)
    chosen = jax.random.uniform(lookup_projection[3], (EMBED_SIZE,), jnp.float32) < slow_share
    slow_rate = jnp.exp(jax.random.uniform(lookup_projection[4], (EMBED_SIZE,), jnp.float32, jnp.log(0.05 / GROUP), jnp.log(2.0 / GROUP)))
    fast_rate = jnp.exp(jax.random.uniform(lookup_projection[5], (EMBED_SIZE,), jnp.float32, jnp.log(1.0 / 50.0), jnp.log(1.0 / 20.0)))
    fading_speed = jnp.log(jnp.where(chosen, slow_rate, fast_rate))
    present_reward = jax.random.uniform(lookup_projection[6], (EMBED_SIZE,), jnp.float32, -1.0, 1.0)
    later_scaling = jax.random.uniform(lookup_projection[7], (EMBED_SIZE,), jnp.float32, 0.5, 1.5)
    later_offset = jax.random.uniform(lookup_projection[8], (EMBED_SIZE,), jnp.float32, -0.5, 0.5)
    channel_indices = [initial_scaling, initial_offset, blend_coefficients[0], blend_coefficients[1], blend_coefficients[2], fading_speed, present_reward, later_scaling, later_offset, blend_coefficients[3], blend_coefficients[4]]
    return jnp.stack(channel_indices, axis=1).astype(jnp.bfloat16)


def levels(key, extent, cuts, least, largest):
    loudness, own = 1.0, jax.random.fold_in(key, 6)
    for axis_at, blocks in cuts:
        steps = jnp.exp(jax.random.uniform(jax.random.fold_in(own, axis_at), (blocks,), jnp.float32, least / len(cuts), largest / len(cuts)))
        loudness = loudness * jnp.repeat(steps, extent[axis_at] // blocks).reshape([-1 if axis == axis_at else 1 for axis in range(len(extent))])
    return loudness


def scatter_about(rng, dims, width, bound, shards=(), kind=jnp.bfloat16):
    level = levels(rng, dims, shards, -0.22, 0.18) if shards else 1.0
    result = jax.random.normal(rng, dims, jnp.float32) * width * level
    return jnp.minimum(jnp.maximum(result, -bound), bound).astype(kind)


def setup_inputs(seed: int = 0) -> dict:
    splits = jax.random.split(jax.random.key(seed), 12)
    tokens = scatter_about(splits[0], (MB, N_DP, GROUP, EMBED_SIZE), 1.0, 6.0, ((1, 4), (2, 8)))
    cotangent = scatter_about(splits[1], (MB, N_DP, GROUP, EMBED_SIZE), 1.0, 6.0, ((1, 4), (2, 8)))
    lengths = draw_lengths(jax.random.fold_in(splits[11], 71), 0)
    att_key = scatter_about(splits[3], (EMBED_SIZE, EMBED_SIZE), EMBED_SIZE ** -0.5, 0.21875, ((0, 4),))
    att_value = scatter_about(splits[4], (EMBED_SIZE, EMBED_SIZE), EMBED_SIZE ** -0.5, 0.21875, ((0, 4),))
    att_recept = scatter_about(splits[5], (EMBED_SIZE, EMBED_SIZE), EMBED_SIZE ** -0.5, 0.21875, ((0, 4),))
    att_out = scatter_about(splits[6], (EMBED_SIZE, EMBED_SIZE), (EMBED_SIZE // 16) ** -0.5, 0.875, ((0, 4),))
    ffn_key = scatter_about(splits[7], (EMBED_SIZE, FF), EMBED_SIZE ** -0.5, 0.21875, ((0, 4),))
    ffn_value = scatter_about(splits[8], (FF, EMBED_SIZE), FF ** -0.5, 0.109375, ((0, 4),))
    ffn_recept = scatter_about(splits[9], (EMBED_SIZE, EMBED_SIZE), EMBED_SIZE ** -0.5, 0.21875, ((0, 4),))
    params = draw_params(jax.random.fold_in(splits[11], 71), 0)
    return {"tokens": tokens, "cotangent": cotangent, "lengths": lengths, "att_key": att_key, "att_value": att_value, "att_recept": att_recept, "att_out": att_out, "ffn_key": ffn_key, "ffn_value": ffn_value, "ffn_recept": ffn_recept, "params": params}


@jax.custom_vjp
def low(v):
    return lax.optimization_barrier(v.astype(jnp.bfloat16)).astype(jnp.float32)

@jax.custom_vjp
def low_back(v):
    return v

def low_keep(v):
    return (low(v), None)

def low_pass(kept, grad):
    return (grad,)

def back_keep(v):
    return (v, None)

def back_low(kept, grad):
    return (low(grad),)
low.defvjp(low_keep, low_pass)
low_back.defvjp(back_keep, back_low)
EPS = 1e-05

def matmul(left, right):
    return jnp.dot(left, right, precision=lax.Precision.HIGHEST)

def layer_norm(values, gain, bias):
    mean = lax.optimization_barrier(jnp.mean(values, axis=1, keepdims=True))
    centred = values - mean
    spread = lax.optimization_barrier(jnp.mean(centred * centred, axis=1, keepdims=True))
    return centred * lax.rsqrt(spread + EPS) * gain + bias

def stream_marks(counts):
    ends = jnp.cumsum(counts).astype(jnp.int32)
    bounds = jnp.concatenate([jnp.zeros((1,), jnp.int32), ends])
    position = jnp.arange(GROUP, dtype=jnp.int32)
    segment_beginnings = jnp.any(position[:, None] == bounds[None, :], axis=1)
    live = position < ends[-1]
    return (segment_beginnings.astype(jnp.float32), live.astype(jnp.float32))

def token_shift(hidden_rows, segment_beginnings):
    before = jnp.concatenate([jnp.zeros((1, hidden_rows.shape[1]), jnp.float32), hidden_rows[:-1]], axis=0)
    return before * (1.0 - segment_beginnings)[:, None]

def attention_recurrence(lookup_tile_entries, payload_tile_entries, segment_beginnings, fading_speed, present_reward):
    fading_speed_raw = jnp.exp(-jnp.exp(fading_speed))
    reward_coefficient = jnp.exp(present_reward)

    def advance(carry, inputs):
        num_state, den_state = carry
        key_now, payload_present, start_now = inputs
        dividend_earlier = (1.0 - start_now) * num_state
        normalizer_earlier = (1.0 - start_now) * den_state
        exponentiated_lookup = jnp.exp(key_now)
        recurrence_result = (dividend_earlier + reward_coefficient * exponentiated_lookup * payload_present) / (normalizer_earlier + reward_coefficient * exponentiated_lookup)
        return ((fading_speed_raw * dividend_earlier + exponentiated_lookup * payload_present, fading_speed_raw * normalizer_earlier + exponentiated_lookup), recurrence_result)
    zeros = jnp.zeros_like(fading_speed)
    _, recurrence_result = lax.scan(advance, (zeros, zeros), (lookup_tile_entries, payload_tile_entries, segment_beginnings))
    return recurrence_result

def stream_layer(inputs, counts, att_key, att_value, att_recept, att_out, ffn_key, ffn_value, ffn_recept, params):
    segment_beginnings, _ = stream_marks(counts)
    first = layer_norm(inputs, params[:, 0], params[:, 1])
    shifted_one = token_shift(first, segment_beginnings)
    mix_key = low(first * params[:, 2] + shifted_one * (1.0 - params[:, 2]))
    mix_value = low(first * params[:, 3] + shifted_one * (1.0 - params[:, 3]))
    mix_recept = low(first * params[:, 4] + shifted_one * (1.0 - params[:, 4]))
    lookup_tile_entries = low_back(matmul(mix_key, att_key))
    payload_tile_entries = low_back(matmul(mix_value, att_value))
    recept = low_back(matmul(mix_recept, att_recept))
    wkv = attention_recurrence(lookup_tile_entries, payload_tile_entries, segment_beginnings, params[:, 5], params[:, 6])
    gated = low(jax.nn.sigmoid(recept) * wkv)
    middle = inputs + low_back(matmul(gated, att_out))
    second = layer_norm(middle, params[:, 7], params[:, 8])
    shifted_two = token_shift(second, segment_beginnings)
    ffn_in = low(second * params[:, 9] + shifted_two * (1.0 - params[:, 9]))
    ffn_gate_in = low(second * params[:, 10] + shifted_two * (1.0 - params[:, 10]))
    inner = low_back(matmul(ffn_in, ffn_key))
    hidden = low(jnp.square(jax.nn.relu(inner)))
    carried = low_back(matmul(hidden, ffn_value))
    gate = low_back(matmul(ffn_gate_in, ffn_recept))
    return middle + jax.nn.sigmoid(gate) * carried

def reference(tokens, cotangent, lengths, att_key, att_value, att_recept, att_out, ffn_key, ffn_value, ffn_recept, params):
    weights = tuple((item.astype(jnp.float32) for item in (att_key, att_value, att_recept, att_out, ffn_key, ffn_value, ffn_recept, params)))
    streams = tokens.astype(jnp.float32).reshape(MB * N_DP, GROUP, EMBED_SIZE)
    counts = lengths.reshape(MB * N_DP, SEQS)
    layer = jax.checkpoint(stream_layer)

    def forward(inputs, *mats):

        def one_stream(pair):
            return layer(pair[0], pair[1], *mats)
        return lax.map(one_stream, (inputs, counts))
    outputs, pull = jax.vjp(forward, streams, *weights)

    def live_rows(row_counts):
        return stream_marks(row_counts)[1]
    live = lax.map(live_rows, counts)
    grad_in = cotangent.astype(jnp.float32).reshape(MB * N_DP, GROUP, EMBED_SIZE) * live[:, :, None]
    grads = pull(grad_in)
    mixed = outputs.reshape(MB, N_DP, GROUP, EMBED_SIZE).astype(jnp.bfloat16)
    tokens_grad = grads[0].reshape(MB, N_DP, GROUP, EMBED_SIZE)
    return (mixed, tokens_grad, grads[1], grads[2], grads[3], grads[4], grads[5], grads[6], grads[7], grads[8])
```

```python
import functools

import jax
import jax.numpy as jnp
from jax import lax
from jax.experimental import pallas as pl
from jax.experimental.pallas import tpu as pltpu
from jax.sharding import PartitionSpec as P

EPS = 1e-05
BF = jnp.bfloat16
F32 = jnp.float32
PAD = 16
FAR = 1 << 30
PER = 9
HEAD = 4


def bounds_of(info, batch, seqs):
    ends = [jnp.int32(0)]
    for i in range(seqs):
        ends.append(ends[-1] + info[HEAD + batch * seqs + i])
    return ends


def positions(info, row, count):
    return lax.broadcasted_iota(jnp.int32, (count, 128), 0) + (row - PAD + info[0])


def since_start(pos, bounds):
    best = jnp.full(pos.shape, FAR, jnp.int32)
    for b in bounds:
        best = jnp.where(pos >= b, jnp.minimum(best, pos - b), best)
    return best


def until_start(pos, bounds):
    best = jnp.full(pos.shape, FAR, jnp.int32)
    for b in bounds:
        best = jnp.where(pos < b, jnp.minimum(best, b - pos), best)
    return best


def wide(mask, width):
    return jnp.concatenate([mask] * (width // 128), axis=1)


def flag(cond, width):
    return wide(jnp.where(cond, 1.0, 0.0).astype(F32), width)


def rows_of(count, width):
    return wide(lax.broadcasted_iota(jnp.int32, (count, 128), 0), width)


def down(x, carry):
    rolled = pltpu.roll(x, 1, 0)
    return jnp.where(rows_of(*x.shape) == 0, carry, rolled)


def up(x, carry):
    n = x.shape[0]
    rolled = pltpu.roll(x, n - 1, 0)
    return jnp.where(rows_of(*x.shape) == n - 1, carry, rolled)


def nn(a, b):
    return jnp.dot(a, b, preferred_element_type=F32)


def nt(a, b):
    return lax.dot_general(a, b, (((1,), (1,)), ((), ())), preferred_element_type=F32)


def tn(a, b):
    return lax.dot_general(a, b, (((0,), (0,)), ((), ())), preferred_element_type=F32)


def slabs(span, body, init, reverse=False, unroll=4):
    step = 32
    many = span // step

    def one(i, carry):
        at = many - 1 - i if reverse else i
        return body(pl.multiple_of(PAD + at * step, PAD), step, True, carry)

    first, last = (PAD + span, 0) if reverse else (0, PAD + span)
    carry = body(first, PAD, False, init)
    carry = lax.fori_loop(0, many, one, carry, unroll=unroll)
    return body(last, PAD, False, carry)


def lanes(x):
    return sum(x[:, i : i + 128] for i in range(0, x.shape[1], 128))


def tile(x, i):
    return x[:, i * 128 : (i + 1) * 128]


def row_mean(ref, width):
    total = jnp.sum(ref[...], axis=1, keepdims=True) * (1.0 / width)
    return jnp.broadcast_to(total, ref.shape)


def steps_of(low, high, body, carry, reverse=False, unroll=4):
    def one(i, carry):
        return body(high - 1 - i if reverse else low + i, carry)

    count = high - low
    while count % unroll:
        unroll -= 1
    return lax.fori_loop(0, count, one, carry, unroll=unroll)


def fold(x):
    n, c = x.shape
    return jnp.sum(x.reshape(n // 8, 8, c), axis=0)


def no_start(bounds, low, high):
    hit = jnp.int32(0)
    for b in bounds:
        hit = hit | jnp.where((b > low) & (b <= high), 1, 0)
    return jnp.where(hit == 0, 1.0, 0.0).astype(F32)


def incoming(info, states, batch, bounds, speed, span, ranks, reverse):
    me, base = info[2], info[0]
    num = jnp.zeros(speed.shape, F32)
    den = jnp.zeros(speed.shape, F32)
    for k in range(1, ranks):
        other = me ^ k
        if reverse:
            gap = other - me - 1
            clear = no_start(bounds, base + span + 1, other * span + 1)
        else:
            gap = me - 1 - other
            clear = no_start(bounds, (other + 1) * span - 2, base - 2)
        use = jnp.where(gap >= 0, clear, 0.0).astype(F32)
        weight = jnp.exp(-speed * (jnp.maximum(gap, 0) * span).astype(F32)) * use
        per = sum(r.shape[0] for r in states) // ranks
        many = states[0].shape[0] // per
        at = (k % many) * per + 2 * batch
        num += weight * states[k // many][pl.ds(at, 1), :]
        den += weight * states[k // many][pl.ds(at + 1, 1), :]
    return num, den


def start_all(copies):
    for c in copies:
        c.start()


def wait_all(copies):
    for c in copies:
        c.wait()


def copies_of(info, owns, pieces, blocks, target, sems, at=0):
    d, c = info[1], info[3]
    shard = owns[0].shape[0]
    half = shard // 2
    out = []
    for k, own in enumerate(owns):
        out.append(pltpu.make_async_copy(own, target.at[k, pl.ds(pl.multiple_of(d * shard, 16), shard)], sems.at[at]))
        at += 1
    for which, arrays in enumerate(pieces):
        core = (c + which) % 2
        for mask, shift, ref in zip((1, 2, 3, 3), (0, 0, 0, half // 2), arrays):
            row = pl.multiple_of((d ^ mask) * shard + core * half + shift, 16)
            source = ref.at[blocks]
            out.append(pltpu.make_async_copy(source, target.at[:, pl.ds(row, source.shape[1])], sems.at[at]))
            at += 1
    return out


def value_copies(info, own, pieces, target, sems, at=0):
    d, c = info[1], info[3]
    half = target.shape[1] // 2
    out = [pltpu.make_async_copy(own, target.at[pl.ds(4 * d, 4)], sems.at[at])]
    at += 1
    for which, arrays in enumerate(pieces):
        core = (c + which) % 2
        for mask, shift, ref in zip((1, 2, 3, 3), (0, 0, 0, half // 2), arrays):
            place = target.at[pl.ds(4 * (d ^ mask), 4), pl.ds(pl.multiple_of(core * half + shift, 16), ref.shape[1])]
            out.append(pltpu.make_async_copy(ref.at[pl.ds(0, 4)], place, sems.at[at]))
            at += 1
    return out


def place(info, plain):
    if plain:
        return 0, 0, 0
    return info[1], info[2] // 2, info[3]


def scatter_rows(info, src, keep, send, plan, write):
    zorder, plain = plan
    d, z, c = place(info, plain)
    nz = len(zorder)
    block = src.shape[0] // (8 * nz)
    per = 4 * nz * block // 16
    groups = block // 8
    for ref, core in ((keep, c), (send, 1 - c)):
        for slab in range(per):
            parts = []
            for g in (2 * slab, 2 * slab + 1):
                i = g % groups
                q = (g // groups) % nz
                p = g // (groups * nz)
                row = ((d ^ p) * nz + (z ^ zorder[q])) * (2 * block) + core * block + i * 8
                parts.append(src[pl.ds(pl.multiple_of(row, 8), 8), :])
            write(ref, slab * 16, jnp.concatenate(parts, axis=0).astype(BF))


def mix_kernel(
    span, seqs, info, tokens, cotangent, halo, par, mix_key, mix_value, mix_recept, change, tok_ext, cot_ext, stats, held
):
    batch = pl.program_id(0)
    bounds = bounds_of(info, batch, seqs)
    gain, bias = par[0:1, :], par[1:2, :]
    mixes = (par[2:3, :], par[3:4, :], par[4:5, :])
    width = tokens.shape[3]
    mean, scale = stats.at[0, 0], stats.at[0, 1]

    def load(row, n, owned, carry):
        at = pl.ds(row, n)
        if owned:
            x, g = tokens[0, 0, pl.ds(row - PAD, n), :], cotangent[0, 0, pl.ds(row - PAD, n), :]
        else:
            low = 0 if row == 0 else PAD
            x, g = halo[0, 0, low : low + PAD, :], halo[1, 0, low : low + PAD, :]
        tok_ext[0, at, :] = x
        cot_ext[0, at, :] = g
        x = x.astype(F32)
        held[at, :] = x
        mean[at, :] = lanes(x)
        return carry

    slabs(span, load, 0)
    mean[...] = row_mean(mean, width)

    def spread(row, n, owned, carry):
        at = pl.ds(row, n)
        x = held[at, :] - wide(mean[at, :], width)
        scale[at, :] = lanes(x * x)
        return carry

    slabs(span, spread, 0)
    scale[...] = lax.rsqrt(row_mean(scale, width) + EPS)

    def body(row, n, owned, carry):
        at = pl.ds(row, n)
        normed = (held[at, :] - wide(mean[at, :], width)) * wide(scale[at, :], width)
        first = normed * gain + bias
        keep = flag(since_start(positions(info, row, n), bounds) >= 1, width)
        shifted = down(first, carry) * keep
        diff = first - shifted
        for mu, ref in zip(mixes, (mix_key, mix_value, mix_recept)):
            ref[0, at, :] = (shifted + diff * mu).astype(BF)
        change[0, at, :] = diff.astype(BF)
        return first[n - 1 : n]

    slabs(span, body, jnp.zeros((1, width), F32))


class Chunks:
    def __init__(self, info, bounds, rows, speed):
        self.size = rows // 8
        self.bounds = bounds
        self.base = info[0] - PAD
        self.row8 = lax.broadcasted_iota(jnp.int32, (8, 128), 0)
        self.start = self.row8 * self.size + self.base
        self.speed = speed
        self.tiles = speed.shape[1] // 128
        self.rate = self.split(jnp.exp(-speed))

    def split(self, row):
        return [jnp.broadcast_to(tile(row, i), (8, 128)) for i in range(self.tiles)]

    def at(self, j):
        return pl.ds(j, 8, stride=self.size)

    def keep(self, j, ahead=0):
        pos = self.start + (j + ahead)
        hit = pos == self.bounds[0]
        for b in self.bounds[1:]:
            hit = hit | (pos == b)
        return jnp.where(hit, 0.0, 1.0).astype(F32)

    def decay(self, low, high, count):
        clear = no_start(self.bounds, self.base + low, self.base + high)
        return jnp.exp(-self.speed * float(count)) * clear


def join(tiles):
    return jnp.concatenate(tiles, axis=1)


def write_state(state, batch, num, den):
    for i in range(state.shape[0] // 2):

        @pl.when(batch == i)
        def _():
            state[2 * i : 2 * i + 1, :] = num
            state[2 * i + 1 : 2 * i + 2, :] = den


def project_kernel(
    span, seqs, info, mix_key, mix_value, mix_recept, par, own_key, own_value, own_recept, *refs
):
    pieces = (refs[0:4], refs[4:8])
    exp_key, value, gate, ends, state, weights, sems = refs[8:]
    batch = pl.program_id(0)
    bounds = bounds_of(info, batch, seqs)
    rows, width = mix_key.shape[1:]

    def copies():
        return copies_of(info, (own_key, own_value, own_recept), pieces, pl.ds(0, 3), weights, sems)

    @pl.when(batch == 0)
    def _():
        start_all(copies())
        wait_all(copies())

    acts = (jnp.exp, lambda x: x, jax.nn.sigmoid)
    for k, (left, ref, act) in enumerate(zip((mix_key, mix_value, mix_recept), (exp_key, value, gate), acts)):
        for i in range(0, width, 256):
            part = act(nn(left[0], weights[k, :, i : i + 256]))
            ref[0, i // 128] = part[:, :128]
            ref[0, i // 128 + 1] = part[:, 128:]

    speed = jnp.exp(par[5:6, :])
    chunks = Chunks(info, bounds, rows, speed)
    size = chunks.size

    def step(j, carry, cut=False):
        nums, dens = carry
        at = chunks.at(j)
        keep = chunks.keep(j)
        num_out, den_out = [], []
        for i in range(chunks.tiles):
            ek = exp_key[0, i, at, :]
            if cut:
                ek = jnp.where(chunks.row8 == 0, 0.0, ek)
            factor = chunks.rate[i] * keep
            num_out.append(factor * nums[i] + ek * value[0, i, at, :])
            den_out.append(factor * dens[i] + ek)
        return tuple(num_out), tuple(den_out)

    zero = tuple(jnp.zeros((8, 128), F32) for _ in range(chunks.tiles))
    last = PAD + span - 2 - 7 * size
    carry = (zero, zero)
    for j in range(PAD - 1):
        carry = step(j, carry, cut=True)
    carry = steps_of(PAD - 1, last + 1, step, carry)
    inside = [join(c)[7:8] for c in carry]
    carry = steps_of(last + 1, size, step, carry, unroll=size)
    whole_ends = [join(c) for c in carry]
    out = []
    for k in range(2):
        ends[0, k] = whole_ends[k]
        total = whole_ends[k][0:1]
        for s in range(1, 7):
            total = whole_ends[k][s : s + 1] + chunks.decay(s * size - 1, (s + 1) * size - 1, size) * total
        out.append(inside[k] + chunks.decay(7 * size - 1, 7 * size + last, last + 1) * total)
    write_state(state, batch, *out)


def forward_scan(info, states, batch, chunks, exp_key, value, ends, span, ranks, emit):
    size, width = chunks.size, chunks.speed.shape[1]
    entering = incoming(info, states, batch, chunks.bounds, chunks.speed, span, ranks, False)
    begin = []
    for k in range(2):
        lines = [jnp.zeros((1, width), F32)]
        lines.append(ends[0, k, 0:1, :] + chunks.decay(PAD - 2, size - 1, size - PAD + 1) * entering[k])
        for s in range(1, 7):
            lines.append(ends[0, k, s : s + 1, :] + chunks.decay(s * size - 1, (s + 1) * size - 1, size) * lines[-1])
        begin.append(jnp.concatenate(lines, axis=0))
    carry = tuple(tuple(tile(b, i) for i in range(chunks.tiles)) for b in begin)

    def step(j, carry, insert=None):
        nums, dens = carry
        at = chunks.at(j)
        keep = chunks.keep(j)
        num_out, den_out = [], []
        for i in range(chunks.tiles):
            ek, v = exp_key[0, i, at, :], value[0, i, at, :]
            before_num = keep * nums[i]
            before_den = keep * dens[i]
            x, y = ek * v, ek
            emit(at, i, before_num, before_den, ek, x)
            if insert is not None:
                x = jnp.where(chunks.row8 == 0, insert[0][i], x)
                y = jnp.where(chunks.row8 == 0, insert[1][i], y)
            num_out.append(chunks.rate[i] * before_num + x)
            den_out.append(chunks.rate[i] * before_den + y)
        return tuple(num_out), tuple(den_out)

    none = [[0.0] * chunks.tiles] * 2
    for j in range(PAD - 2):
        carry = step(j, carry, none)
    carry = step(PAD - 2, carry, [chunks.split(e) for e in entering])
    steps_of(PAD - 1, size, step, carry)


def recur_kernel(span, seqs, ranks, parts, info, exp_key, value, gate, ends, tokens, par, own_out, *refs):
    states, refs = refs[:parts], refs[parts:]
    pieces = (refs[0:4], refs[4:8])
    (
        gated,
        by_num,
        by_recept,
        wkv,
        middle,
        ffn_in,
        ffn_gate_in,
        change,
        stats,
        wo,
        line_wkv,
        line_inverse,
        sems,
    ) = refs[8:]
    batch = pl.program_id(0)
    bounds = bounds_of(info, batch, seqs)
    rows, width = tokens.shape[1:]

    def copies():
        return copies_of(info, (own_out,), pieces, pl.ds(3, 1), wo, sems)

    @pl.when(batch == 0)
    def _():
        start_all(copies())

    chunks = Chunks(info, bounds, rows, jnp.exp(par[5:6, :]))
    boost = chunks.split(jnp.exp(par[6:7, :]))

    def emit(at, i, before_num, before_den, ek, x):
        inverse = 1.0 / (before_den + boost[i] * ek)
        line_inverse[i, at, :] = inverse
        line_wkv[i, at, :] = (before_num + boost[i] * x) * inverse

    forward_scan(info, states, batch, chunks, exp_key, value, ends, span, ranks, emit)

    def pack(row, n, owned, carry):
        at = pl.ds(row, n)
        out = ([], [], [], [])
        for i in range(chunks.tiles):
            w, sig = line_wkv[i, at, :], gate[0, i, at, :]
            g = w * sig
            out[0].append(g)
            out[1].append(sig * line_inverse[i, at, :])
            out[2].append(g * (1.0 - sig))
            out[3].append(w)
        for ref, tiles in zip((gated, by_num, by_recept, wkv), out):
            ref[0, at, :] = join(tiles).astype(BF)
        return carry

    slabs(span, pack, 0)

    @pl.when(batch == 0)
    def _():
        wait_all(copies())

    middle[0] = nn(gated[0], wo[0])
    gain, bias = par[7:8, :], par[8:9, :]
    mean, scale = stats.at[0, 0], stats.at[0, 1]

    def residual(row, n, owned, carry):
        at = pl.ds(row, n)
        mid = middle[0, at, :] + tokens[0, at, :].astype(F32)
        middle[0, at, :] = mid
        mean[at, :] = lanes(mid)
        return carry

    slabs(span, residual, 0)
    mean[...] = row_mean(mean, width)

    def spread(row, n, owned, carry):
        at = pl.ds(row, n)
        x = middle[0, at, :] - wide(mean[at, :], width)
        scale[at, :] = lanes(x * x)
        return carry

    slabs(span, spread, 0)
    scale[...] = lax.rsqrt(row_mean(scale, width) + EPS)

    def body(row, n, owned, carry):
        at = pl.ds(row, n)
        normed = (middle[0, at, :] - wide(mean[at, :], width)) * wide(scale[at, :], width)
        second = normed * gain + bias
        keep = flag(since_start(positions(info, row, n), bounds) >= 1, width)
        shifted = down(second, carry) * keep
        diff = second - shifted
        ffn_in[0, at, :] = (shifted + diff * par[9:10, :]).astype(BF)
        ffn_gate_in[0, at, :] = (shifted + diff * par[10:11, :]).astype(BF)
        change[0, at, :] = diff.astype(BF)
        return second[n - 1 : n]

    slabs(span, body, jnp.zeros((1, width), F32))


def hidden_kernel(info, ffn_in, own_key, *refs):
    pieces = (refs[0:4], refs[4:8])
    hidden, wk, sems = refs[8:]
    width = ffn_in.shape[2]
    tiles = wk.shape[0]

    def copies():
        owns = [own_key.at[:, pl.ds(j * width, width)] for j in range(tiles)]
        return copies_of(info, owns, pieces, pl.ds(0, tiles), wk, sems)

    @pl.when(pl.program_id(0) == 0)
    def _():
        start_all(copies())
        wait_all(copies())

    for j in range(tiles):
        for i in range(0, width, 256):
            relu = jnp.maximum(nn(ffn_in[0], wk[j, :, i : i + 256]), 0.0)
            hidden[0, :, pl.ds(j * width + i, 256)] = (relu * relu).astype(BF)


def gate_kernel(
    span, seqs, info, hidden, ffn_gate_in, middle, cotangent, own_value, own_recept, *refs
):
    pieces = (refs[0:4], refs[4:8])
    mixed, grad_carried, grad_gate, wv, wr, sems = refs[8:]
    batch = pl.program_id(0)
    bounds = bounds_of(info, batch, seqs)
    rows, width = middle.shape[1:]

    def copies():
        return (
            copies_of(info, (own_recept,), pieces, pl.ds(4, 1), wr, sems),
            value_copies(info, own_value, pieces, wv, sems, PER),
        )

    @pl.when(batch == 0)
    def _():
        for c in copies():
            start_all(c)
        wait_all(copies()[0])


    @pl.when(batch == 0)
    def _():
        wait_all(copies()[1])

    flat = wv[...].reshape(wv.shape[0] * wv.shape[1], width)
    total = bounds[-1]
    step = rows // 2
    for low in range(0, rows, step):
        gate = nn(ffn_gate_in[0, low : low + step, :], wr[0])
        carried = nn(hidden[0, low : low + step, :], flat)
        for i in range(0, step, PAD):
            row = low + i
            at = pl.ds(row, PAD)
            sig = jax.nn.sigmoid(gate[i : i + PAD])
            car = carried[i : i + PAD]
            live = flag(positions(info, row, PAD) < total, width)
            grad = cotangent[0, at, :].astype(F32) * live
            if PAD <= row < PAD + span:
                mixed[0, 0, row - PAD : row, :] = (middle[0, at, :] + sig * car).astype(BF)
            part = grad * sig
            grad_carried[0, at, :] = part.astype(BF)
            grad_gate[0, at, :] = (part * car * (1.0 - sig)).astype(BF)


def over_own(left, right, span):
    own = pl.ds(PAD, span)
    both = [jnp.concatenate([f[b, own] for b in range(f.shape[0])], axis=0) for f in (left, right)]
    return tn(*both)


def store_sixteen(ref, row, value):
    ref[row : row + 16, :] = value


def value_grad_kernel(span, plan, info, hidden, grad_carried, keep, send, total):
    zorder, plain = plan
    d, z, c = place(info, plain)
    width = total.shape[1]
    column = pl.ds(pl.multiple_of((pl.program_id(0) ^ d) * width, width), width)
    block = keep.shape[2]
    total[...] = over_own(hidden.at[:, :, column], grad_carried, span)
    for q, zr in enumerate(zorder):
        for ref, core in ((keep, c), (send, 1 - c)):
            row = pl.multiple_of(((z ^ zr) * 2 + core) * block, 8)
            ref[0, q] = total[pl.ds(row, block), :].astype(BF)


def gate_back_kernel(span, plan, info, ffn_gate_in, grad_gate, keep, send, total):
    total[...] = over_own(ffn_gate_in, grad_gate, span)
    scatter_rows(info, total, keep, send, plan, store_sixteen)


def inner_kernel(span, plan, info, _, __, hidden, grad_carried, ffn_in, own_key, own_value, *refs):
    key_pieces, value_pieces = (refs[0:4], refs[4:8]), (refs[8:12], refs[12:16])
    keep, send, grad_inner, grad_in, wk, wv, total, sems = refs[16:]
    step = pl.program_id(0)
    batches, _, width = grad_in.shape
    tiles = wk.shape[0]

    def copies():
        owns = [own_key.at[:, pl.ds(j * width, width)] for j in range(tiles)]
        return (
            value_copies(info, own_value, value_pieces, wv, sems),
            copies_of(info, owns, key_pieces, pl.ds(0, tiles), wk, sems, PER),
        )

    @pl.when(step == 0)
    def _():
        for c in copies():
            start_all(c)
        wait_all(copies()[0])

    here = pl.multiple_of(step * width, width)
    value = wv[pl.ds(4 * step, 4)].reshape(4 * wv.shape[1], width)
    for b in range(batches):
        for i in range(0, width, 256):
            back = nt(grad_carried[b], value[i : i + 256])
            at = pl.ds(here + i, 256)
            square = hidden[b, :, at].astype(F32)
            relu = square * lax.rsqrt(jnp.maximum(square, 1e-30))
            grad_inner[b, :, at] = (back * (2.0 * relu)).astype(BF)
    total[...] = over_own(ffn_in, grad_inner.at[:, :, pl.ds(here, width)], span)
    scatter_rows(info, total, keep, send, plan, store_sixteen)

    @pl.when(step == tiles - 1)
    def _():
        wait_all(copies()[1])
        right = jnp.concatenate([wk[j] for j in range(tiles)], axis=1)
        for b in range(batches):
            grad_in[b] = nt(grad_inner[b], right).astype(BF)


def attend_back_kernel(
    span,
    seqs,
    info,
    grad_gate,
    grad_in,
    change,
    middle,
    stats,
    cotangent,
    by_num,
    by_recept,
    wkv,
    par,
    own_out,
    own_gate,
    *refs,
):
    pieces, gate_pieces = (refs[0:4], refs[4:8]), (refs[8:12], refs[12:16])
    (grad_middle, grad_att, grad_recept, grad_num, grad_den, ends, state, sums, wo, wr, acc, held, back_gate, part_a, part_b, sems) = refs[16:]
    batch = pl.program_id(0)
    bounds = bounds_of(info, batch, seqs)
    rows, width = middle.shape[1:]

    def copies():
        return copies_of(info, (own_out,), pieces, pl.ds(3, 1), wo, sems, PER)

    def gate_copies():
        return copies_of(info, (own_gate,), gate_pieces, pl.ds(4, 1), wr, sems)

    @pl.when(batch == 0)
    def _():
        start_all(gate_copies())
        start_all(copies())
        acc[...] = jnp.zeros_like(acc)

    gain = par[7:8, :]
    mu, nu = par[9:10, :], par[10:11, :]
    total = bounds[-1]

    @pl.when(batch == 0)
    def _():
        wait_all(gate_copies())

    back_gate[...] = nt(grad_gate[0], wr[0])
    mean, scale = stats.at[0, 0], stats.at[0, 1]

    def normed_of(at):
        return (middle[0, at, :] - wide(mean[at, :], width)) * wide(scale[at, :], width)

    def gather(row, n, owned, carry):
        at = pl.ds(row, n)
        a, b = grad_in[0, at, :].astype(F32), back_gate[at, :]
        keep = flag(since_start(positions(info, row, n), bounds) >= 1, width)
        normed = normed_of(at)
        direct = a * mu + b * nu
        moved = (a + b - direct) * keep
        second = direct + up(moved, carry)
        if owned:
            diff = change[0, at, :].astype(F32)
            acc[0] += fold(second * normed)
            acc[1] += fold(second)
            acc[2] += fold(a * diff)
            acc[3] += fold(b * diff)
        inner = second * gain
        held[at, :] = inner
        part_a[at, :] = lanes(inner)
        part_b[at, :] = lanes(inner * normed)
        return moved[0:1]

    slabs(span, gather, jnp.zeros((1, width), F32), reverse=True)
    part_a[...] = row_mean(part_a, width)
    part_b[...] = row_mean(part_b, width)


    def apply(row, n, owned, carry):
        at = pl.ds(row, n)
        back = wide(scale[at, :], width) * (
            held[at, :] - wide(part_a[at, :], width) - normed_of(at) * wide(part_b[at, :], width)
        )
        live = flag(positions(info, row, n) < total, width)
        grad = cotangent[0, at, :].astype(F32) * live + back
        grad_middle[0, at, :] = grad
        grad_att[0, at, :] = grad.astype(BF)
        return carry

    slabs(span, apply, 0)

    @pl.when(batch == 0)
    def _():
        wait_all(copies())

    held[...] = nt(grad_att[0], wo[0])
    speed = jnp.exp(par[5:6, :])
    chunks = Chunks(info, bounds, rows, speed)
    size = chunks.size


    def point(row, n, owned, carry):
        at = pl.ds(row, n)
        back = held[at, :]
        num = back * by_num[0, at, :].astype(F32)
        den = num * wkv[0, at, :].astype(F32)
        for i in range(chunks.tiles):
            grad_num[0, i, at, :] = tile(num, i)
            grad_den[0, i, at, :] = -tile(den, i)
        grad_recept[0, at, :] = (back * by_recept[0, at, :].astype(F32)).astype(BF)
        return carry

    slabs(span, point, 0)

    def step(j, carry, cut=False):
        nums, dens = carry
        at = chunks.at(j)
        keep = chunks.keep(j, 1)
        num_out, den_out = [], []
        for i in range(chunks.tiles):
            gn, gd = grad_num[0, i, at, :], grad_den[0, i, at, :]
            if cut:
                gn, gd = jnp.where(chunks.row8 == 7, 0.0, gn), jnp.where(chunks.row8 == 7, 0.0, gd)
            factor = chunks.rate[i] * keep
            num_out.append(factor * nums[i] + gn)
            den_out.append(factor * dens[i] + gd)
        return tuple(num_out), tuple(den_out)

    zero = tuple(jnp.zeros((8, 128), F32) for _ in range(chunks.tiles))
    after = PAD + span + 1 - 7 * size
    carry = (zero, zero)
    for j in reversed(range(after, size)):
        carry = step(j, carry, cut=True)
    carry = steps_of(PAD + 1, after, step, carry, reverse=True)
    inside = [join(c)[0:1] for c in carry]
    carry = steps_of(0, PAD + 1, step, carry, reverse=True, unroll=size)
    whole_ends = [join(c) for c in carry]
    out = []
    for k in range(2):
        ends[0, k] = whole_ends[k]
        line = whole_ends[k][7:8]
        for s in range(6, 0, -1):
            line = whole_ends[k][s : s + 1] + chunks.decay(s * size, (s + 1) * size, size) * line
        out.append(inside[k] + chunks.decay(PAD + 1, size, size - PAD - 1) * line)
    write_state(state, batch, *out)

    @pl.when(batch == pl.num_programs(0) - 1)
    def _():
        sums[...] = jnp.zeros_like(sums)
        for i in range(4):
            sums[i : i + 1, :] = jnp.sum(acc[i], axis=0, keepdims=True)


def recept_kernel(span, plan, info, gated, grad_att, mix_recept, grad_recept, keep, send, total):
    def grad(left, right):
        total[...] = over_own(left, right, span)
        scatter_rows(info, total, keep, send, plan, store_sixteen)

    pl.when(pl.program_id(0) == 0)(lambda: grad(gated, grad_att))
    pl.when(pl.program_id(0) == 1)(lambda: grad(mix_recept, grad_recept))


def recur_back_kernel(
    span,
    seqs,
    ranks,
    parts,
    parts_back,
    plan,
    info,
    grad_num,
    grad_den,
    exp_key,
    value,
    ends_forward,
    ends,
    mix_key,
    mix_value,
    par,
    *refs,
):
    states_forward, states, refs = refs[:parts], refs[parts : parts + parts_back], refs[parts + parts_back :]
    grad_key, grad_value, keep, send, sums, num_prev, den_prev, line_key, line_value, total, total2, acc = refs
    batch = pl.program_id(0)
    bounds = bounds_of(info, batch, seqs)
    rows, width = mix_key.shape[1:]

    @pl.when(batch == 0)
    def _():
        acc[...] = jnp.zeros_like(acc)

    speed = jnp.exp(par[5:6, :])
    chunks = Chunks(info, bounds, rows, speed)
    size = chunks.size
    boost = chunks.split(jnp.exp(par[6:7, :]))

    def emit(at, i, before_num, before_den, ek, x):
        num_prev[i, at, :] = before_num
        den_prev[i, at, :] = before_den

    forward_scan(info, states_forward, batch, chunks, exp_key, value, ends_forward, span, ranks, emit)
    entering = incoming(info, states, batch, bounds, speed, span, ranks, True)
    after = PAD + span + 1 - 7 * size
    begin = []
    for k in range(2):
        lines = [jnp.zeros((1, width), F32)]
        lines.append(ends[0, k, 7:8, :] + chunks.decay(7 * size, 7 * size + after, after) * entering[k])
        for s in range(6, 0, -1):
            lines.append(ends[0, k, s : s + 1, :] + chunks.decay(s * size, (s + 1) * size, size) * lines[-1])
        begin.append(jnp.concatenate(lines[::-1], axis=0))
    zero = tuple(jnp.zeros((8, 128), F32) for _ in range(chunks.tiles))
    carry = tuple(tuple(tile(b, i) for i in range(chunks.tiles)) for b in begin) + (zero, zero)

    def step(j, carry, insert=None, mask=None):
        nums, dens, bonuses, decays = carry
        at = chunks.at(j)
        keep_next = chunks.keep(j, 1)
        outs = ([], [], [], [])
        for i in range(chunks.tiles):
            gn, ek, v = grad_num[0, i, at, :], exp_key[0, i, at, :], value[0, i, at, :]
            gd = grad_den[0, i, at, :]
            after_num = keep_next * nums[i]
            after_den = keep_next * dens[i]
            bek = boost[i] * ek
            bonus = bek * (v * gn + gd)
            line_key[i, at, :] = bonus + ek * (v * after_num + after_den)
            line_value[i, at, :] = bek * gn + ek * after_num
            decay = num_prev[i, at, :] * after_num + den_prev[i, at, :] * after_den
            if mask is not None:
                bonus = jnp.where(mask, bonus, 0.0)
                decay = jnp.where(mask, decay, 0.0)
            if insert is not None:
                gn = jnp.where(chunks.row8 == 7, insert[0][i], gn)
                gd = jnp.where(chunks.row8 == 7, insert[1][i], gd)
            outs[0].append(chunks.rate[i] * after_num + gn)
            outs[1].append(chunks.rate[i] * after_den + gd)
            outs[2].append(bonuses[i] + bonus)
            outs[3].append(decays[i] + decay)
        return tuple(tuple(o) for o in outs)

    none = [[0.0] * chunks.tiles] * 2
    upper = chunks.row8 < 7
    for j in reversed(range(after + 1, size)):
        carry = step(j, carry, none, upper)
    carry = step(after, carry, [chunks.split(e) for e in entering], upper)
    edge = PAD + span - 7 * size
    for j in reversed(range(edge, after)):
        carry = step(j, carry, None, upper)
    carry = steps_of(PAD, edge, step, carry, reverse=True)
    lower = chunks.row8 > 0
    carry = steps_of(0, PAD, lambda j, c: step(j, c, None, lower), carry, reverse=True)
    acc[0] += join(carry[2])
    acc[1] += join(carry[3])

    def pack(row, n, owned, carry):
        at = pl.ds(row, n)
        grad_key[0, at, :] = join([line_key[i, at, :] for i in range(chunks.tiles)]).astype(BF)
        grad_value[0, at, :] = join([line_value[i, at, :] for i in range(chunks.tiles)]).astype(BF)
        return carry

    slabs(span, pack, 0)
    own = pl.ds(PAD, span)
    key_part = tn(mix_key[0, own, :], grad_key[0, own, :])
    value_part = tn(mix_value[0, own, :], grad_value[0, own, :])

    @pl.when(batch == 0)
    def _():
        total[...] = key_part
        total2[...] = value_part

    @pl.when(batch > 0)
    def _():
        total[...] += key_part
        total2[...] += value_part

    @pl.when(batch == pl.num_programs(0) - 1)
    def _():
        sums[...] = jnp.zeros_like(sums)
        for i in range(2):
            sums[i : i + 1, :] = jnp.sum(acc[i], axis=0, keepdims=True)
        for source, low in ((total, 0), (total2, width)):

            def write(ref, row, value):
                ref[row : row + 16, low : low + width] = value

            scatter_rows(info, source, keep, send, plan, write)


def first_back_kernel(
    span,
    seqs,
    plan,
    info,
    grad_key,
    grad_value,
    grad_recept,
    tokens,
    stats,
    change,
    sums,
    sums_back,
    par,
    own_key,
    own_value,
    own_recept,
    *refs,
):
    pieces = (refs[0:4], refs[4:8])
    inners, part_ref, keep, send, weights, back_key, back_value, back_recept, acc, turned, sems = refs[8:]
    part_a, part_b = part_ref.at[0, 0], part_ref.at[0, 1]
    batch = pl.program_id(0)
    bounds = bounds_of(info, batch, seqs)
    width = tokens.shape[2]

    def copies():
        return copies_of(info, (own_key, own_value, own_recept), pieces, pl.ds(0, 3), weights, sems)

    @pl.when(batch == 0)
    def _():
        start_all(copies())
        acc[...] = jnp.zeros_like(acc)
        wait_all(copies())

    backs = (back_key, back_value, back_recept)
    for k, (grad, back) in enumerate(zip((grad_key, grad_value, grad_recept), backs)):
        back[...] = nt(grad[0], weights[k])
    gain = par[0:1, :]
    mixes = (par[2:3, :], par[3:4, :], par[4:5, :])
    mean, scale = stats.at[0, 0], stats.at[0, 1]

    def normed_of(at):
        return (tokens[0, at, :].astype(F32) - wide(mean[at, :], width)) * wide(scale[at, :], width)

    def gather(row, n, owned, carry):
        at = pl.ds(row, n)
        parts = (back_key[at, :], back_value[at, :], back_recept[at, :])
        keep = flag(since_start(positions(info, row, n), bounds) >= 1, width)
        direct = sum(g * mu for g, mu in zip(parts, mixes))
        moved = (parts[0] + parts[1] + parts[2] - direct) * keep
        if owned:
            normed = normed_of(at)
            first = direct + up(moved, carry)
            diff = change[0, at, :].astype(F32)
            acc[2] += fold(first * normed)
            acc[3] += fold(first)
            for i in range(3):
                acc[4 + i] += fold(parts[i] * diff)
            inner = first * gain
            inners[0, at, :] = inner
            part_a[at, :] = lanes(inner)
            part_b[at, :] = lanes(inner * normed)
        return moved[0:1]

    slabs(span, gather, jnp.zeros((1, width), F32), reverse=True)
    part_a[...] = row_mean(part_a, width)
    part_b[...] = row_mean(part_b, width)

    @pl.when(batch == pl.num_programs(0) - 1)
    def _():
        def final(i):
            return jnp.sum(acc[i], axis=0, keepdims=True)

        speed = jnp.exp(par[5:6, :])
        decay = sums_back[1:2, :] * jnp.exp(-speed) * -speed
        columns = [final(i) for i in (2, 3, 4, 5, 6)] + [decay, sums_back[0:1, :]]
        columns += [sums[i : i + 1, :] for i in range(4)]
        stacked = jnp.concatenate(columns + [jnp.zeros((128 - len(columns), width), F32)], axis=0)
        turned[...] = stacked.T
        scatter_rows(info, turned, keep, send, plan, store_sixteen)


def tokens_grad_kernel(span, info, inners, parts, tokens, stats, grad_middle, tokens_grad):
    width = inners.shape[2]
    mean, scale = stats.at[0, 0], stats.at[0, 1]
    part_a, part_b = parts.at[0, 0], parts.at[0, 1]

    def apply(row, n, owned, carry):
        if owned:
            at = pl.ds(row, n)
            rate = wide(scale[at, :], width)
            normed = (tokens[0, at, :].astype(F32) - wide(mean[at, :], width)) * rate
            back = rate * (inners[0, at, :] - wide(part_a[at, :], width) - normed * wide(part_b[at, :], width))
            tokens_grad[0, 0, pl.ds(row - PAD, n), :] = grad_middle[0, at, :] + back
        return carry

    slabs(span, apply, 0)


def swap(x, axis, mask):
    size = lax.axis_size(axis)
    if mask == "next":
        return lax.ppermute(x, axis, [(i, i + 1) for i in range(size - 1)])
    if mask == "last":
        return lax.ppermute(x, axis, [(i + 1, i) for i in range(size - 1)])
    return lax.ppermute(x, axis, [(i, i ^ mask) for i in range(size)])


def add(terms):
    return sum(t.astype(F32) for t in terms)


def hold(x, deps):
    return lax.optimization_barrier((x,) + tuple(deps))[0] if deps else x


def launch(deps, *items):
    items = [item for item in items if item.sends()]
    sends = [s for item in items for s in item.sends()]
    if not sends:
        return list(deps)
    held = lax.optimization_barrier(tuple(s[0] for s in sends) + tuple(deps))
    came = [swap(x, axis, mask) for x, (_, axis, mask) in zip(held, sends)]
    left = list(came)
    for item in items:
        count = len(item.sends())
        item.receive(left[:count])
        left = left[count:]
    return came


class Gather:
    def __init__(self, blocks, core):
        half = blocks.shape[1] // 2
        mine = lax.dynamic_slice_in_dim(blocks, core * half, half, axis=1)
        self.next = [(mine, "dp", 1), (mine, "dp", 2)]
        self.stage = 0

    def sends(self):
        return self.next

    def receive(self, came):
        if self.stage == 0:
            x, y = came
            cut = x.shape[1] // 2
            self.mine = [x, y]
            self.next = [(x[:, :cut], "dp", 2), (y[:, cut:], "dp", 1), (x, "seq", 1), (y, "seq", 1)]
        elif self.stage == 1:
            self.mine += came[:2]
            self.other = came[2:]
            self.next = [(p, "seq", 1) for p in came[:2]]
        else:
            self.pieces = self.mine + self.other + came
            self.next = []
        self.stage += 1


class Table:
    def __init__(self, params):
        self.own = jnp.pad(params.T, ((0, 16 - params.shape[1]), (0, 0)))

    def sends(self):
        return [(self.own, "dp", mask) for mask in (1, 2, 3)]

    def receive(self, came):
        d = lax.axis_index("dp")
        a = [self.own] + came
        a = [jnp.where(d % 2 == 1, a[i ^ 1], a[i]) for i in range(4)]
        a = [jnp.where(d // 2 == 1, a[i ^ 2], a[i]) for i in range(4)]
        self.whole = jnp.concatenate(a, axis=1).astype(F32)


class States:
    def __init__(self, state):
        self.parts = [state]
        self.mask = 1

    def sends(self):
        return [(self.parts[0], "seq", self.mask)] if self.mask < lax.axis_size("seq") else []

    def receive(self, came):
        self.parts = self.parts + came
        self.mask *= 2
        if self.sends():
            self.parts = [jnp.concatenate(self.parts, axis=0)]


class Halo:
    def __init__(self, tokens, cotangent):
        span = tokens.shape[2]
        toks, cots = tokens[:, 0], cotangent[:, 0]
        self.next = [(toks[:, span - 2 :], "seq", "next"), (jnp.stack([toks[:, :2], cots[:, :2]]), "seq", "last")]

    def sends(self):
        return self.next

    def receive(self, came):
        before, after = came
        blank = jnp.zeros(after.shape[:2] + (PAD - 2,) + after.shape[3:], BF)
        before = jnp.stack([before, jnp.zeros_like(before)])
        self.rows = jnp.concatenate([blank, before, after, blank], axis=2)


class Core:
    def __init__(self, keep, send, plain):
        self.keep, self.send, self.plain = keep, send, plain

    def sends(self):
        return [] if self.plain else [(self.send, "seq", 1)]

    def receive(self, came):
        self.terms = [self.keep, came[0]]

    def whole(self):
        full = jnp.stack([self.keep, self.send], axis=1).reshape(-1, self.keep.shape[-1]).astype(F32)
        return lax.psum_scatter(full, ("dp", "seq"), scatter_dimension=0, tiled=True)


class Quarter:
    def __init__(self, *cores):
        self.cores = cores
        self.rows = cores[0].keep.shape[1]
        self.plain = cores[0].plain
        self.came = []

    def value(self, y, x, rows):
        p = 2 * y + x if isinstance(x, int) and isinstance(y, int) else slice(1, None, 2) if x == 1 else slice(2, None)
        return jnp.concatenate([add([t[p, rows] for t in c.terms]) for c in self.cores], axis=-1)

    def sends(self):
        half = self.rows // 2
        low, high = slice(0, half), slice(half, None)
        if self.plain or len(self.came) == 2:
            return []
        if not self.came:
            return [(self.value(None, 1, low).astype(BF), "dp", 1), (self.value(1, None, high).astype(BF), "dp", 2)]
        left, right = self.came[0]
        return [
            ((self.value(1, 0, low) + left[1].astype(F32)).astype(BF), "dp", 2),
            ((self.value(0, 1, high) + right[1].astype(F32)).astype(BF), "dp", 1),
        ]

    def receive(self, came):
        self.came.append(came)

    def final(self, rows):
        half = self.rows // 2
        side = 0 if rows.start < half else 1
        near = slice(rows.start - side * half, rows.stop - side * half)
        return self.value(0, 0, rows) + self.came[0][side][0][near].astype(F32) + self.came[1][side][near].astype(F32)


class SmallQuarter(Quarter):
    def sends(self):
        if self.plain or self.came:
            return []
        return [(self.value(p // 2, p % 2, slice(None)).astype(BF), "dp", p) for p in (1, 2, 3)]

    def final(self, rows):
        return self.value(0, 0, rows) + add([t[rows] for t in self.came[0]])


class Finish:
    def __init__(self, *quarters):
        self.quarters = quarters
        self.plain = quarters[0].plain
        self.count = 1 if self.plain else lax.axis_size("seq") // 2
        self.block = quarters[0].rows // self.count
        self.came = None
        if self.plain:
            self.total = jnp.concatenate([c.whole() for q in quarters for c in q.cores], axis=-1)

    def value(self, k):
        rows = slice(k * self.block, (k + 1) * self.block)
        return jnp.concatenate([q.final(rows) for q in self.quarters], axis=-1)

    def sends(self):
        if self.plain or self.came:
            return []
        return [(self.value(k).astype(BF), "seq", 2 * k) for k in range(1, self.count)]

    def receive(self, came):
        self.came = came
        self.total = self.value(0) + add(came)


ANY = pl.BlockSpec(memory_space=pl.ANY)
SMEM = pl.BlockSpec(memory_space=pltpu.SMEM)


def shape(s, dtype):
    return jax.ShapeDtypeStruct(s, dtype)


BATCH = "batch"
VMEM = pl.BlockSpec(memory_space=pltpu.VMEM)


def call(name, kernel, grid, ins, outs, scratch, mib, deps=(), aliases=None):
    ins = [(hold(ins[0][0], deps), ins[0][1])] + ins[1:]
    views = [i for i, (_, spec) in enumerate(ins + outs) if spec is BATCH]

    def run(*refs):
        refs = list(refs)
        for i in views:
            refs[i] = refs[i].at[pl.ds(pl.program_id(0), 1)]
        kernel(*refs)

    def spec_of(spec):
        return VMEM if spec is BATCH else spec

    return pl.pallas_call(
        run,
        grid=grid,
        in_specs=[spec_of(s) for _, s in ins],
        out_specs=[spec_of(s) for _, s in outs],
        out_shape=[a for a, _ in outs],
        scratch_shapes=scratch,
        input_output_aliases=aliases or {},
        compiler_params=pltpu.CompilerParams(vmem_limit_bytes=mib * 2**20),
        name=name,
    )(*[a for a, _ in ins])


def body(
    tokens,
    cotangent,
    lengths,
    att_key,
    att_value,
    att_recept,
    att_out,
    ffn_key,
    ffn_value,
    ffn_recept,
    params,
):
    batches, _, span, width = tokens.shape
    seqs = lengths.shape[2]
    ff = ffn_key.shape[1]
    tiles = ff // width
    ranks = lax.axis_size("seq")
    rows = span + 2 * PAD
    d, s = lax.axis_index("dp"), lax.axis_index("seq")
    core = s % 2
    at = lax.iota(jnp.int32, HEAD + batches * seqs)
    info = jnp.pad(lengths.reshape(batches * seqs), (HEAD, 0))
    for i, number in enumerate((s * span, d, s, core)):
        info = jnp.where(at == i, number, info)
    shard = att_key.shape[0]
    group_a = Gather(jnp.stack([att_key, att_value, att_recept, att_out]), core)
    group_b = Gather(jnp.stack([ffn_key[:, j * width : (j + 1) * width] for j in range(tiles)]), core)
    group_c = Gather(jnp.concatenate([ffn_value.reshape(-1, shard, width), ffn_recept[None]], axis=0), core)
    table = Table(params)

    edge = Halo(tokens, cotangent)
    came = launch((), group_a, edge, table)
    halo = edge.rows
    par = table.whole

    ext = (batches, rows, width)
    ext_f, ext_b = shape(ext, F32), shape(ext, BF)
    line_f = shape((batches, width // 128, rows, 128), F32)
    stats_shape = shape((batches, 2, rows, 128), F32)
    ends_shape = shape((batches, 2, 8, width), F32)
    wide_b = shape((batches, rows, ff), BF)
    square = pltpu.VMEM((1, width, width), BF)
    three = pltpu.VMEM((3, width, width), BF)
    square_f = pltpu.VMEM((width, width), F32)
    block_f = pltpu.VMEM((rows, width), F32)
    block_line = pltpu.VMEM((width // 128, rows, 128), F32)
    part = pltpu.VMEM((rows, 128), F32)

    def sems(n):
        return pltpu.SemaphoreType.DMA((n,))

    def refs(group):
        return [(p, ANY) for p in group.pieces]

    info_in = (info, SMEM)

    came = launch(came, group_a)
    mix_key, mix_value, mix_recept, change_one, tok_ext, cot_ext, stats_one = call(
        "mix",
        functools.partial(mix_kernel, span, seqs),
        (batches,),
        [
            info_in,
            (tokens, BATCH),
            (cotangent, BATCH),
            (halo, pl.BlockSpec((2, 1, 2 * PAD, width), lambda i: (0, i, 0, 0))),
            (par, VMEM),
        ],
        [(ext_b, BATCH)] * 6 + [(stats_shape, BATCH)],
        [block_f],
        9,
    )
    came = launch(came + [stats_one], group_a)
    deps = came
    came = launch(deps, group_b)
    state_shape = shape((2 * batches, width), F32)
    exp_key, value, gate_one, ends, state = call(
        "project",
        functools.partial(project_kernel, span, seqs),
        (batches,),
        [info_in]
        + [(a, BATCH) for a in (mix_key, mix_value, mix_recept)]
        + [(par, VMEM), (att_key, ANY), (att_value, ANY), (att_recept, ANY)]
        + refs(group_a),
        [(line_f, BATCH)] * 3
        + [(ends_shape, BATCH), (state_shape, VMEM)],
        [three, sems(PER + 2)],
        8,
        deps,
    )
    exchange = States(state)
    came = launch(came, exchange)
    came = launch(came, exchange, group_b)
    while exchange.sends():
        came = launch(came, exchange)
    states = exchange.parts
    deps = came
    came = launch(deps, group_b, group_c)
    gated, by_num, by_recept, wkv, middle, ffn_in, ffn_gate_in, change_two, stats_two = call(
        "recur",
        functools.partial(recur_kernel, span, seqs, ranks, len(states)),
        (batches,),
        [info_in]
        + [(a, BATCH) for a in (exp_key, value, gate_one)]
        + [(ends, BATCH), (tok_ext, BATCH)]
        + [(par, VMEM), (att_out, ANY)]
        + [(a, VMEM) for a in states]
        + refs(group_a),
        [
            (a, BATCH)
            for a in (ext_b, ext_b, ext_b, ext_b, ext_f, ext_b, ext_b, ext_b, stats_shape)
        ],
        [square, block_line, block_line, sems(PER)],
        10,
        deps,
    )
    deps = came + [stats_two]
    came = launch(deps, group_c)
    key_buf = pltpu.VMEM((tiles, width, width), BF)
    own_value = ffn_value.reshape(4, shard, width)
    (hidden,) = call(
        "hidden",
        hidden_kernel,
        (batches,),
        [info_in, (ffn_in, BATCH), (ffn_key, ANY)] + refs(group_b),
        [(wide_b, BATCH)],
        [key_buf, sems(tiles + PER)],
        9,
        deps,
    )
    came = launch(came + [hidden], group_c)
    mixed_shape = shape((batches, 1, span, width), BF)
    value_buf = pltpu.VMEM((4 * tiles, shard, width), BF)
    mixed, grad_carried, grad_gate = call(
        "gate",
        functools.partial(gate_kernel, span, seqs),
        (batches,),
        [info_in]
        + [(a, BATCH) for a in (hidden, ffn_gate_in, middle, cot_ext)]
        + [(own_value, ANY), (ffn_recept, ANY)]
        + refs(group_c),
        [(mixed_shape, BATCH)] + [(ext_b, BATCH)] * 2,
        [value_buf, square, sems(2 * PER)],
        17,
        came,
    )

    plain = (width // (4 * ranks)) % 8 != 0
    nz = 1 if plain else ranks // 2
    plan = (tuple(range(nz)), plain)

    def core_of(keep, send):
        return Core(*(a.reshape(4, -1, a.shape[-1]) for a in (keep, send)), plain)

    big = shape((4, nz, ff // (8 * nz), width), BF)
    big_spec = pl.BlockSpec((1,) + big.shape[1:], lambda i: (i, 0, 0, 0))
    keep_v, send_v = call(
        "value_grad",
        functools.partial(value_grad_kernel, span, plan),
        (4,),
        [info_in, (hidden, VMEM), (grad_carried, VMEM)],
        [(big, big_spec)] * 2,
        [square_f],
        10,
    )
    core_value = core_of(keep_v, send_v)
    deps = [keep_v]
    came = launch(deps, core_value)
    wide_half = shape((width // 2, ff + width), BF)
    keep_k, send_k = call(
        "gate_back",
        functools.partial(gate_back_kernel, span, plan),
        (1,),
        [info_in, (ffn_gate_in, VMEM), (grad_gate, VMEM)],
        [(wide_half, pl.BlockSpec((width // 2, width), lambda i: (0, tiles)))] * 2,
        [square_f],
        10,
        deps,
    )
    deps = came + [keep_k]
    sum_value = Quarter(core_value)
    came = launch(deps, sum_value)
    out_tile = pl.BlockSpec((width // 2, width), lambda i: (0, i))
    keep_k, send_k, _, grad_in = call(
        "inner",
        functools.partial(inner_kernel, span, plan),
        (tiles,),
        [
            info_in,
            (keep_k, ANY),
            (send_k, ANY),
            (hidden, VMEM),
            (grad_carried, VMEM),
            (ffn_in, VMEM),
            (ffn_key, ANY),
            (own_value, ANY),
        ]
        + refs(group_b)
        + refs(group_c),
        [(wide_half, out_tile)] * 2 + [(pltpu.VMEM(wide_b.shape, BF), VMEM), (ext_b, VMEM)],
        [
            key_buf,
            value_buf,
            square_f,
            sems(tiles + 2 * PER),
        ],
        21,
        deps,
        {1: 0, 2: 1, 3: 2},
    )
    core_key = core_of(keep_k, send_k)
    deps = came + [grad_in]
    came = launch(deps, sum_value, core_key)
    sums_shape = shape((8, width), F32)
    grad_middle, grad_att, grad_recept, grad_num, grad_den, ends_back, state_back, sums = call(
        "attend_back",
        functools.partial(attend_back_kernel, span, seqs),
        (batches,),
        [info_in]
        + [
            (a, BATCH)
            for a in (
                grad_gate,
                grad_in,
                change_two,
                middle,
                stats_two,
                cot_ext,
                by_num,
                by_recept,
                wkv,
            )
        ]
        + [(par, VMEM), (att_out, ANY), (ffn_recept, ANY)]
        + refs(group_a)
        + refs(group_c),
        [(a, BATCH) for a in (ext_f, ext_b, ext_b, pltpu.VMEM(line_f.shape, F32), pltpu.VMEM(line_f.shape, F32))]
        + [(ends_shape, BATCH)]
        + [(state_shape, VMEM), (sums_shape, VMEM)],
        [square, square, pltpu.VMEM((4, 8, width), F32), block_f, block_f, part, part, sems(2 * PER)],
        11,
        deps,
    )
    exchange = States(state_back)
    came = launch(came, exchange)
    deps = came
    sum_key = Quarter(core_key)
    came = launch(deps, exchange, sum_key)
    two = shape((width // 2, 2 * width), BF)
    keep_o, send_o = call(
        "recept",
        functools.partial(recept_kernel, span, plan),
        (2,),
        [info_in] + [(a, VMEM) for a in (gated, grad_att, mix_recept, grad_recept)],
        [(two, pl.BlockSpec((width // 2, width), lambda i: (0, i)))] * 2,
        [square_f],
        10,
        deps,
    )
    while exchange.sends():
        came = launch(came, exchange)
    states_back = exchange.parts
    core_out = core_of(keep_o, send_o)
    deps = came + [keep_o]
    all_value = Finish(sum_value)
    came = launch(deps, all_value, sum_key, core_out)
    grad_key, grad_value, keep_l, send_l, sums_back = call(
        "recur_back",
        functools.partial(recur_back_kernel, span, seqs, ranks, len(states), len(states_back), plan),
        (batches,),
        [info_in]
        + [
            (a, BATCH)
            for a in (
                grad_num,
                grad_den,
                exp_key,
                value,
                ends,
                ends_back,
                mix_key,
                mix_value,
            )
        ]
        + [(par, VMEM)]
        + [(a, VMEM) for a in states + states_back],
        [(ext_b, BATCH)] * 2 + [(two, VMEM)] * 2 + [(sums_shape, VMEM)],
        [block_line, block_line, block_line, block_line, square_f, square_f, pltpu.VMEM((2, 8, width), F32)],
        17,
        deps,
    )
    core_last = core_of(keep_l, send_l)
    deps = launch(came + [sums_back], core_last)
    all_key = Finish(sum_key)
    sum_last = Quarter(core_last, core_out)
    came = launch(deps, all_key, sum_last)
    grad_shape = shape((batches, 1, span, width), F32)
    half_table = shape((width // 2, 128), BF)
    inners, parts, keep_p, send_p = call(
        "first_back",
        functools.partial(first_back_kernel, span, seqs, plan),
        (batches,),
        [info_in]
        + [(a, BATCH) for a in (grad_key, grad_value, grad_recept, tok_ext, stats_one, change_one)]
        + [(sums, VMEM), (sums_back, VMEM), (par, VMEM)]
        + [(att_key, ANY), (att_value, ANY), (att_recept, ANY)]
        + refs(group_a),
        [(ext_f, BATCH), (stats_shape, BATCH)] + [(half_table, VMEM)] * 2,
        [
            three,
            block_f,
            block_f,
            block_f,
            pltpu.VMEM((7, 8, width), F32),
            pltpu.VMEM((width, 128), F32),
            sems(PER + 2),
        ],
        13,
        deps,
    )
    core_table = core_of(keep_p, send_p)
    deps = launch(came + [keep_p], core_table)
    sum_table = SmallQuarter(core_table)
    came = launch(deps, sum_last, sum_table)
    (tokens_grad,) = call(
        "tokens_grad",
        functools.partial(tokens_grad_kernel, span),
        (batches,),
        [info_in] + [(a, BATCH) for a in (inners, parts, tok_ext, stats_one, grad_middle)],
        [(grad_shape, BATCH)],
        [],
        7,
        deps,
    )
    all_last = Finish(sum_last, sum_table)
    launch(came + [tokens_grad], all_last)
    key, last = all_key.total, all_last.total
    return (
        mixed,
        tokens_grad,
        last[:, :width],
        last[:, width : 2 * width],
        last[:, 3 * width : 4 * width],
        last[:, 2 * width : 3 * width],
        key[:, :ff],
        all_value.total,
        key[:, ff:],
        last[:, 4 * width : 4 * width + params.shape[1]],
    )


def solution(mesh):
    split = P(("dp", "seq"), None)
    rows = P("dp", None)
    stream = P(None, "dp", "seq", None)
    return jax.shard_map(
        body,
        mesh=mesh,
        in_specs=(stream, stream, P(None, "dp", None)) + (rows,) * 8,
        out_specs=(stream, stream) + (split,) * 8,
        check_vma=False,
    )
```

```python
import functools

import jax
import jax.numpy as jnp
from jax import lax
from jax.experimental import pallas as pl
from jax.experimental.pallas import tpu as pltpu
from jax.sharding import PartitionSpec as P

EPS = 1e-05
BF = jnp.bfloat16
F32 = jnp.float32
PAD = 16
FAR = 1 << 30
PER = 9
HEAD = 4


def bounds_of(info, batch, seqs):
    ends = [jnp.int32(0)]
    for i in range(seqs):
        ends.append(ends[-1] + info[HEAD + batch * seqs + i])
    return ends


def positions(info, row, count):
    return lax.broadcasted_iota(jnp.int32, (count, 128), 0) + (row - PAD + info[0])


def since_start(pos, bounds):
    best = jnp.full(pos.shape, FAR, jnp.int32)
    for b in bounds:
        best = jnp.where(pos >= b, jnp.minimum(best, pos - b), best)
    return best


def until_start(pos, bounds):
    best = jnp.full(pos.shape, FAR, jnp.int32)
    for b in bounds:
        best = jnp.where(pos < b, jnp.minimum(best, b - pos), best)
    return best


def wide(mask, width):
    return jnp.concatenate([mask] * (width // 128), axis=1)


def flag(cond, width):
    return wide(jnp.where(cond, 1.0, 0.0).astype(F32), width)


def rows_of(count, width):
    return wide(lax.broadcasted_iota(jnp.int32, (count, 128), 0), width)


def down(x, carry):
    rolled = pltpu.roll(x, 1, 0)
    return jnp.where(rows_of(*x.shape) == 0, carry, rolled)


def up(x, carry):
    n = x.shape[0]
    rolled = pltpu.roll(x, n - 1, 0)
    return jnp.where(rows_of(*x.shape) == n - 1, carry, rolled)


def nn(a, b):
    return jnp.dot(a, b, preferred_element_type=F32)


def nt(a, b):
    return lax.dot_general(a, b, (((1,), (1,)), ((), ())), preferred_element_type=F32)


def tn(a, b):
    return lax.dot_general(a, b, (((0,), (0,)), ((), ())), preferred_element_type=F32)


def slabs(span, body, init, reverse=False, unroll=4):
    step = 32
    many = span // step

    def one(i, carry):
        at = many - 1 - i if reverse else i
        return body(pl.multiple_of(PAD + at * step, PAD), step, True, carry)

    first, last = (PAD + span, 0) if reverse else (0, PAD + span)
    carry = body(first, PAD, False, init)
    carry = lax.fori_loop(0, many, one, carry, unroll=unroll)
    return body(last, PAD, False, carry)


def lanes(x):
    return sum(x[:, i : i + 128] for i in range(0, x.shape[1], 128))


def tile(x, i):
    return x[:, i * 128 : (i + 1) * 128]


def row_mean(ref, width):
    total = jnp.sum(ref[...], axis=1, keepdims=True) * (1.0 / width)
    return jnp.broadcast_to(total, ref.shape)


def steps_of(low, high, body, carry, reverse=False, unroll=4):
    def one(i, carry):
        return body(high - 1 - i if reverse else low + i, carry)

    count = high - low
    while count % unroll:
        unroll -= 1
    return lax.fori_loop(0, count, one, carry, unroll=unroll)


def fold(x):
    n, c = x.shape
    return jnp.sum(x.reshape(n // 8, 8, c), axis=0)


def no_start(bounds, low, high):
    hit = jnp.int32(0)
    for b in bounds:
        hit = hit | jnp.where((b > low) & (b <= high), 1, 0)
    return jnp.where(hit == 0, 1.0, 0.0).astype(F32)


def incoming(info, states, batch, bounds, speed, span, ranks, reverse):
    me, base = info[2], info[0]
    num = jnp.zeros(speed.shape, F32)
    den = jnp.zeros(speed.shape, F32)
    for k in range(1, ranks):
        other = me ^ k
        if reverse:
            gap = other - me - 1
            clear = no_start(bounds, base + span + 1, other * span + 1)
        else:
            gap = me - 1 - other
            clear = no_start(bounds, (other + 1) * span - 2, base - 2)
        use = jnp.where(gap >= 0, clear, 0.0).astype(F32)
        weight = jnp.exp(-speed * (jnp.maximum(gap, 0) * span).astype(F32)) * use
        per = sum(r.shape[0] for r in states) // ranks
        many = states[0].shape[0] // per
        at = (k % many) * per + 2 * batch
        num += weight * states[k // many][pl.ds(at, 1), :]
        den += weight * states[k // many][pl.ds(at + 1, 1), :]
    return num, den


def start_all(copies):
    for c in copies:
        c.start()


def wait_all(copies):
    for c in copies:
        c.wait()


def copies_of(info, owns, pieces, blocks, target, sems, at=0):
    d, c = info[1], info[3]
    shard = owns[0].shape[0]
    half = shard // 2
    out = []
    for k, own in enumerate(owns):
        out.append(pltpu.make_async_copy(own, target.at[k, pl.ds(pl.multiple_of(d * shard, 16), shard)], sems.at[at]))
        at += 1
    for which, arrays in enumerate(pieces):
        core = (c + which) % 2
        for mask, shift, ref in zip((1, 2, 3, 3), (0, 0, 0, half // 2), arrays):
            row = pl.multiple_of((d ^ mask) * shard + core * half + shift, 16)
            source = ref.at[blocks]
            out.append(pltpu.make_async_copy(source, target.at[:, pl.ds(row, source.shape[1])], sems.at[at]))
            at += 1
    return out


def value_copies(info, own, pieces, target, sems, at=0):
    d, c = info[1], info[3]
    half = target.shape[1] // 2
    out = [pltpu.make_async_copy(own, target.at[pl.ds(4 * d, 4)], sems.at[at])]
    at += 1
    for which, arrays in enumerate(pieces):
        core = (c + which) % 2
        for mask, shift, ref in zip((1, 2, 3, 3), (0, 0, 0, half // 2), arrays):
            place = target.at[pl.ds(4 * (d ^ mask), 4), pl.ds(pl.multiple_of(core * half + shift, 16), ref.shape[1])]
            out.append(pltpu.make_async_copy(ref.at[pl.ds(0, 4)], place, sems.at[at]))
            at += 1
    return out


def place(info, plain):
    if plain:
        return 0, 0, 0
    return info[1], info[2] // 2, info[3]


def scatter_rows(info, src, keep, send, plan, write):
    zorder, plain = plan
    d, z, c = place(info, plain)
    nz = len(zorder)
    block = src.shape[0] // (8 * nz)
    per = 4 * nz * block // 16
    groups = block // 8
    for ref, core in ((keep, c), (send, 1 - c)):
        for slab in range(per):
            parts = []
            for g in (2 * slab, 2 * slab + 1):
                i = g % groups
                q = (g // groups) % nz
                p = g // (groups * nz)
                row = ((d ^ p) * nz + (z ^ zorder[q])) * (2 * block) + core * block + i * 8
                parts.append(src[pl.ds(pl.multiple_of(row, 8), 8), :])
            write(ref, slab * 16, jnp.concatenate(parts, axis=0).astype(BF))


def keep_whole(batch, buffer, target, sem):
    def copy():
        return pltpu.make_async_copy(buffer, target, sem)

    pl.when(batch == 0)(lambda: copy().start())
    pl.when(batch == pl.num_programs(0) - 1)(lambda: copy().wait())


class Late:
    def __init__(self, source, buffer, sems, index):
        self.source, self.buffer, self.sems, self.index = source, buffer, sems, index
        self.shape = (1,) + tuple(buffer.shape[1:])

    def copy(self, b):
        return pltpu.make_async_copy(self.source.at[b], self.buffer.at[b], self.sems.at[self.index, b])

    def ready(self):
        b = pl.program_id(0)
        self.copy(b).wait()
        return self.buffer.at[pl.ds(b, 1)]


def mix_kernel(
    span, seqs, info, tokens, cotangent, halo, par, mix_key, mix_value, mix_recept, change, tok_ext, cot_ext, stats, held
):
    batch = pl.program_id(0)
    bounds = bounds_of(info, batch, seqs)
    gain, bias = par[0:1, :], par[1:2, :]
    mixes = (par[2:3, :], par[3:4, :], par[4:5, :])
    width = tokens.shape[3]
    mean, scale = stats.at[0, 0], stats.at[0, 1]

    def load(row, n, owned, carry):
        at = pl.ds(row, n)
        if owned:
            x, g = tokens[0, 0, pl.ds(row - PAD, n), :], cotangent[0, 0, pl.ds(row - PAD, n), :]
        else:
            low = 0 if row == 0 else PAD
            x, g = halo[0, 0, low : low + PAD, :], halo[1, 0, low : low + PAD, :]
        tok_ext[0, at, :] = x
        cot_ext[0, at, :] = g
        x = x.astype(F32)
        held[at, :] = x
        mean[at, :] = lanes(x)
        return carry

    slabs(span, load, 0)
    mean[...] = row_mean(mean, width)

    def spread(row, n, owned, carry):
        at = pl.ds(row, n)
        x = held[at, :] - wide(mean[at, :], width)
        scale[at, :] = lanes(x * x)
        return carry

    slabs(span, spread, 0)
    scale[...] = lax.rsqrt(row_mean(scale, width) + EPS)

    def body(row, n, owned, carry):
        at = pl.ds(row, n)
        normed = (held[at, :] - wide(mean[at, :], width)) * wide(scale[at, :], width)
        first = normed * gain + bias
        keep = flag(since_start(positions(info, row, n), bounds) >= 1, width)
        shifted = down(first, carry) * keep
        diff = first - shifted
        for mu, ref in zip(mixes, (mix_key, mix_value, mix_recept)):
            ref[0, at, :] = (shifted + diff * mu).astype(BF)
        change[0, at, :] = diff.astype(BF)
        return first[n - 1 : n]

    slabs(span, body, jnp.zeros((1, width), F32))


class Chunks:
    def __init__(self, info, bounds, rows, speed):
        self.size = rows // 8
        self.bounds = bounds
        self.base = info[0] - PAD
        self.row8 = lax.broadcasted_iota(jnp.int32, (8, 128), 0)
        self.start = self.row8 * self.size + self.base
        self.speed = speed
        self.tiles = speed.shape[1] // 128
        self.rate = self.split(jnp.exp(-speed))

    def split(self, row):
        return [jnp.broadcast_to(tile(row, i), (8, 128)) for i in range(self.tiles)]

    def at(self, j):
        return pl.ds(j, 8, stride=self.size)

    def keep(self, j, ahead=0):
        pos = self.start + (j + ahead)
        hit = pos == self.bounds[0]
        for b in self.bounds[1:]:
            hit = hit | (pos == b)
        return jnp.where(hit, 0.0, 1.0).astype(F32)

    def decay(self, low, high, count):
        clear = no_start(self.bounds, self.base + low, self.base + high)
        return jnp.exp(-self.speed * float(count)) * clear


def join(tiles):
    return jnp.concatenate(tiles, axis=1)


def write_state(state, batch, num, den):
    for i in range(state.shape[0] // 2):

        @pl.when(batch == i)
        def _():
            state[2 * i : 2 * i + 1, :] = num
            state[2 * i + 1 : 2 * i + 2, :] = den


def project_kernel(
    span, seqs, info, mix_key, mix_value, mix_recept, par, own_key, own_value, own_recept, *refs
):
    pieces = (refs[0:4], refs[4:8])
    exp_key, value, gate, ends, state, kept, weights, sems = refs[8:]
    batch = pl.program_id(0)
    bounds = bounds_of(info, batch, seqs)
    rows, width = mix_key.shape[1:]

    def copies():
        return copies_of(info, (own_key, own_value, own_recept), pieces, pl.ds(0, 3), weights, sems)

    @pl.when(batch == 0)
    def _():
        start_all(copies())
        wait_all(copies())

    acts = (jnp.exp, lambda x: x, jax.nn.sigmoid)
    for k, (left, ref, act) in enumerate(zip((mix_key, mix_value, mix_recept), (exp_key, value, gate), acts)):
        for i in range(0, width, 256):
            part = act(nn(left[0], weights[k, :, i : i + 256]))
            ref[0, i // 128] = part[:, :128]
            ref[0, i // 128 + 1] = part[:, 128:]

    speed = jnp.exp(par[5:6, :])
    chunks = Chunks(info, bounds, rows, speed)
    size = chunks.size

    def step(j, carry, cut=False):
        nums, dens = carry
        at = chunks.at(j)
        keep = chunks.keep(j)
        num_out, den_out = [], []
        for i in range(chunks.tiles):
            ek = exp_key[0, i, at, :]
            if cut:
                ek = jnp.where(chunks.row8 == 0, 0.0, ek)
            factor = chunks.rate[i] * keep
            num_out.append(factor * nums[i] + ek * value[0, i, at, :])
            den_out.append(factor * dens[i] + ek)
        return tuple(num_out), tuple(den_out)

    zero = tuple(jnp.zeros((8, 128), F32) for _ in range(chunks.tiles))
    last = PAD + span - 2 - 7 * size
    carry = (zero, zero)
    for j in range(PAD - 1):
        carry = step(j, carry, cut=True)
    carry = steps_of(PAD - 1, last + 1, step, carry)
    inside = [join(c)[7:8] for c in carry]
    carry = steps_of(last + 1, size, step, carry, unroll=size)
    whole_ends = [join(c) for c in carry]
    out = []
    for k in range(2):
        ends[0, k] = whole_ends[k]
        total = whole_ends[k][0:1]
        for s in range(1, 7):
            total = whole_ends[k][s : s + 1] + chunks.decay(s * size - 1, (s + 1) * size - 1, size) * total
        out.append(inside[k] + chunks.decay(7 * size - 1, 7 * size + last, last + 1) * total)
    write_state(state, batch, *out)
    keep_whole(batch, weights, kept, sems.at[PER + 2])


def forward_scan(info, states, batch, chunks, exp_key, value, ends, span, ranks, emit):
    size, width = chunks.size, chunks.speed.shape[1]
    entering = incoming(info, states, batch, chunks.bounds, chunks.speed, span, ranks, False)
    begin = []
    for k in range(2):
        lines = [jnp.zeros((1, width), F32)]
        lines.append(ends[0, k, 0:1, :] + chunks.decay(PAD - 2, size - 1, size - PAD + 1) * entering[k])
        for s in range(1, 7):
            lines.append(ends[0, k, s : s + 1, :] + chunks.decay(s * size - 1, (s + 1) * size - 1, size) * lines[-1])
        begin.append(jnp.concatenate(lines, axis=0))
    carry = tuple(tuple(tile(b, i) for i in range(chunks.tiles)) for b in begin)

    def step(j, carry, insert=None):
        nums, dens = carry
        at = chunks.at(j)
        keep = chunks.keep(j)
        num_out, den_out = [], []
        for i in range(chunks.tiles):
            ek, v = exp_key[0, i, at, :], value[0, i, at, :]
            before_num = keep * nums[i]
            before_den = keep * dens[i]
            x, y = ek * v, ek
            emit(at, i, before_num, before_den, ek, x)
            if insert is not None:
                x = jnp.where(chunks.row8 == 0, insert[0][i], x)
                y = jnp.where(chunks.row8 == 0, insert[1][i], y)
            num_out.append(chunks.rate[i] * before_num + x)
            den_out.append(chunks.rate[i] * before_den + y)
        return tuple(num_out), tuple(den_out)

    none = [[0.0] * chunks.tiles] * 2
    for j in range(PAD - 2):
        carry = step(j, carry, none)
    carry = step(PAD - 2, carry, [chunks.split(e) for e in entering])
    steps_of(PAD - 1, size, step, carry)


def recur_kernel(span, seqs, ranks, parts, info, exp_key, value, gate, ends, tokens, par, own_out, *refs):
    states, refs = refs[:parts], refs[parts:]
    pieces = (refs[0:4], refs[4:8])
    (
        gated,
        by_num,
        by_recept,
        wkv,
        middle,
        ffn_in,
        ffn_gate_in,
        change,
        stats,
        kept,
        wo,
        line_wkv,
        line_inverse,
        sems,
    ) = refs[8:]
    batch = pl.program_id(0)
    bounds = bounds_of(info, batch, seqs)
    rows, width = tokens.shape[1:]

    def copies():
        return copies_of(info, (own_out,), pieces, pl.ds(3, 1), wo, sems)

    @pl.when(batch == 0)
    def _():
        start_all(copies())

    chunks = Chunks(info, bounds, rows, jnp.exp(par[5:6, :]))
    boost = chunks.split(jnp.exp(par[6:7, :]))

    def emit(at, i, before_num, before_den, ek, x):
        inverse = 1.0 / (before_den + boost[i] * ek)
        line_inverse[i, at, :] = inverse
        line_wkv[i, at, :] = (before_num + boost[i] * x) * inverse

    forward_scan(info, states, batch, chunks, exp_key, value, ends, span, ranks, emit)

    def pack(row, n, owned, carry):
        at = pl.ds(row, n)
        out = ([], [], [], [])
        for i in range(chunks.tiles):
            w, sig = line_wkv[i, at, :], gate[0, i, at, :]
            g = w * sig
            out[0].append(g)
            out[1].append(sig * line_inverse[i, at, :])
            out[2].append(g * (1.0 - sig))
            out[3].append(w)
        for ref, tiles in zip((gated, by_num, by_recept, wkv), out):
            ref[0, at, :] = join(tiles).astype(BF)
        return carry

    slabs(span, pack, 0)

    @pl.when(batch == 0)
    def _():
        wait_all(copies())

    middle[0] = nn(gated[0], wo[0])
    gain, bias = par[7:8, :], par[8:9, :]
    mean, scale = stats.at[0, 0], stats.at[0, 1]

    def residual(row, n, owned, carry):
        at = pl.ds(row, n)
        mid = middle[0, at, :] + tokens[0, at, :].astype(F32)
        middle[0, at, :] = mid
        mean[at, :] = lanes(mid)
        return carry

    slabs(span, residual, 0)
    mean[...] = row_mean(mean, width)

    def spread(row, n, owned, carry):
        at = pl.ds(row, n)
        x = middle[0, at, :] - wide(mean[at, :], width)
        scale[at, :] = lanes(x * x)
        return carry

    slabs(span, spread, 0)
    scale[...] = lax.rsqrt(row_mean(scale, width) + EPS)

    def body(row, n, owned, carry):
        at = pl.ds(row, n)
        normed = (middle[0, at, :] - wide(mean[at, :], width)) * wide(scale[at, :], width)
        second = normed * gain + bias
        keep = flag(since_start(positions(info, row, n), bounds) >= 1, width)
        shifted = down(second, carry) * keep
        diff = second - shifted
        ffn_in[0, at, :] = (shifted + diff * par[9:10, :]).astype(BF)
        ffn_gate_in[0, at, :] = (shifted + diff * par[10:11, :]).astype(BF)
        change[0, at, :] = diff.astype(BF)
        return second[n - 1 : n]

    slabs(span, body, jnp.zeros((1, width), F32))
    keep_whole(batch, wo, kept, sems.at[PER])


def hidden_kernel(info, ffn_in, own_key, *refs):
    pieces = (refs[0:4], refs[4:8])
    hidden, kept, wk, sems = refs[8:]
    width = ffn_in.shape[2]
    tiles = wk.shape[0]

    def copies():
        owns = [own_key.at[:, pl.ds(j * width, width)] for j in range(tiles)]
        return copies_of(info, owns, pieces, pl.ds(0, tiles), wk, sems)

    @pl.when(pl.program_id(0) == 0)
    def _():
        start_all(copies())
        wait_all(copies())

    for j in range(tiles):
        for i in range(0, width, 256):
            relu = jnp.maximum(nn(ffn_in[0], wk[j, :, i : i + 256]), 0.0)
            hidden[0, :, pl.ds(j * width + i, 256)] = (relu * relu).astype(BF)
    keep_whole(pl.program_id(0), wk, kept, sems.at[tiles + PER])


def gate_kernel(
    span, seqs, info, hidden, ffn_gate_in, middle, cotangent, own_value, own_recept, *refs
):
    pieces = (refs[0:4], refs[4:8])
    mixed, grad_carried, grad_gate, kept, kept_gate, wv, wr, sems = refs[8:]
    batch = pl.program_id(0)
    bounds = bounds_of(info, batch, seqs)
    rows, width = middle.shape[1:]

    def copies():
        return (
            copies_of(info, (own_recept,), pieces, pl.ds(4, 1), wr, sems),
            value_copies(info, own_value, pieces, wv, sems, PER),
        )

    @pl.when(batch == 0)
    def _():
        for c in copies():
            start_all(c)
        wait_all(copies()[0])
    keep_whole(batch, wv, kept, sems.at[2 * PER])
    keep_whole(batch, wr, kept_gate, sems.at[2 * PER + 1])


    @pl.when(batch == 0)
    def _():
        wait_all(copies()[1])

    flat = wv[...].reshape(wv.shape[0] * wv.shape[1], width)
    total = bounds[-1]
    step = rows // 2
    for low in range(0, rows, step):
        gate = nn(ffn_gate_in[0, low : low + step, :], wr[0])
        carried = nn(hidden[0, low : low + step, :], flat)
        for i in range(0, step, PAD):
            row = low + i
            at = pl.ds(row, PAD)
            sig = jax.nn.sigmoid(gate[i : i + PAD])
            car = carried[i : i + PAD]
            live = flag(positions(info, row, PAD) < total, width)
            grad = cotangent[0, at, :].astype(F32) * live
            if PAD <= row < PAD + span:
                mixed[0, 0, row - PAD : row, :] = (middle[0, at, :] + sig * car).astype(BF)
            part = grad * sig
            grad_carried[0, at, :] = part.astype(BF)
            grad_gate[0, at, :] = (part * car * (1.0 - sig)).astype(BF)


def over_own(left, right, span):
    own = pl.ds(PAD, span)
    both = [jnp.concatenate([f[b, own] for b in range(f.shape[0])], axis=0) for f in (left, right)]
    return tn(*both)


def store_sixteen(ref, row, value):
    ref[row : row + 16, :] = value


def value_grad_kernel(span, plan, info, hidden, grad_carried, keep, send, total):
    zorder, plain = plan
    d, z, c = place(info, plain)
    width = total.shape[1]
    column = pl.ds(pl.multiple_of((pl.program_id(0) ^ d) * width, width), width)
    block = keep.shape[2]
    total[...] = over_own(hidden.at[:, :, column], grad_carried, span)
    for q, zr in enumerate(zorder):
        for ref, core in ((keep, c), (send, 1 - c)):
            row = pl.multiple_of(((z ^ zr) * 2 + core) * block, 8)
            ref[0, q] = total[pl.ds(row, block), :].astype(BF)


def gate_back_kernel(span, plan, info, ffn_gate_in, grad_gate, keep, send, total):
    total[...] = over_own(ffn_gate_in, grad_gate, span)
    scatter_rows(info, total, keep, send, plan, store_sixteen)


def inner_kernel(
    span, plan, info, _, __, hidden, grad_carried, ffn_in, key, whole_value, keep, send, grad_inner, grad_in, wk, wv, total, sems
):
    step = pl.program_id(0)
    batches, _, width = grad_in.shape
    tiles = wk.shape[0]

    def copies():
        out = []
        for j in range(tiles):
            block = pl.ds(4 * j, 4)
            out.append(pltpu.make_async_copy(whole_value.at[block], wv.at[block], sems.at[j]))
        return out + [pltpu.make_async_copy(key, wk, sems.at[tiles])]

    @pl.when(step == 0)
    def _():
        start_all(copies())

    here = pl.multiple_of(step * width, width)
    for j in range(tiles):
        pl.when(step == j)(lambda: copies()[j].wait())
    value = wv[pl.ds(4 * step, 4)].reshape(4 * wv.shape[1], width)
    for b in range(batches):
        for i in range(0, width, 256):
            back = nt(grad_carried[b], value[i : i + 256])
            at = pl.ds(here + i, 256)
            square = hidden[b, :, at].astype(F32)
            relu = square * lax.rsqrt(jnp.maximum(square, 1e-30))
            grad_inner[b, :, at] = (back * (2.0 * relu)).astype(BF)
    total[...] = over_own(ffn_in, grad_inner.at[:, :, pl.ds(here, width)], span)
    scatter_rows(info, total, keep, send, plan, store_sixteen)

    @pl.when(step == tiles - 1)
    def _():
        copies()[tiles].wait()
        right = jnp.concatenate([wk[j] for j in range(tiles)], axis=1)
        for b in range(batches):
            grad_in[b] = nt(grad_inner[b], right).astype(BF)


def attend_back_kernel(
    span,
    seqs,
    info,
    grad_gate,
    grad_in,
    change,
    middle,
    stats,
    cotangent,
    by_num,
    by_recept,
    wkv,
    par,
    whole_out,
    whole_gate,
    *refs,
):
    (grad_middle, grad_att, grad_recept, grad_num, grad_den, ends, state, sums, wo, wr, acc, held, back_gate, part_a, part_b, sems) = refs
    batch = pl.program_id(0)
    bounds = bounds_of(info, batch, seqs)
    rows, width = middle.shape[1:]

    def copies():
        return [pltpu.make_async_copy(whole_out, wo, sems.at[0])]

    def gate_copies():
        return [pltpu.make_async_copy(whole_gate, wr, sems.at[1])]

    @pl.when(batch == 0)
    def _():
        start_all(gate_copies())
        start_all(copies())
        acc[...] = jnp.zeros_like(acc)

    gain = par[7:8, :]
    mu, nu = par[9:10, :], par[10:11, :]
    total = bounds[-1]

    @pl.when(batch == 0)
    def _():
        wait_all(gate_copies())

    back_gate[...] = nt(grad_gate[0], wr[0])
    mean, scale = stats.at[0, 0], stats.at[0, 1]

    def normed_of(at):
        return (middle[0, at, :] - wide(mean[at, :], width)) * wide(scale[at, :], width)

    def gather(row, n, owned, carry):
        at = pl.ds(row, n)
        a, b = grad_in[0, at, :].astype(F32), back_gate[at, :]
        keep = flag(since_start(positions(info, row, n), bounds) >= 1, width)
        normed = normed_of(at)
        direct = a * mu + b * nu
        moved = (a + b - direct) * keep
        second = direct + up(moved, carry)
        if owned:
            diff = change[0, at, :].astype(F32)
            acc[0] += fold(second * normed)
            acc[1] += fold(second)
            acc[2] += fold(a * diff)
            acc[3] += fold(b * diff)
        inner = second * gain
        held[at, :] = inner
        part_a[at, :] = lanes(inner)
        part_b[at, :] = lanes(inner * normed)
        return moved[0:1]

    slabs(span, gather, jnp.zeros((1, width), F32), reverse=True)
    part_a[...] = row_mean(part_a, width)
    part_b[...] = row_mean(part_b, width)


    def apply(row, n, owned, carry):
        at = pl.ds(row, n)
        back = wide(scale[at, :], width) * (
            held[at, :] - wide(part_a[at, :], width) - normed_of(at) * wide(part_b[at, :], width)
        )
        live = flag(positions(info, row, n) < total, width)
        grad = cotangent[0, at, :].astype(F32) * live + back
        grad_middle[0, at, :] = grad
        grad_att[0, at, :] = grad.astype(BF)
        return carry

    cotangent = cotangent.ready()
    slabs(span, apply, 0)

    @pl.when(batch == 0)
    def _():
        wait_all(copies())

    held[...] = nt(grad_att[0], wo[0])
    speed = jnp.exp(par[5:6, :])
    chunks = Chunks(info, bounds, rows, speed)
    size = chunks.size


    def point(row, n, owned, carry):
        at = pl.ds(row, n)
        back = held[at, :]
        num = back * by_num[0, at, :].astype(F32)
        den = num * wkv[0, at, :].astype(F32)
        for i in range(chunks.tiles):
            grad_num[0, i, at, :] = tile(num, i)
            grad_den[0, i, at, :] = -tile(den, i)
        grad_recept[0, at, :] = (back * by_recept[0, at, :].astype(F32)).astype(BF)
        return carry

    by_num, by_recept, wkv = by_num.ready(), by_recept.ready(), wkv.ready()
    slabs(span, point, 0)

    def step(j, carry, cut=False):
        nums, dens = carry
        at = chunks.at(j)
        keep = chunks.keep(j, 1)
        num_out, den_out = [], []
        for i in range(chunks.tiles):
            gn, gd = grad_num[0, i, at, :], grad_den[0, i, at, :]
            if cut:
                gn, gd = jnp.where(chunks.row8 == 7, 0.0, gn), jnp.where(chunks.row8 == 7, 0.0, gd)
            factor = chunks.rate[i] * keep
            num_out.append(factor * nums[i] + gn)
            den_out.append(factor * dens[i] + gd)
        return tuple(num_out), tuple(den_out)

    zero = tuple(jnp.zeros((8, 128), F32) for _ in range(chunks.tiles))
    after = PAD + span + 1 - 7 * size
    carry = (zero, zero)
    for j in reversed(range(after, size)):
        carry = step(j, carry, cut=True)
    carry = steps_of(PAD + 1, after, step, carry, reverse=True)
    inside = [join(c)[0:1] for c in carry]
    carry = steps_of(0, PAD + 1, step, carry, reverse=True, unroll=size)
    whole_ends = [join(c) for c in carry]
    out = []
    for k in range(2):
        ends[0, k] = whole_ends[k]
        line = whole_ends[k][7:8]
        for s in range(6, 0, -1):
            line = whole_ends[k][s : s + 1] + chunks.decay(s * size, (s + 1) * size, size) * line
        out.append(inside[k] + chunks.decay(PAD + 1, size, size - PAD - 1) * line)
    write_state(state, batch, *out)

    @pl.when(batch == pl.num_programs(0) - 1)
    def _():
        sums[...] = jnp.zeros_like(sums)
        for i in range(4):
            sums[i : i + 1, :] = jnp.sum(acc[i], axis=0, keepdims=True)


def recept_kernel(span, plan, info, gated, grad_att, mix_recept, grad_recept, keep, send, total):
    def grad(left, right):
        total[...] = over_own(left, right, span)
        scatter_rows(info, total, keep, send, plan, store_sixteen)

    pl.when(pl.program_id(0) == 0)(lambda: grad(gated, grad_att))
    pl.when(pl.program_id(0) == 1)(lambda: grad(mix_recept, grad_recept))


def again_kernel(span, seqs, ranks, parts, info, exp_key, value, ends, grad_recept, par, whole_a, *refs):
    states, (num_prev, den_prev, back_recept, wr, sems) = refs[:parts], refs[parts:]
    batch = pl.program_id(0)
    bounds = bounds_of(info, batch, seqs)
    chunks = Chunks(info, bounds, grad_recept.shape[1], jnp.exp(par[5:6, :]))

    def copy():
        return pltpu.make_async_copy(whole_a.at[2], wr, sems.at[0])

    pl.when(batch == 0)(lambda: copy().start())

    def emit(at, i, before_num, before_den, ek, x):
        num_prev[0, i, at, :] = before_num
        den_prev[0, i, at, :] = before_den

    forward_scan(info, states, batch, chunks, exp_key, value, ends, span, ranks, emit)
    pl.when(batch == 0)(lambda: copy().wait())
    back_recept[0] = nt(grad_recept[0], wr[...]).astype(BF)


def recur_back_kernel(
    span,
    seqs,
    ranks,
    parts,
    plan,
    info,
    grad_num,
    grad_den,
    exp_key,
    value,
    num_prev,
    den_prev,
    ends,
    mix_key,
    mix_value,
    par,
    *refs,
):
    states, refs = refs[:parts], refs[parts:]
    grad_key, grad_value, keep, send, sums, line_key, line_value, total, total2, acc = refs
    batch = pl.program_id(0)
    bounds = bounds_of(info, batch, seqs)
    rows, width = mix_key.shape[1:]

    @pl.when(batch == 0)
    def _():
        acc[...] = jnp.zeros_like(acc)

    speed = jnp.exp(par[5:6, :])
    chunks = Chunks(info, bounds, rows, speed)
    size = chunks.size
    boost = chunks.split(jnp.exp(par[6:7, :]))
    entering = incoming(info, states, batch, bounds, speed, span, ranks, True)
    after = PAD + span + 1 - 7 * size
    begin = []
    for k in range(2):
        lines = [jnp.zeros((1, width), F32)]
        lines.append(ends[0, k, 7:8, :] + chunks.decay(7 * size, 7 * size + after, after) * entering[k])
        for s in range(6, 0, -1):
            lines.append(ends[0, k, s : s + 1, :] + chunks.decay(s * size, (s + 1) * size, size) * lines[-1])
        begin.append(jnp.concatenate(lines[::-1], axis=0))
    zero = tuple(jnp.zeros((8, 128), F32) for _ in range(chunks.tiles))
    carry = tuple(tuple(tile(b, i) for i in range(chunks.tiles)) for b in begin) + (zero, zero)

    def step(j, carry, insert=None, mask=None):
        nums, dens, bonuses, decays = carry
        at = chunks.at(j)
        keep_next = chunks.keep(j, 1)
        outs = ([], [], [], [])
        for i in range(chunks.tiles):
            gn, ek, v = grad_num[0, i, at, :], exp_key[0, i, at, :], value[0, i, at, :]
            gd = grad_den[0, i, at, :]
            after_num = keep_next * nums[i]
            after_den = keep_next * dens[i]
            bek = boost[i] * ek
            bonus = bek * (v * gn + gd)
            line_key[i, at, :] = bonus + ek * (v * after_num + after_den)
            line_value[i, at, :] = bek * gn + ek * after_num
            decay = num_prev[0, i, at, :] * after_num + den_prev[0, i, at, :] * after_den
            if mask is not None:
                bonus = jnp.where(mask, bonus, 0.0)
                decay = jnp.where(mask, decay, 0.0)
            if insert is not None:
                gn = jnp.where(chunks.row8 == 7, insert[0][i], gn)
                gd = jnp.where(chunks.row8 == 7, insert[1][i], gd)
            outs[0].append(chunks.rate[i] * after_num + gn)
            outs[1].append(chunks.rate[i] * after_den + gd)
            outs[2].append(bonuses[i] + bonus)
            outs[3].append(decays[i] + decay)
        return tuple(tuple(o) for o in outs)

    none = [[0.0] * chunks.tiles] * 2
    upper = chunks.row8 < 7
    for j in reversed(range(after + 1, size)):
        carry = step(j, carry, none, upper)
    carry = step(after, carry, [chunks.split(e) for e in entering], upper)
    edge = PAD + span - 7 * size
    for j in reversed(range(edge, after)):
        carry = step(j, carry, None, upper)
    carry = steps_of(PAD, edge, step, carry, reverse=True)
    lower = chunks.row8 > 0
    carry = steps_of(0, PAD, lambda j, c: step(j, c, None, lower), carry, reverse=True)
    acc[0] += join(carry[2])
    acc[1] += join(carry[3])

    def pack(row, n, owned, carry):
        at = pl.ds(row, n)
        grad_key[0, at, :] = join([line_key[i, at, :] for i in range(chunks.tiles)]).astype(BF)
        grad_value[0, at, :] = join([line_value[i, at, :] for i in range(chunks.tiles)]).astype(BF)
        return carry

    slabs(span, pack, 0)
    mix_key, mix_value = mix_key.ready(), mix_value.ready()
    own = pl.ds(PAD, span)
    key_part = tn(mix_key[0, own, :], grad_key[0, own, :])
    value_part = tn(mix_value[0, own, :], grad_value[0, own, :])

    @pl.when(batch == 0)
    def _():
        total[...] = key_part
        total2[...] = value_part

    @pl.when(batch > 0)
    def _():
        total[...] += key_part
        total2[...] += value_part

    @pl.when(batch == pl.num_programs(0) - 1)
    def _():
        sums[...] = jnp.zeros_like(sums)
        for i in range(2):
            sums[i : i + 1, :] = jnp.sum(acc[i], axis=0, keepdims=True)
        for source, low in ((total, 0), (total2, width)):

            def write(ref, row, value):
                ref[row : row + 16, low : low + width] = value

            scatter_rows(info, source, keep, send, plan, write)


def first_back_kernel(
    span,
    seqs,
    plan,
    info,
    grad_key,
    grad_value,
    back_recept,
    tokens,
    stats,
    change,
    sums,
    sums_back,
    par,
    whole_a,
    *refs,
):
    inners, part_ref, keep, send, weights, back_key, back_value, acc, turned, sems = refs
    part_a, part_b = part_ref.at[0, 0], part_ref.at[0, 1]
    batch = pl.program_id(0)
    bounds = bounds_of(info, batch, seqs)
    width = tokens.shape[2]

    def copies():
        return [pltpu.make_async_copy(whole_a.at[pl.ds(0, 2)], weights, sems.at[0])]

    @pl.when(batch == 0)
    def _():
        start_all(copies())
        acc[...] = jnp.zeros_like(acc)
        wait_all(copies())

    back_key[...] = nt(grad_key[0], weights[0])
    back_value[...] = nt(grad_value[0], weights[1])
    gain = par[0:1, :]
    mixes = (par[2:3, :], par[3:4, :], par[4:5, :])
    tokens, stats, change = tokens.ready(), stats.ready(), change.ready()
    mean, scale = stats.at[0, 0], stats.at[0, 1]

    def normed_of(at):
        return (tokens[0, at, :].astype(F32) - wide(mean[at, :], width)) * wide(scale[at, :], width)

    def gather(row, n, owned, carry):
        at = pl.ds(row, n)
        parts = (back_key[at, :], back_value[at, :], back_recept[0, at, :].astype(F32))
        keep = flag(since_start(positions(info, row, n), bounds) >= 1, width)
        direct = sum(g * mu for g, mu in zip(parts, mixes))
        moved = (parts[0] + parts[1] + parts[2] - direct) * keep
        if owned:
            normed = normed_of(at)
            first = direct + up(moved, carry)
            diff = change[0, at, :].astype(F32)
            acc[2] += fold(first * normed)
            acc[3] += fold(first)
            for i in range(3):
                acc[4 + i] += fold(parts[i] * diff)
            inner = first * gain
            inners[0, at, :] = inner
            part_a[at, :] = lanes(inner)
            part_b[at, :] = lanes(inner * normed)
        return moved[0:1]

    slabs(span, gather, jnp.zeros((1, width), F32), reverse=True)
    part_a[...] = row_mean(part_a, width)
    part_b[...] = row_mean(part_b, width)

    @pl.when(batch == pl.num_programs(0) - 1)
    def _():
        def final(i):
            return jnp.sum(acc[i], axis=0, keepdims=True)

        speed = jnp.exp(par[5:6, :])
        decay = sums_back[1:2, :] * jnp.exp(-speed) * -speed
        columns = [final(i) for i in (2, 3, 4, 5, 6)] + [decay, sums_back[0:1, :]]
        columns += [sums[i : i + 1, :] for i in range(4)]
        stacked = jnp.concatenate(columns + [jnp.zeros((128 - len(columns), width), F32)], axis=0)
        turned[...] = stacked.T
        scatter_rows(info, turned, keep, send, plan, store_sixteen)


def tokens_grad_kernel(span, info, inners, parts, tokens, stats, grad_middle, tokens_grad):
    width = inners.shape[2]
    mean, scale = stats.at[0, 0], stats.at[0, 1]
    part_a, part_b = parts.at[0, 0], parts.at[0, 1]

    def apply(row, n, owned, carry):
        if owned:
            at = pl.ds(row, n)
            rate = wide(scale[at, :], width)
            normed = (tokens[0, at, :].astype(F32) - wide(mean[at, :], width)) * rate
            back = rate * (inners[0, at, :] - wide(part_a[at, :], width) - normed * wide(part_b[at, :], width))
            tokens_grad[0, 0, pl.ds(row - PAD, n), :] = grad_middle[0, at, :] + back
        return carry

    slabs(span, apply, 0)


def swap(x, axis, mask):
    size = lax.axis_size(axis)
    if mask == "next":
        return lax.ppermute(x, axis, [(i, i + 1) for i in range(size - 1)])
    if mask == "last":
        return lax.ppermute(x, axis, [(i + 1, i) for i in range(size - 1)])
    return lax.ppermute(x, axis, [(i, i ^ mask) for i in range(size)])


def add(terms):
    return sum(t.astype(F32) for t in terms)


def hold(x, deps):
    return lax.optimization_barrier((x,) + tuple(deps))[0] if deps else x


def launch(deps, *items):
    items = [item for item in items if item.sends()]
    sends = [s for item in items for s in item.sends()]
    if not sends:
        return list(deps)
    held = lax.optimization_barrier(tuple(s[0] for s in sends) + tuple(deps))
    came = [swap(x, axis, mask) for x, (_, axis, mask) in zip(held, sends)]
    left = list(came)
    for item in items:
        count = len(item.sends())
        item.receive(left[:count])
        left = left[count:]
    return came


class Gather:
    def __init__(self, blocks, core):
        half = blocks.shape[1] // 2
        mine = lax.dynamic_slice_in_dim(blocks, core * half, half, axis=1)
        self.next = [(mine, "dp", 1), (mine, "dp", 2)]
        self.stage = 0

    def sends(self):
        return self.next

    def receive(self, came):
        if self.stage == 0:
            x, y = came
            cut = x.shape[1] // 2
            self.mine = [x, y]
            self.next = [(x[:, :cut], "dp", 2), (y[:, cut:], "dp", 1), (x, "seq", 1), (y, "seq", 1)]
        elif self.stage == 1:
            self.mine += came[:2]
            self.other = came[2:]
            self.next = [(p, "seq", 1) for p in came[:2]]
        else:
            self.pieces = self.mine + self.other + came
            self.next = []
        self.stage += 1


class Table:
    def __init__(self, params):
        self.own = jnp.pad(params.T, ((0, 16 - params.shape[1]), (0, 0)))

    def sends(self):
        return [(self.own, "dp", mask) for mask in (1, 2, 3)]

    def receive(self, came):
        d = lax.axis_index("dp")
        a = [self.own] + came
        a = [jnp.where(d % 2 == 1, a[i ^ 1], a[i]) for i in range(4)]
        a = [jnp.where(d // 2 == 1, a[i ^ 2], a[i]) for i in range(4)]
        self.whole = jnp.concatenate(a, axis=1).astype(F32)


class States:
    def __init__(self, state):
        self.parts = [state]
        self.mask = 1

    def sends(self):
        return [(self.parts[0], "seq", self.mask)] if self.mask < lax.axis_size("seq") else []

    def receive(self, came):
        self.parts = self.parts + came
        self.mask *= 2
        if self.sends():
            self.parts = [jnp.concatenate(self.parts, axis=0)]


class Halo:
    def __init__(self, tokens, cotangent):
        span = tokens.shape[2]
        toks, cots = tokens[:, 0], cotangent[:, 0]
        self.next = [(toks[:, span - 2 :], "seq", "next"), (jnp.stack([toks[:, :2], cots[:, :2]]), "seq", "last")]

    def sends(self):
        return self.next

    def receive(self, came):
        before, after = came
        blank = jnp.zeros(after.shape[:2] + (PAD - 2,) + after.shape[3:], BF)
        before = jnp.stack([before, jnp.zeros_like(before)])
        self.rows = jnp.concatenate([blank, before, after, blank], axis=2)


class Core:
    def __init__(self, keep, send, plain):
        self.keep, self.send, self.plain = keep, send, plain

    def sends(self):
        return [] if self.plain else [(self.send, "seq", 1)]

    def receive(self, came):
        self.terms = [self.keep, came[0]]

    def whole(self):
        full = jnp.stack([self.keep, self.send], axis=1).reshape(-1, self.keep.shape[-1]).astype(F32)
        return lax.psum_scatter(full, ("dp", "seq"), scatter_dimension=0, tiled=True)


class Quarter:
    def __init__(self, *cores):
        self.cores = cores
        self.rows = cores[0].keep.shape[1]
        self.plain = cores[0].plain
        self.came = []

    def value(self, y, x, rows):
        p = 2 * y + x if isinstance(x, int) and isinstance(y, int) else slice(1, None, 2) if x == 1 else slice(2, None)
        return jnp.concatenate([add([t[p, rows] for t in c.terms]) for c in self.cores], axis=-1)

    def sends(self):
        half = self.rows // 2
        low, high = slice(0, half), slice(half, None)
        if self.plain or len(self.came) == 2:
            return []
        if not self.came:
            return [(self.value(None, 1, low).astype(BF), "dp", 1), (self.value(1, None, high).astype(BF), "dp", 2)]
        left, right = self.came[0]
        return [
            ((self.value(1, 0, low) + left[1].astype(F32)).astype(BF), "dp", 2),
            ((self.value(0, 1, high) + right[1].astype(F32)).astype(BF), "dp", 1),
        ]

    def receive(self, came):
        self.came.append(came)

    def final(self, rows):
        half = self.rows // 2
        side = 0 if rows.start < half else 1
        near = slice(rows.start - side * half, rows.stop - side * half)
        return self.value(0, 0, rows) + self.came[0][side][0][near].astype(F32) + self.came[1][side][near].astype(F32)


class SmallQuarter(Quarter):
    def sends(self):
        if self.plain or self.came:
            return []
        return [(self.value(p // 2, p % 2, slice(None)).astype(BF), "dp", p) for p in (1, 2, 3)]

    def final(self, rows):
        return self.value(0, 0, rows) + add([t[rows] for t in self.came[0]])


class Finish:
    def __init__(self, *quarters):
        self.quarters = quarters
        self.plain = quarters[0].plain
        self.count = 1 if self.plain else lax.axis_size("seq") // 2
        self.block = quarters[0].rows // self.count
        self.came = None
        if self.plain:
            self.total = jnp.concatenate([c.whole() for q in quarters for c in q.cores], axis=-1)

    def value(self, k):
        rows = slice(k * self.block, (k + 1) * self.block)
        return jnp.concatenate([q.final(rows) for q in self.quarters], axis=-1)

    def sends(self):
        if self.plain or self.came:
            return []
        return [(self.value(k).astype(BF), "seq", 2 * k) for k in range(1, self.count)]

    def receive(self, came):
        self.came = came
        self.total = self.value(0) + add(came)


ANY = pl.BlockSpec(memory_space=pl.ANY)
SMEM = pl.BlockSpec(memory_space=pltpu.SMEM)


def shape(s, dtype):
    return jax.ShapeDtypeStruct(s, dtype)


BATCH = "batch"
LATE = "late"
HELD = "held"
VMEM = pl.BlockSpec(memory_space=pltpu.VMEM)


def call(name, kernel, grid, ins, outs, scratch, mib, deps=(), aliases=None):
    ins = [(hold(ins[0][0], deps), ins[0][1])] + ins[1:]
    views = [i for i, (_, spec) in enumerate(ins + outs) if spec is BATCH]
    lates = [i for i, (_, spec) in enumerate(ins) if spec is LATE]
    extra = [pltpu.VMEM(ins[i][0].shape, ins[i][0].dtype) for i in lates]
    if lates:
        extra.append(pltpu.SemaphoreType.DMA((len(lates), grid[0])))

    def run(*refs):
        refs = list(refs)
        if lates:
            held, sems = refs[-len(extra) : -1], refs[-1]
            refs = refs[: -len(extra)]
            for k, i in enumerate(lates):
                refs[i] = Late(refs[i], held[k], sems, k)

            @pl.when(pl.program_id(0) == 0)
            def _():
                for b in range(grid[0]):
                    for i in lates:
                        refs[i].copy(b).start()

        for i in views:
            refs[i] = refs[i].at[pl.ds(pl.program_id(0), 1)]
        kernel(*refs)

    specs = {id(BATCH): VMEM, id(LATE): ANY, id(HELD): ANY}
    held = (LATE, HELD)
    operands = [pltpu.with_memory_space_constraint(a, pltpu.HBM) if any(s is h for h in held) else a for a, s in ins]
    return pl.pallas_call(
        run,
        grid=grid,
        in_specs=[specs.get(id(s), s) for _, s in ins],
        out_specs=[specs.get(id(s), s) for _, s in outs],
        out_shape=[a for a, _ in outs],
        scratch_shapes=list(scratch) + extra,
        input_output_aliases=aliases or {},
        compiler_params=pltpu.CompilerParams(vmem_limit_bytes=mib * 2**20),
        name=name,
    )(*operands)


def body(
    tokens,
    cotangent,
    lengths,
    att_key,
    att_value,
    att_recept,
    att_out,
    ffn_key,
    ffn_value,
    ffn_recept,
    params,
):
    batches, _, span, width = tokens.shape
    seqs = lengths.shape[2]
    ff = ffn_key.shape[1]
    tiles = ff // width
    ranks = lax.axis_size("seq")
    rows = span + 2 * PAD
    d, s = lax.axis_index("dp"), lax.axis_index("seq")
    core = s % 2
    at = lax.iota(jnp.int32, HEAD + batches * seqs)
    info = jnp.pad(lengths.reshape(batches * seqs), (HEAD, 0))
    for i, number in enumerate((s * span, d, s, core)):
        info = jnp.where(at == i, number, info)
    shard = att_key.shape[0]
    group_a = Gather(jnp.stack([att_key, att_value, att_recept, att_out]), core)
    group_b = Gather(jnp.stack([ffn_key[:, j * width : (j + 1) * width] for j in range(tiles)]), core)
    group_c = Gather(jnp.concatenate([ffn_value.reshape(-1, shard, width), ffn_recept[None]], axis=0), core)
    table = Table(params)

    edge = Halo(tokens, cotangent)
    came = launch((), group_a) + launch([info], edge, table)
    halo = edge.rows
    par = table.whole

    ext = (batches, rows, width)
    ext_f, ext_b = shape(ext, F32), shape(ext, BF)
    line_f = shape((batches, width // 128, rows, 128), F32)
    stats_shape = shape((batches, 2, rows, 128), F32)
    ends_shape = shape((batches, 2, 8, width), F32)
    wide_b = shape((batches, rows, ff), BF)
    square = pltpu.VMEM((1, width, width), BF)
    three = pltpu.VMEM((3, width, width), BF)
    square_f = pltpu.VMEM((width, width), F32)
    block_f = pltpu.VMEM((rows, width), F32)
    block_line = pltpu.VMEM((width // 128, rows, 128), F32)
    part = pltpu.VMEM((rows, 128), F32)

    def sems(n):
        return pltpu.SemaphoreType.DMA((n,))

    def refs(group):
        return [(p, ANY) for p in group.pieces]

    info_in = (info, SMEM)

    deps = came
    came = launch(deps, group_a)
    mix_key, mix_value, mix_recept, change_one, tok_ext, cot_ext, stats_one = call(
        "mix",
        functools.partial(mix_kernel, span, seqs),
        (batches,),
        [
            info_in,
            (tokens, pl.BlockSpec((1,) + tokens.shape[1:], lambda i: (i, 0, 0, 0))),
            (cotangent, pl.BlockSpec((1,) + tokens.shape[1:], lambda i: (i, 0, 0, 0))),
            (halo, pl.BlockSpec((2, 1, 2 * PAD, width), lambda i: (0, i, 0, 0))),
            (par, VMEM),
        ],
        [(ext_b, BATCH)] * 6 + [(stats_shape, BATCH)],
        [block_f],
        13,
        deps,
    )
    came = launch(came + [stats_one], group_a, group_b)
    deps, far = came[:2], came[2:]
    state_shape = shape((2 * batches, width), F32)
    exp_key, value, gate_one, ends, state, whole_a = call(
        "project",
        functools.partial(project_kernel, span, seqs),
        (batches,),
        [info_in]
        + [(a, BATCH) for a in (mix_key, mix_value, mix_recept)]
        + [(par, VMEM), (att_key, ANY), (att_value, ANY), (att_recept, ANY)]
        + refs(group_a),
        [(line_f, BATCH)] * 3
        + [(ends_shape, BATCH), (state_shape, VMEM), (pltpu.HBM((3, width, width), BF), ANY)],
        [three, sems(PER + 3)],
        8,
        deps,
    )
    exchange = States(state)
    came = launch(far + [state], exchange)
    came = launch(came, exchange, group_b)
    while exchange.sends():
        came = launch(came, exchange)
    states = exchange.parts
    deps = came
    came = launch(deps, group_b, group_c)
    gated, by_num, by_recept, wkv, middle, ffn_in, ffn_gate_in, change_two, stats_two, whole_out = call(
        "recur",
        functools.partial(recur_kernel, span, seqs, ranks, len(states)),
        (batches,),
        [info_in]
        + [(a, BATCH) for a in (exp_key, value, gate_one)]
        + [(ends, BATCH), (tok_ext, BATCH)]
        + [(par, VMEM), (att_out, ANY)]
        + [(a, VMEM) for a in states]
        + refs(group_a),
        [
            (a, BATCH)
            for a in (ext_b, ext_b, ext_b, ext_b, ext_f, ext_b, ext_b, ext_b, stats_shape)
        ]
        + [(pltpu.HBM((1, width, width), BF), ANY)],
        [square, block_line, block_line, sems(PER + 1)],
        10,
        deps,
    )
    deps = came + [stats_two]
    came = launch(deps, group_c)
    key_buf = pltpu.VMEM((tiles, width, width), BF)
    own_value = ffn_value.reshape(4, shard, width)
    hidden, whole_key = call(
        "hidden",
        hidden_kernel,
        (batches,),
        [info_in, (ffn_in, BATCH), (ffn_key, ANY)] + refs(group_b),
        [(wide_b, BATCH), (pltpu.HBM((tiles, width, width), BF), ANY)],
        [key_buf, sems(tiles + PER + 1)],
        9,
        deps,
    )
    came = launch(came + [hidden], group_c)
    mixed_shape = shape((batches, 1, span, width), BF)
    value_buf = pltpu.VMEM((4 * tiles, shard, width), BF)
    mixed, grad_carried, grad_gate, whole_value, whole_gate = call(
        "gate",
        functools.partial(gate_kernel, span, seqs),
        (batches,),
        [info_in]
        + [(a, BATCH) for a in (hidden, ffn_gate_in, middle, cot_ext)]
        + [(own_value, ANY), (ffn_recept, ANY)]
        + refs(group_c),
        [(mixed_shape, BATCH)]
        + [(ext_b, BATCH)] * 2
        + [(pltpu.HBM(value_buf.shape, BF), ANY), (pltpu.HBM((1, width, width), BF), ANY)],
        [value_buf, square, sems(2 * PER + 2)],
        17,
        came,
    )

    plain = (width // (4 * ranks)) % 8 != 0
    nz = 1 if plain else ranks // 2
    plan = (tuple(range(nz)), plain)

    def core_of(keep, send):
        return Core(*(a.reshape(4, -1, a.shape[-1]) for a in (keep, send)), plain)

    big = pltpu.HBM((4, nz, ff // (8 * nz), width), BF)
    big_spec = pl.BlockSpec((1,) + big.shape[1:], lambda i: (i, 0, 0, 0))
    keep_v, send_v = call(
        "value_grad",
        functools.partial(value_grad_kernel, span, plan),
        (4,),
        [info_in, (hidden, VMEM), (grad_carried, VMEM)],
        [(big, big_spec)] * 2,
        [square_f],
        10,
    )
    core_value = core_of(keep_v, send_v)
    deps = [keep_v]
    came = launch(deps, core_value)
    wide_half = pltpu.HBM((width // 2, ff + width), BF)
    keep_k, send_k = call(
        "gate_back",
        functools.partial(gate_back_kernel, span, plan),
        (1,),
        [info_in, (ffn_gate_in, VMEM), (grad_gate, VMEM)],
        [(wide_half, pl.BlockSpec((width // 2, width), lambda i: (0, tiles)))] * 2,
        [square_f],
        10,
        deps,
    )
    deps = came + [keep_k]
    sum_value = Quarter(core_value)
    came = launch(deps, sum_value)
    out_tile = pl.BlockSpec((width // 2, width), lambda i: (0, i))
    keep_k, send_k, _, grad_in = call(
        "inner",
        functools.partial(inner_kernel, span, plan),
        (tiles,),
        [
            info_in,
            (keep_k, HELD),
            (send_k, HELD),
            (hidden, VMEM),
            (grad_carried, VMEM),
            (ffn_in, VMEM),
            (whole_key, HELD),
            (whole_value, HELD),
        ],
        [(wide_half, out_tile)] * 2 + [(pltpu.VMEM(wide_b.shape, BF), VMEM), (ext_b, VMEM)],
        [
            key_buf,
            value_buf,
            square_f,
            sems(tiles + 1),
        ],
        21,
        deps,
        {1: 0, 2: 1, 3: 2},
    )
    core_key = core_of(keep_k, send_k)
    deps = came + [grad_in]
    came = launch(deps, sum_value, core_key)
    sums_shape = shape((8, width), F32)
    grad_middle, grad_att, grad_recept, grad_num, grad_den, ends_back, state_back, sums = call(
        "attend_back",
        functools.partial(attend_back_kernel, span, seqs),
        (batches,),
        [info_in]
        + [
            (a, LATE if a is cot_ext or a is by_num or a is by_recept or a is wkv else BATCH)
            for a in (
                grad_gate,
                grad_in,
                change_two,
                middle,
                stats_two,
                cot_ext,
                by_num,
                by_recept,
                wkv,
            )
        ]
        + [(par, VMEM), (whole_out, HELD), (whole_gate, HELD)],
        [(a, BATCH) for a in (ext_f, ext_b, ext_b, pltpu.VMEM(line_f.shape, F32), pltpu.VMEM(line_f.shape, F32))]
        + [(ends_shape, BATCH)]
        + [(state_shape, VMEM), (sums_shape, VMEM)],
        [square, square, pltpu.VMEM((4, 8, width), F32), block_f, block_f, part, part, sems(2)],
        18,
        deps,
    )
    exchange = States(state_back)
    came = launch(came, exchange)
    deps = came
    sum_key = Quarter(core_key)
    came = launch(deps, exchange, sum_key)
    two = pltpu.HBM((width // 2, 2 * width), BF)
    keep_o, send_o = call(
        "recept",
        functools.partial(recept_kernel, span, plan),
        (2,),
        [info_in] + [(a, VMEM) for a in (gated, grad_att, mix_recept, grad_recept)],
        [(two, pl.BlockSpec((width // 2, width), lambda i: (0, i)))] * 2,
        [square_f],
        10,
        deps,
    )
    num_prev, den_prev, back_recept = call(
        "again",
        functools.partial(again_kernel, span, seqs, ranks, len(states)),
        (batches,),
        [info_in]
        + [(a, BATCH) for a in (exp_key, value, ends, grad_recept)]
        + [(par, VMEM), (whole_a, HELD)]
        + [(a, VMEM) for a in states],
        [(line_f, BATCH)] * 2 + [(ext_b, BATCH)],
        [pltpu.VMEM((width, width), BF), sems(1)],
        8,
        deps + [keep_o],
    )
    came = came + [back_recept]
    while exchange.sends():
        came = launch(came, exchange)
    states_back = exchange.parts
    core_out = core_of(keep_o, send_o)
    deps = came + [keep_o]
    all_value = Finish(sum_value)
    came = launch(deps, all_value, sum_key, core_out)
    grad_key, grad_value, keep_l, send_l, sums_back = call(
        "recur_back",
        functools.partial(recur_back_kernel, span, seqs, ranks, len(states_back), plan),
        (batches,),
        [info_in]
        + [
            (a, LATE if a is mix_key or a is mix_value else BATCH)
            for a in (
                grad_num,
                grad_den,
                exp_key,
                value,
                num_prev,
                den_prev,
                ends_back,
                mix_key,
                mix_value,
            )
        ]
        + [(par, VMEM)]
        + [(a, VMEM) for a in states_back],
        [(ext_b, BATCH)] * 2 + [(two, VMEM)] * 2 + [(sums_shape, VMEM)],
        [block_line, block_line, square_f, square_f, pltpu.VMEM((2, 8, width), F32)],
        20,
        deps,
    )
    core_last = core_of(keep_l, send_l)
    deps = launch(came + [sums_back], core_last)
    all_key = Finish(sum_key)
    sum_last = Quarter(core_last, core_out)
    came = launch(deps, all_key, sum_last)
    grad_shape = shape((batches, 1, span, width), F32)
    half_table = shape((width // 2, 128), BF)
    inners, parts, keep_p, send_p = call(
        "first_back",
        functools.partial(first_back_kernel, span, seqs, plan),
        (batches,),
        [info_in]
        + [(a, BATCH) for a in (grad_key, grad_value, back_recept)]
        + [(a, LATE) for a in (tok_ext, stats_one, change_one)]
        + [(sums, VMEM), (sums_back, VMEM), (par, VMEM)]
        + [(whole_a, HELD)],
        [(ext_f, BATCH), (stats_shape, BATCH)] + [(half_table, VMEM)] * 2,
        [
            pltpu.VMEM((2, width, width), BF),
            block_f,
            block_f,
            pltpu.VMEM((7, 8, width), F32),
            pltpu.VMEM((width, 128), F32),
            sems(1),
        ],
        18,
        deps,
    )
    core_table = core_of(keep_p, send_p)
    deps = launch(came + [keep_p], core_table)
    sum_table = SmallQuarter(core_table)
    came = launch(deps, sum_last, sum_table)
    (tokens_grad,) = call(
        "tokens_grad",
        functools.partial(tokens_grad_kernel, span),
        (batches,),
        [info_in] + [(a, BATCH) for a in (inners, parts, tok_ext, stats_one, grad_middle)],
        [(grad_shape, BATCH)],
        [],
        7,
        deps,
    )
    all_last = Finish(sum_last, sum_table)
    launch(came + [tokens_grad], all_last)
    key, last = all_key.total, all_last.total
    return (
        mixed,
        tokens_grad,
        last[:, :width],
        last[:, width : 2 * width],
        last[:, 3 * width : 4 * width],
        last[:, 2 * width : 3 * width],
        key[:, :ff],
        all_value.total,
        key[:, ff:],
        last[:, 4 * width : 4 * width + params.shape[1]],
    )


def solution(mesh):
    split = P(("dp", "seq"), None)
    rows = P("dp", None)
    stream = P(None, "dp", "seq", None)
    return jax.shard_map(
        body,
        mesh=mesh,
        in_specs=(stream, stream, P(None, "dp", None)) + (rows,) * 8,
        out_specs=(stream, stream) + (split,) * 8,
        check_vma=False,
    )
```

```python
import functools

import jax
import jax.numpy as jnp
from jax import lax
from jax.experimental import pallas as pl
from jax.experimental.pallas import tpu as pltpu
from jax.sharding import PartitionSpec as P

EPS = 1e-05
BF = jnp.bfloat16
F32 = jnp.float32
PAD = 16
FAR = 1 << 30
PER = 5
HEAD = 4


def bounds_of(info, batch, seqs):
    ends = [jnp.int32(0)]
    for i in range(seqs):
        ends.append(ends[-1] + info[HEAD + batch * seqs + i])
    return ends


def positions(info, row, count):
    return lax.broadcasted_iota(jnp.int32, (count, 128), 0) + (row - PAD + info[0])


def since_start(pos, bounds):
    best = jnp.full(pos.shape, FAR, jnp.int32)
    for b in bounds:
        best = jnp.where(pos >= b, jnp.minimum(best, pos - b), best)
    return best


def until_start(pos, bounds):
    best = jnp.full(pos.shape, FAR, jnp.int32)
    for b in bounds:
        best = jnp.where(pos < b, jnp.minimum(best, b - pos), best)
    return best


def wide(mask, width):
    return jnp.concatenate([mask] * (width // 128), axis=1)


def flag(cond, width):
    return wide(jnp.where(cond, 1.0, 0.0).astype(F32), width)


def keep_flag(pos, bounds, width):
    hit = pos == bounds[0]
    for b in bounds[1:]:
        hit = hit | (pos == b)
    return wide(jnp.where(hit, 0.0, 1.0).astype(F32), width)


def rows_of(count, width):
    return wide(lax.broadcasted_iota(jnp.int32, (count, 128), 0), width)


def down(x, carry):
    rolled = pltpu.roll(x, 1, 0)
    return jnp.where(rows_of(*x.shape) == 0, carry, rolled)


def up(x, carry):
    n = x.shape[0]
    rolled = pltpu.roll(x, n - 1, 0)
    return jnp.where(rows_of(*x.shape) == n - 1, carry, rolled)


def nn(a, b):
    return jnp.dot(a, b, preferred_element_type=F32)


def nt(a, b):
    return lax.dot_general(a, b, (((1,), (1,)), ((), ())), preferred_element_type=F32)


def tn(a, b):
    return lax.dot_general(a, b, (((0,), (0,)), ((), ())), preferred_element_type=F32)


def slabs(span, body, init, reverse=False, unroll=4):
    step = 32
    many = span // step

    def one(i, carry):
        at = many - 1 - i if reverse else i
        return body(pl.multiple_of(PAD + at * step, PAD), step, True, carry)

    first, last = (PAD + span, 0) if reverse else (0, PAD + span)
    carry = body(first, PAD, False, init)
    carry = lax.fori_loop(0, many, one, carry, unroll=unroll)
    return body(last, PAD, False, carry)


def lanes(x):
    return sum(x[:, i : i + 128] for i in range(0, x.shape[1], 128))


def tile(x, i):
    return x[:, i * 128 : (i + 1) * 128]


def row_mean(ref, width):
    total = jnp.sum(ref[...], axis=1, keepdims=True) * (1.0 / width)
    return jnp.broadcast_to(total, ref.shape)


def steps_of(low, high, body, carry, reverse=False, unroll=4):
    def one(i, carry):
        return body(high - 1 - i if reverse else low + i, carry)

    count = high - low
    while count % unroll:
        unroll -= 1
    return lax.fori_loop(0, count, one, carry, unroll=unroll)


def fold(x):
    n, c = x.shape
    return jnp.sum(x.reshape(n // 8, 8, c), axis=0)


def no_start(bounds, low, high):
    hit = jnp.int32(0)
    for b in bounds:
        hit = hit | jnp.where((b > low) & (b <= high), 1, 0)
    return jnp.where(hit == 0, 1.0, 0.0).astype(F32)


def incoming(info, states, batch, bounds, speed, span, ranks, reverse):
    me, base = info[2], info[0]
    num = jnp.zeros(speed.shape, F32)
    den = jnp.zeros(speed.shape, F32)
    for k in range(1, ranks):
        other = me ^ k
        if reverse:
            gap = other - me - 1
            clear = no_start(bounds, base + span + 1, other * span + 1)
        else:
            gap = me - 1 - other
            clear = no_start(bounds, (other + 1) * span - 2, base - 2)
        use = jnp.where(gap >= 0, clear, 0.0).astype(F32)
        weight = jnp.exp(-speed * (jnp.maximum(gap, 0) * span).astype(F32)) * use
        per = sum(r.shape[0] for r in states) // ranks
        many = states[0].shape[0] // per
        at = (k % many) * per + 2 * batch
        num += weight * states[k // many][pl.ds(at, 1), :]
        den += weight * states[k // many][pl.ds(at + 1, 1), :]
    return num, den


def start_all(copies):
    for c in copies:
        c.start()


def wait_all(copies):
    for c in copies:
        c.wait()


def copies_of(info, owns, pieces, blocks, target, sems, at=0):
    d, c = info[1], info[3]
    shard = owns[0].shape[0]
    half = shard // 2
    out = []
    for k, own in enumerate(owns):
        out.append(pltpu.make_async_copy(own, target.at[k, pl.ds(pl.multiple_of(d * shard, 16), shard)], sems.at[at]))
        at += 1
    places = ((d ^ (1 + c)) * shard, (d ^ (2 - c)) * shard, (d ^ 3) * shard + c * half, (d ^ 3) * shard + (1 - c) * half)
    for row, ref in zip(places, pieces):
        source = ref.at[blocks]
        place = target.at[:, pl.ds(pl.multiple_of(row, 16), source.shape[1])]
        out.append(pltpu.make_async_copy(source, place, sems.at[at]))
        at += 1
    return out


def value_copies(info, own, pieces, target, sems, at=0):
    d, c = info[1], info[3]
    half = target.shape[1] // 2
    out = [pltpu.make_async_copy(own, target.at[pl.ds(4 * d, 4)], sems.at[at])]
    places = ((d ^ (1 + c), 0), (d ^ (2 - c), 0), (d ^ 3, c * half), (d ^ 3, (1 - c) * half))
    for (block, row), ref in zip(places, pieces):
        at += 1
        place = target.at[pl.ds(4 * block, 4), pl.ds(pl.multiple_of(row, 16), ref.shape[1])]
        out.append(pltpu.make_async_copy(ref.at[pl.ds(0, 4)], place, sems.at[at]))
    return out


def place(info, plain):
    if plain:
        return 0, 0, 0
    return info[1], info[2] // 2, info[3]


def turn(core, i):
    return core * i + (1 - core) * (((i & 1) << 1) | (i >> 1))


def scatter_rows(info, src, keep, send, plan, write):
    nz, plain = plan
    d, z, c = place(info, plain)
    block = src.shape[0] // (8 * nz)
    per = 4 * nz * block // 16
    groups = block // 8
    for ref, core in ((keep, c), (send, 1 - c)):
        for slab in range(per):
            parts = []
            for g in (2 * slab, 2 * slab + 1):
                i = g % groups
                q = (g // groups) % nz
                p = g // (groups * nz)
                if not plain:
                    p, q = turn(core, p), turn(core, q)
                row = ((d ^ p) * nz + (z ^ q)) * (2 * block) + core * block + i * 8
                parts.append(src[pl.ds(pl.multiple_of(row, 8), 8), :])
            write(ref, slab * 16, jnp.concatenate(parts, axis=0).astype(BF))


def keep_whole(batch, buffer, target, sem):
    def copy():
        return pltpu.make_async_copy(buffer, target, sem)

    pl.when(batch == 0)(lambda: copy().start())
    pl.when(batch == pl.num_programs(0) - 1)(lambda: copy().wait())


class Late:
    def __init__(self, source, buffer, sems, index):
        self.source, self.buffer, self.sems, self.index = source, buffer, sems, index
        self.shape = (1,) + tuple(buffer.shape[1:])

    def copy(self, b):
        return pltpu.make_async_copy(self.source.at[b], self.buffer.at[b], self.sems.at[self.index, b])

    def ready(self):
        b = pl.program_id(0)
        self.copy(b).wait()
        return self.buffer.at[pl.ds(b, 1)]


def mix_kernel(
    span, seqs, info, tokens, cotangent, halo, par, mix_key, mix_value, mix_recept, change, tok_ext, cot_ext, stats, held
):
    batch = pl.program_id(0)
    bounds = bounds_of(info, batch, seqs)
    gain, bias = par[0:1, :], par[1:2, :]
    mixes = (par[2:3, :], par[3:4, :], par[4:5, :])
    width = tokens.shape[3]
    mean, scale = stats.at[0, 0], stats.at[0, 1]

    def load(row, n, owned, carry):
        at = pl.ds(row, n)
        if owned:
            x, g = tokens[0, 0, pl.ds(row - PAD, n), :], cotangent[0, 0, pl.ds(row - PAD, n), :]
        else:
            low = 0 if row == 0 else PAD
            x, g = halo[0, 0, low : low + PAD, :], halo[1, 0, low : low + PAD, :]
        tok_ext[0, at, :] = x
        cot_ext[0, at, :] = g
        x = x.astype(F32)
        held[at, :] = x
        mean[at, :] = lanes(x)
        return carry

    slabs(span, load, 0)
    mean[...] = row_mean(mean, width)

    def spread(row, n, owned, carry):
        at = pl.ds(row, n)
        x = held[at, :] - wide(mean[at, :], width)
        scale[at, :] = lanes(x * x)
        return carry

    slabs(span, spread, 0)
    scale[...] = lax.rsqrt(row_mean(scale, width) + EPS)

    def body(row, n, owned, carry):
        at = pl.ds(row, n)
        normed = (held[at, :] - wide(mean[at, :], width)) * wide(scale[at, :], width)
        first = normed * gain + bias
        keep = keep_flag(positions(info, row, n), bounds, width)
        shifted = down(first, carry) * keep
        diff = first - shifted
        for mu, ref in zip(mixes, (mix_key, mix_value, mix_recept)):
            ref[0, at, :] = (shifted + diff * mu).astype(BF)
        change[0, at, :] = diff.astype(BF)
        return first[n - 1 : n]

    slabs(span, body, jnp.zeros((1, width), F32))


class Chunks:
    def __init__(self, info, bounds, rows, speed):
        self.size = rows // 8
        self.bounds = bounds
        self.base = info[0] - PAD
        self.row8 = lax.broadcasted_iota(jnp.int32, (8, 128), 0)
        self.start = self.row8 * self.size + self.base
        self.speed = speed
        self.tiles = speed.shape[1] // 128
        self.rate = self.split(jnp.exp(-speed))

    def split(self, row):
        return [jnp.broadcast_to(tile(row, i), (8, 128)) for i in range(self.tiles)]

    def at(self, j):
        return pl.ds(j, 8, stride=self.size)

    def keep(self, j, ahead=0):
        pos = self.start + (j + ahead)
        hit = pos == self.bounds[0]
        for b in self.bounds[1:]:
            hit = hit | (pos == b)
        return jnp.where(hit, 0.0, 1.0).astype(F32)

    def decay(self, low, high, count):
        clear = no_start(self.bounds, self.base + low, self.base + high)
        return jnp.exp(-self.speed * float(count)) * clear


def join(tiles):
    return jnp.concatenate(tiles, axis=1)


def write_state(state, batch, num, den):
    for i in range(state.shape[0] // 2):

        @pl.when(batch == i)
        def _():
            state[2 * i : 2 * i + 1, :] = num
            state[2 * i + 1 : 2 * i + 2, :] = den


def project_kernel(
    span, seqs, info, mix_key, mix_value, mix_recept, par, own_key, own_value, own_recept, *refs
):
    pieces = refs[0:4]
    exp_key, value, gate, ends, state, kept, weights, sems = refs[4:]
    batch = pl.program_id(0)
    bounds = bounds_of(info, batch, seqs)
    rows, width = mix_key.shape[1:]

    def copies():
        return copies_of(info, (own_key, own_value, own_recept), pieces, pl.ds(0, 3), weights, sems)

    @pl.when(batch == 0)
    def _():
        start_all(copies())
        wait_all(copies())

    acts = (jnp.exp, lambda x: x, jax.nn.sigmoid)
    for k, (left, ref, act) in enumerate(zip((mix_key, mix_value, mix_recept), (exp_key, value, gate), acts)):
        part = act(nn(left[0], weights[k]))
        for i in range(width // 128):
            ref[0, i] = tile(part, i)

    speed = jnp.exp(par[5:6, :])
    chunks = Chunks(info, bounds, rows, speed)
    size = chunks.size

    def step(j, carry, cut=False):
        nums, dens = carry
        at = chunks.at(j)
        keep = chunks.keep(j)
        num_out, den_out = [], []
        for i in range(chunks.tiles):
            ek = exp_key[0, i, at, :]
            if cut:
                ek = jnp.where(chunks.row8 == 0, 0.0, ek)
            factor = chunks.rate[i] * keep
            num_out.append(factor * nums[i] + ek * value[0, i, at, :])
            den_out.append(factor * dens[i] + ek)
        return tuple(num_out), tuple(den_out)

    zero = tuple(jnp.zeros((8, 128), F32) for _ in range(chunks.tiles))
    last = PAD + span - 2 - 7 * size
    carry = (zero, zero)
    for j in range(PAD - 1):
        carry = step(j, carry, cut=True)
    carry = steps_of(PAD - 1, last + 1, step, carry)
    inside = [join(c)[7:8] for c in carry]
    carry = steps_of(last + 1, size, step, carry, unroll=size)
    whole_ends = [join(c) for c in carry]
    out = []
    for k in range(2):
        ends[0, k] = whole_ends[k]
        total = whole_ends[k][0:1]
        for s in range(1, 7):
            total = whole_ends[k][s : s + 1] + chunks.decay(s * size - 1, (s + 1) * size - 1, size) * total
        out.append(inside[k] + chunks.decay(7 * size - 1, 7 * size + last, last + 1) * total)
    write_state(state, batch, *out)
    keep_whole(batch, weights, kept, sems.at[PER + 2])


def forward_scan(info, states, batch, chunks, exp_key, value, ends, span, ranks, emit):
    size, width = chunks.size, chunks.speed.shape[1]
    entering = incoming(info, states, batch, chunks.bounds, chunks.speed, span, ranks, False)
    begin = []
    for k in range(2):
        lines = [jnp.zeros((1, width), F32)]
        lines.append(ends[0, k, 0:1, :] + chunks.decay(PAD - 2, size - 1, size - PAD + 1) * entering[k])
        for s in range(1, 7):
            lines.append(ends[0, k, s : s + 1, :] + chunks.decay(s * size - 1, (s + 1) * size - 1, size) * lines[-1])
        begin.append(jnp.concatenate(lines, axis=0))
    carry = tuple(tuple(tile(b, i) for i in range(chunks.tiles)) for b in begin)

    def step(j, carry, insert=None):
        nums, dens = carry
        at = chunks.at(j)
        keep = chunks.keep(j)
        num_out, den_out = [], []
        for i in range(chunks.tiles):
            ek, v = exp_key[0, i, at, :], value[0, i, at, :]
            before_num = keep * nums[i]
            before_den = keep * dens[i]
            x, y = ek * v, ek
            emit(at, i, before_num, before_den, ek, x)
            if insert is not None:
                x = jnp.where(chunks.row8 == 0, insert[0][i], x)
                y = jnp.where(chunks.row8 == 0, insert[1][i], y)
            num_out.append(chunks.rate[i] * before_num + x)
            den_out.append(chunks.rate[i] * before_den + y)
        return tuple(num_out), tuple(den_out)

    none = [[0.0] * chunks.tiles] * 2
    for j in range(PAD - 2):
        carry = step(j, carry, none)
    carry = step(PAD - 2, carry, [chunks.split(e) for e in entering])
    steps_of(PAD - 1, size, step, carry)


def recur_kernel(span, seqs, ranks, parts, info, exp_key, value, gate, ends, tokens, par, own_out, *refs):
    states, refs = refs[:parts], refs[parts:]
    pieces = refs[0:4]
    (
        gated,
        by_num,
        by_recept,
        wkv,
        middle,
        ffn_in,
        ffn_gate_in,
        change,
        stats,
        kept,
        wo,
        line_wkv,
        line_inverse,
        sems,
    ) = refs[4:]
    batch = pl.program_id(0)
    bounds = bounds_of(info, batch, seqs)
    rows, width = tokens.shape[1:]

    def copies():
        return copies_of(info, (own_out,), pieces, pl.ds(3, 1), wo, sems)

    @pl.when(batch == 0)
    def _():
        start_all(copies())

    chunks = Chunks(info, bounds, rows, jnp.exp(par[5:6, :]))
    boost = chunks.split(jnp.exp(par[6:7, :]))

    def emit(at, i, before_num, before_den, ek, x):
        inverse = 1.0 / (before_den + boost[i] * ek)
        line_inverse[i, at, :] = inverse
        line_wkv[i, at, :] = (before_num + boost[i] * x) * inverse

    forward_scan(info, states, batch, chunks, exp_key, value, ends, span, ranks, emit)

    def pack(row, n, owned, carry):
        at = pl.ds(row, n)
        out = ([], [], [], [])
        for i in range(chunks.tiles):
            w, sig = line_wkv[i, at, :], gate[0, i, at, :]
            g = w * sig
            out[0].append(g)
            out[1].append(sig * line_inverse[i, at, :])
            out[2].append(g * (1.0 - sig))
            out[3].append(w)
        for ref, tiles in zip((gated, by_num, by_recept, wkv), out):
            ref[0, at, :] = join(tiles).astype(BF)
        return carry

    slabs(span, pack, 0)

    @pl.when(batch == 0)
    def _():
        wait_all(copies())

    middle[0] = nn(gated[0], wo[0])
    gain, bias = par[7:8, :], par[8:9, :]
    mean, scale = stats.at[0, 0], stats.at[0, 1]

    def residual(row, n, owned, carry):
        at = pl.ds(row, n)
        mid = middle[0, at, :] + tokens[0, at, :].astype(F32)
        middle[0, at, :] = mid
        mean[at, :] = lanes(mid)
        return carry

    slabs(span, residual, 0)
    mean[...] = row_mean(mean, width)

    def spread(row, n, owned, carry):
        at = pl.ds(row, n)
        x = middle[0, at, :] - wide(mean[at, :], width)
        scale[at, :] = lanes(x * x)
        return carry

    slabs(span, spread, 0)
    scale[...] = lax.rsqrt(row_mean(scale, width) + EPS)

    def body(row, n, owned, carry):
        at = pl.ds(row, n)
        normed = (middle[0, at, :] - wide(mean[at, :], width)) * wide(scale[at, :], width)
        second = normed * gain + bias
        keep = keep_flag(positions(info, row, n), bounds, width)
        shifted = down(second, carry) * keep
        diff = second - shifted
        ffn_in[0, at, :] = (shifted + diff * par[9:10, :]).astype(BF)
        ffn_gate_in[0, at, :] = (shifted + diff * par[10:11, :]).astype(BF)
        change[0, at, :] = diff.astype(BF)
        return second[n - 1 : n]

    slabs(span, body, jnp.zeros((1, width), F32))
    keep_whole(batch, wo, kept, sems.at[PER])


def hidden_kernel(info, ffn_in, own_key, *refs):
    pieces = refs[0:4]
    hidden, kept, wk, sems = refs[4:]
    width = ffn_in.shape[2]
    tiles = wk.shape[0]

    def copies():
        owns = [own_key.at[:, pl.ds(j * width, width)] for j in range(tiles)]
        return copies_of(info, owns, pieces, pl.ds(0, tiles), wk, sems)

    @pl.when(pl.program_id(0) == 0)
    def _():
        start_all(copies())
        wait_all(copies())

    for j in range(tiles):
        relu = jnp.maximum(nn(ffn_in[0], wk[j]), 0.0)
        hidden[0, :, pl.ds(j * width, width)] = (relu * relu).astype(BF)
    keep_whole(pl.program_id(0), wk, kept, sems.at[tiles + PER])


def gate_kernel(
    span, seqs, info, hidden, ffn_gate_in, middle, cotangent, own_value, own_recept, *refs
):
    pieces = refs[0:4]
    mixed, grad_carried, grad_gate, kept, kept_gate, wv, wr, sems = refs[4:]
    batch = pl.program_id(0)
    bounds = bounds_of(info, batch, seqs)
    rows, width = middle.shape[1:]

    def copies():
        return (
            copies_of(info, (own_recept,), pieces, pl.ds(4, 1), wr, sems),
            value_copies(info, own_value, pieces, wv, sems, PER),
        )

    @pl.when(batch == 0)
    def _():
        for c in copies():
            start_all(c)
        wait_all(copies()[0])
    keep_whole(batch, wv, kept, sems.at[2 * PER])
    keep_whole(batch, wr, kept_gate, sems.at[2 * PER + 1])


    @pl.when(batch == 0)
    def _():
        wait_all(copies()[1])

    flat = wv[...].reshape(wv.shape[0] * wv.shape[1], width)
    total = bounds[-1]
    step = rows // 2
    for low in range(0, rows, step):
        gate = nn(ffn_gate_in[0, low : low + step, :], wr[0])
        carried = nn(hidden[0, low : low + step, :], flat)
        for i in range(0, step, PAD):
            row = low + i
            at = pl.ds(row, PAD)
            sig = jax.nn.sigmoid(gate[i : i + PAD])
            car = carried[i : i + PAD]
            live = flag(positions(info, row, PAD) < total, width)
            grad = cotangent[0, at, :].astype(F32) * live
            if PAD <= row < PAD + span:
                mixed[0, 0, row - PAD : row, :] = (middle[0, at, :] + sig * car).astype(BF)
            part = grad * sig
            grad_carried[0, at, :] = part.astype(BF)
            grad_gate[0, at, :] = (part * car * (1.0 - sig)).astype(BF)


def over_own(left, right, span):
    own = pl.ds(PAD, span)
    both = [jnp.concatenate([f[b, own] for b in range(f.shape[0])], axis=0) for f in (left, right)]
    return tn(*both)


def store_sixteen(ref, row, value):
    ref[row : row + 16, :] = value


def value_grad_kernel(span, plan, info, hidden, grad_carried, keep, send, total):
    nz, plain = plan
    d, z, c = place(info, plain)
    width = total.shape[1]
    column = pl.ds(pl.multiple_of((pl.program_id(0) ^ d) * width, width), width)
    block = keep.shape[2]
    total[...] = over_own(hidden.at[:, :, column], grad_carried, span)
    for q in range(nz):
        for ref, core in ((keep, c), (send, 1 - c)):
            row = pl.multiple_of(((z ^ (q if plain else turn(core, q))) * 2 + core) * block, 8)
            ref[0, q] = total[pl.ds(row, block), :].astype(BF)


def gate_back_kernel(span, plan, info, ffn_gate_in, grad_gate, keep, send, total):
    total[...] = over_own(ffn_gate_in, grad_gate, span)
    scatter_rows(info, total, keep, send, plan, store_sixteen)


def inner_kernel(
    span, plan, info, _, __, hidden, grad_carried, ffn_in, key, whole_value, keep, send, grad_inner, grad_in, wk, wv, total, sems
):
    step = pl.program_id(0)
    batches, _, width = grad_in.shape
    tiles = wk.shape[0]

    def copies():
        out = []
        for j in range(tiles):
            block = pl.ds(4 * j, 4)
            out.append(pltpu.make_async_copy(whole_value.at[block], wv.at[block], sems.at[j]))
        return out + [pltpu.make_async_copy(key, wk, sems.at[tiles])]

    @pl.when(step == 0)
    def _():
        start_all(copies())

    here = pl.multiple_of(step * width, width)
    for j in range(tiles):
        pl.when(step == j)(lambda: copies()[j].wait())
    value = wv[pl.ds(4 * step, 4)].reshape(4 * wv.shape[1], width)
    for b in range(batches):
        back = nt(grad_carried[b], value)
        at = pl.ds(here, width)
        square = hidden[b, :, at].astype(F32)
        relu = square * lax.rsqrt(jnp.maximum(square, 1e-30))
        grad_inner[b, :, at] = (back * (2.0 * relu)).astype(BF)
    total[...] = over_own(ffn_in, grad_inner.at[:, :, pl.ds(here, width)], span)
    scatter_rows(info, total, keep, send, plan, store_sixteen)

    @pl.when(step == tiles - 1)
    def _():
        copies()[tiles].wait()
        right = jnp.concatenate([wk[j] for j in range(tiles)], axis=1)
        for b in range(batches):
            grad_in[b] = nt(grad_inner[b], right).astype(BF)


def attend_back_kernel(
    span,
    seqs,
    info,
    grad_gate,
    grad_in,
    change,
    middle,
    stats,
    cotangent,
    by_num,
    by_recept,
    wkv,
    par,
    whole_out,
    whole_gate,
    *refs,
):
    (grad_middle, grad_att, grad_recept, grad_num, grad_den, ends, state, sums, wo, wr, acc, held, back_gate, part_a, part_b, sems) = refs
    batch = pl.program_id(0)
    bounds = bounds_of(info, batch, seqs)
    rows, width = middle.shape[1:]

    def copies():
        return [pltpu.make_async_copy(whole_out, wo, sems.at[0])]

    def gate_copies():
        return [pltpu.make_async_copy(whole_gate, wr, sems.at[1])]

    @pl.when(batch == 0)
    def _():
        start_all(gate_copies())
        start_all(copies())
        acc[...] = jnp.zeros_like(acc)

    gain = par[7:8, :]
    mu, nu = par[9:10, :], par[10:11, :]
    total = bounds[-1]

    @pl.when(batch == 0)
    def _():
        wait_all(gate_copies())

    back_gate[...] = nt(grad_gate[0], wr[0])
    mean, scale = stats.at[0, 0], stats.at[0, 1]

    def normed_of(at):
        return (middle[0, at, :] - wide(mean[at, :], width)) * wide(scale[at, :], width)

    def gather(row, n, owned, carry):
        at = pl.ds(row, n)
        a, b = grad_in[0, at, :].astype(F32), back_gate[at, :]
        keep = keep_flag(positions(info, row, n), bounds, width)
        normed = normed_of(at)
        direct = a * mu + b * nu
        moved = (a + b - direct) * keep
        second = direct + up(moved, carry)
        if owned:
            diff = change[0, at, :].astype(F32)
            acc[0] += fold(second * normed)
            acc[1] += fold(second)
            acc[2] += fold(a * diff)
            acc[3] += fold(b * diff)
        inner = second * gain
        held[at, :] = inner
        part_a[at, :] = lanes(inner)
        part_b[at, :] = lanes(inner * normed)
        return moved[0:1]

    slabs(span, gather, jnp.zeros((1, width), F32), reverse=True)
    part_a[...] = row_mean(part_a, width)
    part_b[...] = row_mean(part_b, width)


    def apply(row, n, owned, carry):
        at = pl.ds(row, n)
        back = wide(scale[at, :], width) * (
            held[at, :] - wide(part_a[at, :], width) - normed_of(at) * wide(part_b[at, :], width)
        )
        live = flag(positions(info, row, n) < total, width)
        grad = cotangent[0, at, :].astype(F32) * live + back
        grad_middle[0, at, :] = grad
        grad_att[0, at, :] = grad.astype(BF)
        return carry

    cotangent = cotangent.ready()
    slabs(span, apply, 0)

    @pl.when(batch == 0)
    def _():
        wait_all(copies())

    held[...] = nt(grad_att[0], wo[0])
    speed = jnp.exp(par[5:6, :])
    chunks = Chunks(info, bounds, rows, speed)
    size = chunks.size


    def point(row, n, owned, carry):
        at = pl.ds(row, n)
        back = held[at, :]
        num = back * by_num[0, at, :].astype(F32)
        den = num * wkv[0, at, :].astype(F32)
        for i in range(chunks.tiles):
            grad_num[0, i, at, :] = tile(num, i)
            grad_den[0, i, at, :] = -tile(den, i)
        grad_recept[0, at, :] = (back * by_recept[0, at, :].astype(F32)).astype(BF)
        return carry

    by_num, by_recept, wkv = by_num.ready(), by_recept.ready(), wkv.ready()
    slabs(span, point, 0)

    def step(j, carry, cut=False):
        nums, dens = carry
        at = chunks.at(j)
        keep = chunks.keep(j, 1)
        num_out, den_out = [], []
        for i in range(chunks.tiles):
            gn, gd = grad_num[0, i, at, :], grad_den[0, i, at, :]
            if cut:
                gn, gd = jnp.where(chunks.row8 == 7, 0.0, gn), jnp.where(chunks.row8 == 7, 0.0, gd)
            factor = chunks.rate[i] * keep
            num_out.append(factor * nums[i] + gn)
            den_out.append(factor * dens[i] + gd)
        return tuple(num_out), tuple(den_out)

    zero = tuple(jnp.zeros((8, 128), F32) for _ in range(chunks.tiles))
    after = PAD + span + 1 - 7 * size
    carry = (zero, zero)
    for j in reversed(range(after, size)):
        carry = step(j, carry, cut=True)
    carry = steps_of(PAD + 1, after, step, carry, reverse=True)
    inside = [join(c)[0:1] for c in carry]
    carry = steps_of(0, PAD + 1, step, carry, reverse=True, unroll=size)
    whole_ends = [join(c) for c in carry]
    out = []
    for k in range(2):
        ends[0, k] = whole_ends[k]
        line = whole_ends[k][7:8]
        for s in range(6, 0, -1):
            line = whole_ends[k][s : s + 1] + chunks.decay(s * size, (s + 1) * size, size) * line
        out.append(inside[k] + chunks.decay(PAD + 1, size, size - PAD - 1) * line)
    write_state(state, batch, *out)

    @pl.when(batch == pl.num_programs(0) - 1)
    def _():
        sums[...] = jnp.zeros_like(sums)
        for i in range(4):
            sums[i : i + 1, :] = jnp.sum(acc[i], axis=0, keepdims=True)


def recept_kernel(span, plan, info, gated, grad_att, mix_recept, grad_recept, keep, send, total):
    def grad(left, right):
        total[...] = over_own(left, right, span)
        scatter_rows(info, total, keep, send, plan, store_sixteen)

    pl.when(pl.program_id(0) == 0)(lambda: grad(gated, grad_att))
    pl.when(pl.program_id(0) == 1)(lambda: grad(mix_recept, grad_recept))


def again_kernel(span, seqs, ranks, parts, info, exp_key, value, ends, grad_recept, par, whole_a, *refs):
    states, (num_prev, den_prev, back_recept, wr, sems) = refs[:parts], refs[parts:]
    batch = pl.program_id(0)
    bounds = bounds_of(info, batch, seqs)
    chunks = Chunks(info, bounds, grad_recept.shape[1], jnp.exp(par[5:6, :]))

    def copy():
        return pltpu.make_async_copy(whole_a.at[2], wr, sems.at[0])

    pl.when(batch == 0)(lambda: copy().start())

    def emit(at, i, before_num, before_den, ek, x):
        num_prev[0, i, at, :] = before_num
        den_prev[0, i, at, :] = before_den

    forward_scan(info, states, batch, chunks, exp_key, value, ends, span, ranks, emit)
    pl.when(batch == 0)(lambda: copy().wait())
    back_recept[0] = nt(grad_recept[0], wr[...]).astype(BF)


def recur_back_kernel(
    span,
    seqs,
    ranks,
    parts,
    plan,
    info,
    grad_num,
    grad_den,
    exp_key,
    value,
    num_prev,
    den_prev,
    ends,
    mix_key,
    mix_value,
    par,
    *refs,
):
    states, refs = refs[:parts], refs[parts:]
    grad_key, grad_value, keep, send, sums, line_key, line_value, total, total2, acc = refs
    batch = pl.program_id(0)
    bounds = bounds_of(info, batch, seqs)
    rows, width = mix_key.shape[1:]

    @pl.when(batch == 0)
    def _():
        acc[...] = jnp.zeros_like(acc)

    speed = jnp.exp(par[5:6, :])
    chunks = Chunks(info, bounds, rows, speed)
    size = chunks.size
    boost = chunks.split(jnp.exp(par[6:7, :]))
    entering = incoming(info, states, batch, bounds, speed, span, ranks, True)
    after = PAD + span + 1 - 7 * size
    begin = []
    for k in range(2):
        lines = [jnp.zeros((1, width), F32)]
        lines.append(ends[0, k, 7:8, :] + chunks.decay(7 * size, 7 * size + after, after) * entering[k])
        for s in range(6, 0, -1):
            lines.append(ends[0, k, s : s + 1, :] + chunks.decay(s * size, (s + 1) * size, size) * lines[-1])
        begin.append(jnp.concatenate(lines[::-1], axis=0))
    zero = tuple(jnp.zeros((8, 128), F32) for _ in range(chunks.tiles))
    carry = tuple(tuple(tile(b, i) for i in range(chunks.tiles)) for b in begin) + (zero, zero)

    def step(j, carry, insert=None, mask=None):
        nums, dens, bonuses, decays = carry
        at = chunks.at(j)
        keep_next = chunks.keep(j, 1)
        outs = ([], [], [], [])
        for i in range(chunks.tiles):
            gn, ek, v = grad_num[0, i, at, :], exp_key[0, i, at, :], value[0, i, at, :]
            gd = grad_den[0, i, at, :]
            after_num = keep_next * nums[i]
            after_den = keep_next * dens[i]
            bek = boost[i] * ek
            bonus = bek * (v * gn + gd)
            line_key[i, at, :] = bonus + ek * (v * after_num + after_den)
            line_value[i, at, :] = bek * gn + ek * after_num
            decay = num_prev[0, i, at, :] * after_num + den_prev[0, i, at, :] * after_den
            if mask is not None:
                bonus = jnp.where(mask, bonus, 0.0)
                decay = jnp.where(mask, decay, 0.0)
            if insert is not None:
                gn = jnp.where(chunks.row8 == 7, insert[0][i], gn)
                gd = jnp.where(chunks.row8 == 7, insert[1][i], gd)
            outs[0].append(chunks.rate[i] * after_num + gn)
            outs[1].append(chunks.rate[i] * after_den + gd)
            outs[2].append(bonuses[i] + bonus)
            outs[3].append(decays[i] + decay)
        return tuple(tuple(o) for o in outs)

    none = [[0.0] * chunks.tiles] * 2
    upper = chunks.row8 < 7
    for j in reversed(range(after + 1, size)):
        carry = step(j, carry, none, upper)
    carry = step(after, carry, [chunks.split(e) for e in entering], upper)
    edge = PAD + span - 7 * size
    for j in reversed(range(edge, after)):
        carry = step(j, carry, None, upper)
    carry = steps_of(PAD, edge, step, carry, reverse=True)
    lower = chunks.row8 > 0
    carry = steps_of(0, PAD, lambda j, c: step(j, c, None, lower), carry, reverse=True)
    acc[0] += join(carry[2])
    acc[1] += join(carry[3])

    def pack(row, n, owned, carry):
        at = pl.ds(row, n)
        grad_key[0, at, :] = join([line_key[i, at, :] for i in range(chunks.tiles)]).astype(BF)
        grad_value[0, at, :] = join([line_value[i, at, :] for i in range(chunks.tiles)]).astype(BF)
        return carry

    slabs(span, pack, 0)
    mix_key, mix_value = mix_key.ready(), mix_value.ready()
    own = pl.ds(PAD, span)
    key_part = tn(mix_key[0, own, :], grad_key[0, own, :])
    value_part = tn(mix_value[0, own, :], grad_value[0, own, :])

    @pl.when(batch == 0)
    def _():
        total[...] = key_part
        total2[...] = value_part

    @pl.when(batch > 0)
    def _():
        total[...] += key_part
        total2[...] += value_part

    @pl.when(batch == pl.num_programs(0) - 1)
    def _():
        sums[...] = jnp.zeros_like(sums)
        for i in range(2):
            sums[i : i + 1, :] = jnp.sum(acc[i], axis=0, keepdims=True)
        for source, low in ((total, 0), (total2, width)):

            def write(ref, row, value):
                ref[row : row + 16, low : low + width] = value

            scatter_rows(info, source, keep, send, plan, write)


def first_back_kernel(
    span,
    seqs,
    plan,
    info,
    grad_key,
    grad_value,
    back_recept,
    tokens,
    stats,
    change,
    sums,
    sums_back,
    par,
    whole_a,
    *refs,
):
    inners, part_ref, keep, send, weights, back_key, back_value, acc, turned, sems = refs
    part_a, part_b = part_ref.at[0, 0], part_ref.at[0, 1]
    batch = pl.program_id(0)
    bounds = bounds_of(info, batch, seqs)
    width = tokens.shape[2]

    def copies():
        return [pltpu.make_async_copy(whole_a.at[pl.ds(0, 2)], weights, sems.at[0])]

    @pl.when(batch == 0)
    def _():
        start_all(copies())
        acc[...] = jnp.zeros_like(acc)
        wait_all(copies())

    back_key[...] = nt(grad_key[0], weights[0])
    back_value[...] = nt(grad_value[0], weights[1])
    gain = par[0:1, :]
    mixes = (par[2:3, :], par[3:4, :], par[4:5, :])
    tokens, stats, change = tokens.ready(), stats.ready(), change.ready()
    mean, scale = stats.at[0, 0], stats.at[0, 1]

    def normed_of(at):
        return (tokens[0, at, :].astype(F32) - wide(mean[at, :], width)) * wide(scale[at, :], width)

    def gather(row, n, owned, carry):
        at = pl.ds(row, n)
        parts = (back_key[at, :], back_value[at, :], back_recept[0, at, :].astype(F32))
        keep = keep_flag(positions(info, row, n), bounds, width)
        direct = sum(g * mu for g, mu in zip(parts, mixes))
        moved = (parts[0] + parts[1] + parts[2] - direct) * keep
        if owned:
            normed = normed_of(at)
            first = direct + up(moved, carry)
            diff = change[0, at, :].astype(F32)
            acc[2] += fold(first * normed)
            acc[3] += fold(first)
            for i in range(3):
                acc[4 + i] += fold(parts[i] * diff)
            inner = first * gain
            inners[0, at, :] = inner
            part_a[at, :] = lanes(inner)
            part_b[at, :] = lanes(inner * normed)
        return moved[0:1]

    slabs(span, gather, jnp.zeros((1, width), F32), reverse=True)
    part_a[...] = row_mean(part_a, width)
    part_b[...] = row_mean(part_b, width)

    @pl.when(batch == pl.num_programs(0) - 1)
    def _():
        def final(i):
            return jnp.sum(acc[i], axis=0, keepdims=True)

        speed = jnp.exp(par[5:6, :])
        decay = sums_back[1:2, :] * jnp.exp(-speed) * -speed
        columns = [final(i) for i in (2, 3, 4, 5, 6)] + [decay, sums_back[0:1, :]]
        columns += [sums[i : i + 1, :] for i in range(4)]
        stacked = jnp.concatenate(columns + [jnp.zeros((128 - len(columns), width), F32)], axis=0)
        turned[...] = stacked.T
        scatter_rows(info, turned, keep, send, plan, store_sixteen)


def tokens_grad_kernel(span, info, inners, parts, tokens, stats, grad_middle, tokens_grad):
    width = inners.shape[2]
    mean, scale = stats.at[0, 0], stats.at[0, 1]
    part_a, part_b = parts.at[0, 0], parts.at[0, 1]

    def apply(row, n, owned, carry):
        if owned:
            at = pl.ds(row, n)
            rate = wide(scale[at, :], width)
            normed = (tokens[0, at, :].astype(F32) - wide(mean[at, :], width)) * rate
            back = rate * (inners[0, at, :] - wide(part_a[at, :], width) - normed * wide(part_b[at, :], width))
            tokens_grad[0, 0, pl.ds(row - PAD, n), :] = grad_middle[0, at, :] + back
        return carry

    slabs(span, apply, 0)


def swap(x, kind):
    devices, size = lax.axis_size("dp"), lax.axis_size("seq")
    if kind == "next":
        return lax.ppermute(x, "seq", [(i, i + 1) for i in range(size - 1)])
    if kind == "last":
        return lax.ppermute(x, "seq", [(i + 1, i) for i in range(size - 1)])
    if isinstance(kind, int):
        return lax.ppermute(x, "seq", [(i, i ^ kind) for i in range(size)])
    masks = {"xy": ((1, 0), (2, 0)), "yx": ((2, 0), (1, 0)), "over": ((3, 0), (3, 0)), "near": ((0, 2), (0, 4)), "far": ((0, 4), (0, 2))}
    pairs = []
    for d in range(devices):
        for s in range(size):
            over, along = masks[kind][s % 2]
            pairs.append((d * size + s, (d ^ over) * size + (s ^ along)))
    return lax.ppermute(x, ("dp", "seq"), pairs)


def add(terms):
    return sum(t.astype(F32) for t in terms)


def hold(x, deps):
    return lax.optimization_barrier((x,) + tuple(deps))[0] if deps else x


def launch(deps, *items):
    items = [item for item in items if item.sends()]
    sends = [s for item in items for s in item.sends()]
    if not sends:
        return list(deps)
    held = lax.optimization_barrier(tuple(s[0] for s in sends) + tuple(deps))
    came = [swap(x, kind) for x, (_, kind) in zip(held, sends)]
    left = list(came)
    for item in items:
        count = len(item.sends())
        item.receive(left[:count])
        left = left[count:]
    return came


class Gather:
    def __init__(self, blocks, core):
        self.core = core
        self.next = [(blocks, "xy")]
        self.stage = 0

    def sends(self):
        return self.next

    def receive(self, came):
        if self.stage == 0:
            self.pieces = came
            half = came[0].shape[1] // 2
            part = lax.dynamic_slice_in_dim(came[0], self.core * half, half, axis=1)
            self.next = [(part, "yx"), (came[0], 1)]
        elif self.stage == 1:
            self.pieces = self.pieces + [came[1], came[0]]
            self.next = [(came[0], 1)]
        else:
            self.pieces = self.pieces + came
            self.next = []
        self.stage += 1


class Table:
    def __init__(self, params):
        self.own = jnp.pad(params.T, ((0, 16 - params.shape[1]), (0, 0)))

    def sends(self):
        return [(self.own, kind) for kind in ("xy", "yx", "over")]

    def receive(self, came):
        d = lax.axis_index("dp")
        first = lax.axis_index("seq") % 2 == 0
        a = [self.own, jnp.where(first, came[0], came[1]), jnp.where(first, came[1], came[0]), came[2]]
        a = [jnp.where(d % 2 == 1, a[i ^ 1], a[i]) for i in range(4)]
        a = [jnp.where(d // 2 == 1, a[i ^ 2], a[i]) for i in range(4)]
        self.whole = jnp.concatenate(a, axis=1).astype(F32)


class States:
    def __init__(self, state):
        self.parts = [state]
        self.mask = 1

    def sends(self):
        return [(self.parts[0], self.mask)] if self.mask < lax.axis_size("seq") else []

    def receive(self, came):
        self.parts = self.parts + came
        self.mask *= 2
        if self.sends():
            self.parts = [jnp.concatenate(self.parts, axis=0)]


class Halo:
    def __init__(self, tokens, cotangent):
        span = tokens.shape[2]
        toks, cots = tokens[:, 0], cotangent[:, 0]
        self.next = [(toks[:, span - 2 :], "next"), (jnp.stack([toks[:, :2], cots[:, :2]]), "last")]

    def sends(self):
        return self.next

    def receive(self, came):
        before, after = came
        blank = jnp.zeros(after.shape[:2] + (PAD - 2,) + after.shape[3:], BF)
        before = jnp.stack([before, jnp.zeros_like(before)])
        self.rows = jnp.concatenate([blank, before, after, blank], axis=2)


class Core:
    def __init__(self, keep, send, plain):
        self.keep, self.send, self.plain = keep, send, plain

    def sends(self):
        return [] if self.plain else [(self.send, 1)]

    def receive(self, came):
        self.terms = [self.keep, came[0]]

    def whole(self):
        full = jnp.stack([self.keep, self.send], axis=1).reshape(-1, self.keep.shape[-1]).astype(F32)
        return lax.psum_scatter(full, ("dp", "seq"), scatter_dimension=0, tiled=True)


class Quarter:
    def __init__(self, *cores):
        self.cores = cores
        self.rows = cores[0].keep.shape[1]
        self.plain = cores[0].plain
        self.came = []

    def value(self, p, rows=slice(None)):
        return jnp.concatenate([add([t[p, rows] for t in c.terms]) for c in self.cores], axis=-1)

    def sends(self):
        if self.plain or len(self.came) == 2:
            return []
        if not self.came:
            return [(self.value(slice(2, 4)).astype(BF), "xy")]
        return [((self.value(1) + self.came[0][1].astype(F32)).astype(BF), "yx")]

    def receive(self, came):
        self.came += came

    def final(self, rows):
        return self.value(0, rows) + self.came[0][0, rows].astype(F32) + self.came[1][rows].astype(F32)


class SmallQuarter(Quarter):
    def sends(self):
        if self.plain or self.came:
            return []
        return [(self.value(p).astype(BF), kind) for p, kind in ((2, "xy"), (1, "yx"), (3, "over"))]

    def final(self, rows):
        return self.value(0, rows) + add([t[rows] for t in self.came])


class Finish:
    def __init__(self, *quarters):
        self.quarters = quarters
        self.plain = quarters[0].plain
        self.block = quarters[0].rows // 4
        self.came = []
        if self.plain:
            self.total = jnp.concatenate([c.whole() for q in quarters for c in q.cores], axis=-1)

    def value(self, low, high):
        rows = slice(low * self.block, high * self.block)
        return jnp.concatenate([q.final(rows) for q in self.quarters], axis=-1)

    def sends(self):
        if self.plain or len(self.came) == 2:
            return []
        if not self.came:
            return [(self.value(2, 4).astype(BF), "near")]
        return [((self.value(1, 2) + self.came[0][self.block :].astype(F32)).astype(BF), "far")]

    def receive(self, came):
        self.came += came
        if len(self.came) == 2:
            self.total = self.value(0, 1) + self.came[0][: self.block].astype(F32) + self.came[1].astype(F32)


ANY = pl.BlockSpec(memory_space=pl.ANY)
SMEM = pl.BlockSpec(memory_space=pltpu.SMEM)


def shape(s, dtype):
    return jax.ShapeDtypeStruct(s, dtype)


BATCH = "batch"
LATE = "late"
HELD = "held"
VMEM = pl.BlockSpec(memory_space=pltpu.VMEM)


def call(name, kernel, grid, ins, outs, scratch, mib, deps=(), aliases=None, prefetch=False):
    ins = [(hold(ins[0][0], deps), ins[0][1])] + ins[1:]
    views = [i for i, (_, spec) in enumerate(ins + outs) if spec is BATCH]
    lates = [i for i, (_, spec) in enumerate(ins) if spec is LATE]
    extra = [pltpu.VMEM(ins[i][0].shape, ins[i][0].dtype) for i in lates]
    if lates:
        extra.append(pltpu.SemaphoreType.DMA((len(lates), grid[0])))

    def run(*refs):
        refs = list(refs)
        if lates:
            held, sems = refs[-len(extra) : -1], refs[-1]
            refs = refs[: -len(extra)]
            for k, i in enumerate(lates):
                refs[i] = Late(refs[i], held[k], sems, k)

            @pl.when(pl.program_id(0) == 0)
            def _():
                for b in range(grid[0]):
                    for i in lates:
                        refs[i].copy(b).start()

        for i in views:
            refs[i] = refs[i].at[pl.ds(pl.program_id(0), 1)]
        kernel(*refs)

    specs = {id(BATCH): VMEM, id(LATE): ANY, id(HELD): ANY}
    held = (LATE, HELD)
    operands = [pltpu.with_memory_space_constraint(a, pltpu.HBM) if any(s is h for h in held) else a for a, s in ins]
    grid_spec = pltpu.PrefetchScalarGridSpec(
        num_scalar_prefetch=1 if prefetch else 0,
        grid=grid,
        in_specs=[specs.get(id(s), s) for _, s in ins[1 if prefetch else 0 :]],
        out_specs=[specs.get(id(s), s) for _, s in outs],
        scratch_shapes=list(scratch) + extra,
    )
    return pl.pallas_call(
        run,
        grid_spec=grid_spec,
        out_shape=[a for a, _ in outs],
        input_output_aliases=aliases or {},
        compiler_params=pltpu.CompilerParams(vmem_limit_bytes=mib * 2**20),
        name=name,
    )(*operands)


def body(
    tokens,
    cotangent,
    lengths,
    att_key,
    att_value,
    att_recept,
    att_out,
    ffn_key,
    ffn_value,
    ffn_recept,
    params,
):
    batches, _, span, width = tokens.shape
    seqs = lengths.shape[2]
    ff = ffn_key.shape[1]
    tiles = ff // width
    ranks = lax.axis_size("seq")
    rows = span + 2 * PAD
    d, s = lax.axis_index("dp"), lax.axis_index("seq")
    core = s % 2
    at = lax.iota(jnp.int32, HEAD + batches * seqs)
    info = jnp.pad(lengths.reshape(batches * seqs), (HEAD, 0))
    for i, number in enumerate((s * span, d, s, core)):
        info = jnp.where(at == i, number, info)
    shard = att_key.shape[0]
    group_a = Gather(jnp.stack([att_key, att_value, att_recept, att_out]), core)
    group_b = Gather(jnp.stack([ffn_key[:, j * width : (j + 1) * width] for j in range(tiles)]), core)
    group_c = Gather(jnp.concatenate([ffn_value.reshape(-1, shard, width), ffn_recept[None]], axis=0), core)
    table = Table(params)

    edge = Halo(tokens, cotangent)
    came = launch((), group_a) + launch([info], edge, table)
    halo = edge.rows
    par = table.whole

    ext = (batches, rows, width)
    ext_f, ext_b = shape(ext, F32), shape(ext, BF)
    line_f = shape((batches, width // 128, rows, 128), F32)
    stats_shape = shape((batches, 2, rows, 128), F32)
    ends_shape = shape((batches, 2, 8, width), F32)
    wide_b = shape((batches, rows, ff), BF)
    square = pltpu.VMEM((1, width, width), BF)
    three = pltpu.VMEM((3, width, width), BF)
    square_f = pltpu.VMEM((width, width), F32)
    block_f = pltpu.VMEM((rows, width), F32)
    block_line = pltpu.VMEM((width // 128, rows, 128), F32)
    part = pltpu.VMEM((rows, 128), F32)

    def sems(n):
        return pltpu.SemaphoreType.DMA((n,))

    def refs(group):
        return [(p, ANY) for p in group.pieces]

    info_in = (info, SMEM)

    deps = came
    came = launch(deps, group_a)
    mix_key, mix_value, mix_recept, change_one, tok_ext, cot_ext, stats_one = call(
        "mix",
        functools.partial(mix_kernel, span, seqs),
        (batches,),
        [
            info_in,
            (tokens, pl.BlockSpec((1,) + tokens.shape[1:], lambda i: (i, 0, 0, 0))),
            (cotangent, pl.BlockSpec((1,) + tokens.shape[1:], lambda i: (i, 0, 0, 0))),
            (halo, pl.BlockSpec((2, 1, 2 * PAD, width), lambda i: (0, i, 0, 0))),
            (par, VMEM),
        ],
        [(ext_b, BATCH)] * 6 + [(stats_shape, BATCH)],
        [block_f],
        13,
        deps,
    )
    came = launch(came + [stats_one], group_a, group_b)
    deps, far = came[:1], came[1:]
    state_shape = shape((2 * batches, width), F32)
    exp_key, value, gate_one, ends, state, whole_a = call(
        "project",
        functools.partial(project_kernel, span, seqs),
        (batches,),
        [info_in]
        + [(a, BATCH) for a in (mix_key, mix_value, mix_recept)]
        + [(par, VMEM), (att_key, ANY), (att_value, ANY), (att_recept, ANY)]
        + refs(group_a),
        [(line_f, BATCH)] * 3
        + [(ends_shape, BATCH), (state_shape, VMEM), (pltpu.HBM((3, width, width), BF), ANY)],
        [three, sems(PER + 3)],
        10,
        deps,
    )
    exchange = States(state)
    came = launch([state], exchange)
    far = launch(far + came, group_b)
    came = launch(came, exchange)
    deps = came + far
    far = launch(deps, group_b)
    after = launch(deps, group_c)
    while exchange.sends():
        came = launch(came, exchange)
    states = exchange.parts
    deps = came + far
    came = after
    gated, by_num, by_recept, wkv, middle, ffn_in, ffn_gate_in, change_two, stats_two, whole_out = call(
        "recur",
        functools.partial(recur_kernel, span, seqs, ranks, len(states)),
        (batches,),
        [info_in]
        + [(a, BATCH) for a in (exp_key, value, gate_one)]
        + [(ends, BATCH), (tok_ext, BATCH)]
        + [(par, VMEM), (att_out, ANY)]
        + [(a, VMEM) for a in states]
        + refs(group_a),
        [
            (a, BATCH)
            for a in (ext_b, ext_b, ext_b, ext_b, ext_f, ext_b, ext_b, ext_b, stats_shape)
        ]
        + [(pltpu.HBM((1, width, width), BF), ANY)],
        [square, block_line, block_line, sems(PER + 1)],
        10,
        deps,
    )
    deps = came + [stats_two]
    came = launch(deps, group_c)
    key_buf = pltpu.VMEM((tiles, width, width), BF)
    own_value = ffn_value.reshape(4, shard, width)
    hidden, whole_key = call(
        "hidden",
        hidden_kernel,
        (batches,),
        [info_in, (ffn_in, BATCH), (ffn_key, ANY)] + refs(group_b),
        [(wide_b, BATCH), (pltpu.HBM((tiles, width, width), BF), ANY)],
        [key_buf, sems(tiles + PER + 1)],
        11,
        deps,
    )
    came = launch(came + [hidden], group_c)
    mixed_shape = shape((batches, 1, span, width), BF)
    value_buf = pltpu.VMEM((4 * tiles, shard, width), BF)
    mixed, grad_carried, grad_gate, whole_value, whole_gate = call(
        "gate",
        functools.partial(gate_kernel, span, seqs),
        (batches,),
        [info_in]
        + [(a, BATCH) for a in (hidden, ffn_gate_in, middle, cot_ext)]
        + [(own_value, ANY), (ffn_recept, ANY)]
        + refs(group_c),
        [(mixed_shape, BATCH)]
        + [(ext_b, BATCH)] * 2
        + [(pltpu.HBM(value_buf.shape, BF), ANY), (pltpu.HBM((1, width, width), BF), ANY)],
        [value_buf, square, sems(2 * PER + 2)],
        17,
        came,
    )

    plain = ranks != 8 or (width // (4 * ranks)) % 8 != 0
    nz = 1 if plain else 4
    plan = (nz, plain)

    def core_of(keep, send):
        return Core(*(a.reshape(4, -1, a.shape[-1]) for a in (keep, send)), plain)

    big = pltpu.HBM((4, nz, ff // (8 * nz), width), BF)
    big_kept = shape(big.shape, BF)

    def place_of(other):
        def index(i, info):
            core = (info[3] + other) % 2
            return (i if plain else turn(core, i), 0, 0, 0)

        return pl.BlockSpec((1,) + big.shape[1:], index)

    keep_v, send_v = call(
        "value_grad",
        functools.partial(value_grad_kernel, span, plan),
        (4,),
        [info_in, (hidden, VMEM), (grad_carried, VMEM)],
        [(big_kept, place_of(0)), (big, place_of(1))],
        [square_f],
        10,
        prefetch=True,
    )
    core_value = core_of(keep_v, send_v)
    deps = [keep_v]
    came = launch(deps, core_value)
    wide_half = pltpu.HBM((width // 2, ff + width), BF)
    wide_kept = shape(wide_half.shape, BF)
    keep_k, send_k = call(
        "gate_back",
        functools.partial(gate_back_kernel, span, plan),
        (1,),
        [info_in, (ffn_gate_in, VMEM), (grad_gate, VMEM)],
        [(a, pl.BlockSpec((width // 2, width), lambda i: (0, tiles))) for a in (wide_kept, wide_half)],
        [square_f],
        10,
        deps,
    )
    deps = came + [keep_k]
    sum_value = Quarter(core_value)
    came = launch(deps, sum_value)
    out_tile = pl.BlockSpec((width // 2, width), lambda i: (0, i))
    keep_k, send_k, _, grad_in = call(
        "inner",
        functools.partial(inner_kernel, span, plan),
        (tiles,),
        [
            info_in,
            (keep_k, ANY),
            (send_k, HELD),
            (hidden, VMEM),
            (grad_carried, VMEM),
            (ffn_in, VMEM),
            (whole_key, HELD),
            (whole_value, HELD),
        ],
        [(wide_kept, out_tile), (wide_half, out_tile)] + [(pltpu.VMEM(wide_b.shape, BF), VMEM), (ext_b, VMEM)],
        [
            key_buf,
            value_buf,
            square_f,
            sems(tiles + 1),
        ],
        25,
        deps,
        {1: 0, 2: 1, 3: 2},
    )
    core_key = core_of(keep_k, send_k)
    deps = came + [grad_in]
    came = launch(deps, sum_value, core_key)
    sums_shape = shape((8, width), F32)
    grad_middle, grad_att, grad_recept, grad_num, grad_den, ends_back, state_back, sums = call(
        "attend_back",
        functools.partial(attend_back_kernel, span, seqs),
        (batches,),
        [info_in]
        + [
            (a, LATE if a is cot_ext or a is by_num or a is by_recept or a is wkv else BATCH)
            for a in (
                grad_gate,
                grad_in,
                change_two,
                middle,
                stats_two,
                cot_ext,
                by_num,
                by_recept,
                wkv,
            )
        ]
        + [(par, VMEM), (whole_out, HELD), (whole_gate, HELD)],
        [(a, BATCH) for a in (ext_f, ext_b, ext_b, pltpu.VMEM(line_f.shape, F32), pltpu.VMEM(line_f.shape, F32))]
        + [(ends_shape, BATCH)]
        + [(state_shape, VMEM), (sums_shape, VMEM)],
        [square, square, pltpu.VMEM((4, 8, width), F32), block_f, block_f, part, part, sems(2)],
        18,
        deps,
    )
    exchange = States(state_back)
    sum_key = Quarter(core_key)
    all_value = Finish(sum_value)
    came = launch(came + [state_back], exchange)
    deps = came
    came = launch(came, exchange, sum_key)
    came, far = came[:1], came[1:]
    two = pltpu.HBM((width // 2, 2 * width), BF)
    two_kept = shape(two.shape, BF)
    keep_o, send_o = call(
        "recept",
        functools.partial(recept_kernel, span, plan),
        (2,),
        [info_in] + [(a, VMEM) for a in (gated, grad_att, mix_recept, grad_recept)],
        [(a, pl.BlockSpec((width // 2, width), lambda i: (0, i))) for a in (two_kept, two)],
        [square_f],
        10,
        deps,
    )
    core_out = core_of(keep_o, send_o)
    deps = came + [keep_o]
    came = launch(deps, exchange)
    num_prev, den_prev, back_recept = call(
        "again",
        functools.partial(again_kernel, span, seqs, ranks, len(states)),
        (batches,),
        [info_in]
        + [(a, BATCH) for a in (exp_key, value, ends, grad_recept)]
        + [(par, VMEM), (whole_a, HELD)]
        + [(a, VMEM) for a in states],
        [(line_f, BATCH)] * 2 + [(ext_b, BATCH)],
        [pltpu.VMEM((width, width), BF), sems(1)],
        8,
        deps,
    )
    while exchange.sends():
        came = launch(came, exchange)
    states_back = exchange.parts
    deps = came + far + [back_recept]
    came = launch(deps, all_value, sum_key, core_out)
    grad_key, grad_value, keep_l, send_l, sums_back = call(
        "recur_back",
        functools.partial(recur_back_kernel, span, seqs, ranks, len(states_back), plan),
        (batches,),
        [info_in]
        + [
            (a, LATE if a is mix_key or a is mix_value else BATCH)
            for a in (
                grad_num,
                grad_den,
                exp_key,
                value,
                num_prev,
                den_prev,
                ends_back,
                mix_key,
                mix_value,
            )
        ]
        + [(par, VMEM)]
        + [(a, VMEM) for a in states_back],
        [(ext_b, BATCH)] * 2 + [(two_kept, VMEM), (two, VMEM)] + [(sums_shape, VMEM)],
        [block_line, block_line, square_f, square_f, pltpu.VMEM((2, 8, width), F32)],
        20,
        deps,
    )
    core_last = core_of(keep_l, send_l)
    deps = launch(came + [sums_back], core_last)
    all_key = Finish(sum_key)
    sum_last = Quarter(core_last, core_out)
    came = launch(deps, all_key, sum_last, all_value)
    grad_shape = shape((batches, 1, span, width), F32)
    half_table = shape((width // 2, 128), BF)
    inners, parts, keep_p, send_p = call(
        "first_back",
        functools.partial(first_back_kernel, span, seqs, plan),
        (batches,),
        [info_in]
        + [(a, BATCH) for a in (grad_key, grad_value, back_recept)]
        + [(a, LATE) for a in (tok_ext, stats_one, change_one)]
        + [(sums, VMEM), (sums_back, VMEM), (par, VMEM)]
        + [(whole_a, HELD)],
        [(ext_f, BATCH), (stats_shape, BATCH)] + [(half_table, VMEM)] * 2,
        [
            pltpu.VMEM((2, width, width), BF),
            block_f,
            block_f,
            pltpu.VMEM((7, 8, width), F32),
            pltpu.VMEM((width, 128), F32),
            sems(1),
        ],
        18,
        deps,
    )
    core_table = core_of(keep_p, send_p)
    deps = launch(came + [keep_p], core_table)
    sum_table = SmallQuarter(core_table)
    came = launch(deps, sum_last, sum_table, all_key)
    (tokens_grad,) = call(
        "tokens_grad",
        functools.partial(tokens_grad_kernel, span),
        (batches,),
        [info_in] + [(a, BATCH) for a in (inners, parts, tok_ext, stats_one, grad_middle)],
        [(grad_shape, BATCH)],
        [],
        7,
        deps,
    )
    all_last = Finish(sum_last, sum_table)
    came = launch(came + [tokens_grad], all_last)
    launch(came, all_last)
    key, last = all_key.total, all_last.total
    return (
        mixed,
        tokens_grad,
        last[:, :width],
        last[:, width : 2 * width],
        last[:, 3 * width : 4 * width],
        last[:, 2 * width : 3 * width],
        key[:, :ff],
        all_value.total,
        key[:, ff:],
        last[:, 4 * width : 4 * width + params.shape[1]],
    )


def solution(mesh):
    split = P(("dp", "seq"), None)
    rows = P("dp", None)
    stream = P(None, "dp", "seq", None)
    return jax.shard_map(
        body,
        mesh=mesh,
        in_specs=(stream, stream, P(None, "dp", None)) + (rows,) * 8,
        out_specs=(stream, stream) + (split,) * 8,
        check_vma=False,
    )
```

```python
import functools

import jax
import jax.numpy as jnp
from jax import lax
from jax.experimental import pallas as pl
from jax.experimental.pallas import tpu as pltpu
from jax.sharding import PartitionSpec as P

EPS = 1e-05
BF = jnp.bfloat16
F32 = jnp.float32
PAD = 16
FAR = 1 << 30
PER = 5
HEAD = 4


def bounds_of(info, batch, seqs):
    ends = [jnp.int32(0)]
    for i in range(seqs):
        ends.append(ends[-1] + info[HEAD + batch * seqs + i])
    return ends


def positions(info, row, count):
    return lax.broadcasted_iota(jnp.int32, (count, 128), 0) + (row - PAD + info[0])


def since_start(pos, bounds):
    best = jnp.full(pos.shape, FAR, jnp.int32)
    for b in bounds:
        best = jnp.where(pos >= b, jnp.minimum(best, pos - b), best)
    return best


def until_start(pos, bounds):
    best = jnp.full(pos.shape, FAR, jnp.int32)
    for b in bounds:
        best = jnp.where(pos < b, jnp.minimum(best, b - pos), best)
    return best


def wide(mask, width):
    return jnp.concatenate([mask] * (width // 128), axis=1)


def flag(cond, width):
    return wide(jnp.where(cond, 1.0, 0.0).astype(F32), width)


def keep_flag(pos, bounds, width):
    hit = pos == bounds[0]
    for b in bounds[1:]:
        hit = hit | (pos == b)
    return wide(jnp.where(hit, 0.0, 1.0).astype(F32), width)


def rows_of(count, width):
    return wide(lax.broadcasted_iota(jnp.int32, (count, 128), 0), width)


def down(x, carry):
    rolled = pltpu.roll(x, 1, 0)
    return jnp.where(rows_of(*x.shape) == 0, carry, rolled)


def up(x, carry):
    n = x.shape[0]
    rolled = pltpu.roll(x, n - 1, 0)
    return jnp.where(rows_of(*x.shape) == n - 1, carry, rolled)


def nn(a, b):
    return jnp.dot(a, b, preferred_element_type=F32)


def nt(a, b):
    return lax.dot_general(a, b, (((1,), (1,)), ((), ())), preferred_element_type=F32)


def tn(a, b):
    return lax.dot_general(a, b, (((0,), (0,)), ((), ())), preferred_element_type=F32)


def slabs(span, body, init, reverse=False, unroll=4):
    step = 32
    many = span // step

    def one(i, carry):
        at = many - 1 - i if reverse else i
        return body(pl.multiple_of(PAD + at * step, PAD), step, True, carry)

    first, last = (PAD + span, 0) if reverse else (0, PAD + span)
    carry = body(first, PAD, False, init)
    carry = lax.fori_loop(0, many, one, carry, unroll=unroll)
    return body(last, PAD, False, carry)


def lanes(x):
    return sum(x[:, i : i + 128] for i in range(0, x.shape[1], 128))


def tile(x, i):
    return x[:, i * 128 : (i + 1) * 128]


def row_mean(ref, width):
    total = jnp.sum(ref[...], axis=1, keepdims=True) * (1.0 / width)
    return jnp.broadcast_to(total, ref.shape)


def steps_of(low, high, body, carry, reverse=False, unroll=4):
    def one(i, carry):
        return body(high - 1 - i if reverse else low + i, carry)

    count = high - low
    while count % unroll:
        unroll -= 1
    return lax.fori_loop(0, count, one, carry, unroll=unroll)


def fold(x):
    n, c = x.shape
    return jnp.sum(x.reshape(n // 8, 8, c), axis=0)


def no_start(bounds, low, high):
    hit = jnp.int32(0)
    for b in bounds:
        hit = hit | jnp.where((b > low) & (b <= high), 1, 0)
    return jnp.where(hit == 0, 1.0, 0.0).astype(F32)


def incoming(info, states, batch, bounds, speed, span, ranks, reverse):
    me, base = info[2], info[0]
    num = jnp.zeros(speed.shape, F32)
    den = jnp.zeros(speed.shape, F32)
    for k in range(1, ranks):
        other = me ^ k
        if reverse:
            gap = other - me - 1
            clear = no_start(bounds, base + span + 1, other * span + 1)
        else:
            gap = me - 1 - other
            clear = no_start(bounds, (other + 1) * span - 2, base - 2)
        use = jnp.where(gap >= 0, clear, 0.0).astype(F32)
        weight = jnp.exp(-speed * (jnp.maximum(gap, 0) * span).astype(F32)) * use
        per = sum(r.shape[0] for r in states) // ranks
        many = states[0].shape[0] // per
        at = (k % many) * per + 2 * batch
        num += weight * states[k // many][pl.ds(at, 1), :]
        den += weight * states[k // many][pl.ds(at + 1, 1), :]
    return num, den


def start_all(copies):
    for c in copies:
        c.start()


def wait_all(copies):
    for c in copies:
        c.wait()


def copies_of(info, owns, pieces, blocks, target, sems, at=0):
    d, c = info[1], info[3]
    shard = owns[0].shape[0]
    half = shard // 2
    out = []
    for k, own in enumerate(owns):
        out.append(pltpu.make_async_copy(own, target.at[k, pl.ds(pl.multiple_of(d * shard, 16), shard)], sems.at[at]))
        at += 1
    places = ((d ^ (1 + c)) * shard, (d ^ (2 - c)) * shard, (d ^ 3) * shard + c * half, (d ^ 3) * shard + (1 - c) * half)
    for row, ref in zip(places, pieces):
        source = ref.at[blocks]
        place = target.at[:, pl.ds(pl.multiple_of(row, 16), source.shape[1])]
        out.append(pltpu.make_async_copy(source, place, sems.at[at]))
        at += 1
    return out


def value_copies(info, own, pieces, target, sems, at=0):
    d, c = info[1], info[3]
    half = target.shape[1] // 2
    out = [pltpu.make_async_copy(own, target.at[pl.ds(4 * d, 4)], sems.at[at])]
    places = ((d ^ (1 + c), 0), (d ^ (2 - c), 0), (d ^ 3, c * half), (d ^ 3, (1 - c) * half))
    for (block, row), ref in zip(places, pieces):
        at += 1
        place = target.at[pl.ds(4 * block, 4), pl.ds(pl.multiple_of(row, 16), ref.shape[1])]
        out.append(pltpu.make_async_copy(ref.at[pl.ds(0, 4)], place, sems.at[at]))
    return out


def place(info, plain):
    if plain:
        return 0, 0, 0
    return info[1], info[2] // 2, info[3]


def turn(core, i):
    return core * i + (1 - core) * (((i & 1) << 1) | (i >> 1))


def scatter_rows(info, src, keep, send, plan, write):
    nz, plain = plan
    d, z, c = place(info, plain)
    block = src.shape[0] // (8 * nz)
    per = 4 * nz * block // 16
    groups = block // 8
    for ref, core in ((keep, c), (send, 1 - c)):
        for slab in range(per):
            parts = []
            for g in (2 * slab, 2 * slab + 1):
                i = g % groups
                q = (g // groups) % nz
                p = g // (groups * nz)
                if not plain:
                    p, q = turn(core, p), turn(core, q)
                row = ((d ^ p) * nz + (z ^ q)) * (2 * block) + core * block + i * 8
                parts.append(src[pl.ds(pl.multiple_of(row, 8), 8), :])
            write(ref, slab * 16, jnp.concatenate(parts, axis=0).astype(BF))


def keep_whole(batch, buffer, target, sem):
    def copy():
        return pltpu.make_async_copy(buffer, target, sem)

    pl.when(batch == 0)(lambda: copy().start())
    pl.when(batch == pl.num_programs(0) - 1)(lambda: copy().wait())


class Late:
    def __init__(self, source, buffer, sems, index):
        self.source, self.buffer, self.sems, self.index = source, buffer, sems, index
        self.shape = (1,) + tuple(buffer.shape[1:])

    def copy(self, b):
        return pltpu.make_async_copy(self.source.at[b], self.buffer.at[b], self.sems.at[self.index, b])

    def ready(self):
        b = pl.program_id(0)
        self.copy(b).wait()
        return self.buffer.at[pl.ds(b, 1)]


def mix_kernel(
    span, seqs, info, tokens, cotangent, halo, par, mix_key, mix_value, mix_recept, change, tok_ext, cot_ext, stats, held
):
    batch = pl.program_id(0)
    bounds = bounds_of(info, batch, seqs)
    gain, bias = par[0:1, :], par[1:2, :]
    mixes = (par[2:3, :], par[3:4, :], par[4:5, :])
    width = tokens.shape[3]
    mean, scale = stats.at[0, 0], stats.at[0, 1]

    def load(row, n, owned, carry):
        at = pl.ds(row, n)
        if owned:
            x, g = tokens[0, 0, pl.ds(row - PAD, n), :], cotangent[0, 0, pl.ds(row - PAD, n), :]
        else:
            low = 0 if row == 0 else PAD
            x, g = halo[0, 0, low : low + PAD, :], halo[1, 0, low : low + PAD, :]
        tok_ext[0, at, :] = x
        cot_ext[0, at, :] = g
        x = x.astype(F32)
        held[at, :] = x
        mean[at, :] = lanes(x)
        return carry

    slabs(span, load, 0)
    mean[...] = row_mean(mean, width)

    def spread(row, n, owned, carry):
        at = pl.ds(row, n)
        x = held[at, :] - wide(mean[at, :], width)
        scale[at, :] = lanes(x * x)
        return carry

    slabs(span, spread, 0)
    scale[...] = lax.rsqrt(row_mean(scale, width) + EPS)

    def body(row, n, owned, carry):
        at = pl.ds(row, n)
        normed = (held[at, :] - wide(mean[at, :], width)) * wide(scale[at, :], width)
        first = normed * gain + bias
        keep = keep_flag(positions(info, row, n), bounds, width)
        shifted = down(first, carry) * keep
        diff = first - shifted
        for mu, ref in zip(mixes, (mix_key, mix_value, mix_recept)):
            ref[0, at, :] = (shifted + diff * mu).astype(BF)
        change[0, at, :] = diff.astype(BF)
        return first[n - 1 : n]

    slabs(span, body, jnp.zeros((1, width), F32))


class Chunks:
    def __init__(self, info, bounds, rows, speed):
        self.size = rows // 8
        self.bounds = bounds
        self.base = info[0] - PAD
        self.row8 = lax.broadcasted_iota(jnp.int32, (8, 128), 0)
        self.start = self.row8 * self.size + self.base
        self.speed = speed
        self.tiles = speed.shape[1] // 128
        self.rate = self.split(jnp.exp(-speed))

    def split(self, row):
        return [jnp.broadcast_to(tile(row, i), (8, 128)) for i in range(self.tiles)]

    def at(self, j):
        return pl.ds(j, 8, stride=self.size)

    def keep(self, j, ahead=0):
        pos = self.start + (j + ahead)
        hit = pos == self.bounds[0]
        for b in self.bounds[1:]:
            hit = hit | (pos == b)
        return jnp.where(hit, 0.0, 1.0).astype(F32)

    def decay(self, low, high, count):
        clear = no_start(self.bounds, self.base + low, self.base + high)
        return jnp.exp(-self.speed * float(count)) * clear


def join(tiles):
    return jnp.concatenate(tiles, axis=1)


def write_state(state, batch, num, den):
    for i in range(state.shape[0] // 2):

        @pl.when(batch == i)
        def _():
            state[2 * i : 2 * i + 1, :] = num
            state[2 * i + 1 : 2 * i + 2, :] = den


def project_kernel(
    span, seqs, info, mix_key, mix_value, mix_recept, par, own_key, own_value, own_recept, *refs
):
    pieces = refs[0:4]
    exp_key, value, gate, ends, state, kept, weights, sems = refs[4:]
    batch = pl.program_id(0)
    bounds = bounds_of(info, batch, seqs)
    rows, width = mix_key.shape[1:]

    def copies():
        return copies_of(info, (own_key, own_value, own_recept), pieces, pl.ds(0, 3), weights, sems)

    @pl.when(batch == 0)
    def _():
        start_all(copies())
        wait_all(copies())

    acts = (jnp.exp, lambda x: x, jax.nn.sigmoid)
    for k, (left, ref, act) in enumerate(zip((mix_key, mix_value, mix_recept), (exp_key, value, gate), acts)):
        part = act(nn(left[0], weights[k]))
        for i in range(width // 128):
            ref[0, i] = tile(part, i)

    speed = jnp.exp(par[5:6, :])
    chunks = Chunks(info, bounds, rows, speed)
    size = chunks.size

    def step(j, carry, cut=False):
        nums, dens = carry
        at = chunks.at(j)
        keep = chunks.keep(j)
        num_out, den_out = [], []
        for i in range(chunks.tiles):
            ek = exp_key[0, i, at, :]
            if cut:
                ek = jnp.where(chunks.row8 == 0, 0.0, ek)
            factor = chunks.rate[i] * keep
            num_out.append(factor * nums[i] + ek * value[0, i, at, :])
            den_out.append(factor * dens[i] + ek)
        return tuple(num_out), tuple(den_out)

    zero = tuple(jnp.zeros((8, 128), F32) for _ in range(chunks.tiles))
    last = PAD + span - 2 - 7 * size
    carry = (zero, zero)
    for j in range(PAD - 1):
        carry = step(j, carry, cut=True)
    carry = steps_of(PAD - 1, last + 1, step, carry)
    inside = [join(c)[7:8] for c in carry]
    carry = steps_of(last + 1, size, step, carry, unroll=size)
    whole_ends = [join(c) for c in carry]
    out = []
    for k in range(2):
        ends[0, k] = whole_ends[k]
        total = whole_ends[k][0:1]
        for s in range(1, 7):
            total = whole_ends[k][s : s + 1] + chunks.decay(s * size - 1, (s + 1) * size - 1, size) * total
        out.append(inside[k] + chunks.decay(7 * size - 1, 7 * size + last, last + 1) * total)
    write_state(state, batch, *out)
    keep_whole(batch, weights, kept, sems.at[PER + 2])


def forward_scan(info, states, batch, chunks, exp_key, value, ends, span, ranks, emit):
    size, width = chunks.size, chunks.speed.shape[1]
    entering = incoming(info, states, batch, chunks.bounds, chunks.speed, span, ranks, False)
    begin = []
    for k in range(2):
        lines = [jnp.zeros((1, width), F32)]
        lines.append(ends[0, k, 0:1, :] + chunks.decay(PAD - 2, size - 1, size - PAD + 1) * entering[k])
        for s in range(1, 7):
            lines.append(ends[0, k, s : s + 1, :] + chunks.decay(s * size - 1, (s + 1) * size - 1, size) * lines[-1])
        begin.append(jnp.concatenate(lines, axis=0))
    carry = tuple(tuple(tile(b, i) for i in range(chunks.tiles)) for b in begin)

    def step(j, carry, insert=None):
        nums, dens = carry
        at = chunks.at(j)
        keep = chunks.keep(j)
        num_out, den_out = [], []
        for i in range(chunks.tiles):
            ek, v = exp_key[0, i, at, :], value[0, i, at, :]
            before_num = keep * nums[i]
            before_den = keep * dens[i]
            x, y = ek * v, ek
            emit(at, i, before_num, before_den, ek, x)
            if insert is not None:
                x = jnp.where(chunks.row8 == 0, insert[0][i], x)
                y = jnp.where(chunks.row8 == 0, insert[1][i], y)
            num_out.append(chunks.rate[i] * before_num + x)
            den_out.append(chunks.rate[i] * before_den + y)
        return tuple(num_out), tuple(den_out)

    none = [[0.0] * chunks.tiles] * 2
    for j in range(PAD - 2):
        carry = step(j, carry, none)
    carry = step(PAD - 2, carry, [chunks.split(e) for e in entering])
    steps_of(PAD - 1, size, step, carry)


def recur_kernel(span, seqs, ranks, parts, info, exp_key, value, gate, ends, tokens, par, own_out, *refs):
    states, refs = refs[:parts], refs[parts:]
    pieces = refs[0:4]
    (
        gated,
        by_num,
        by_recept,
        wkv,
        middle,
        ffn_in,
        ffn_gate_in,
        change,
        stats,
        kept,
        wo,
        line_wkv,
        line_inverse,
        sems,
    ) = refs[4:]
    batch = pl.program_id(0)
    bounds = bounds_of(info, batch, seqs)
    rows, width = tokens.shape[1:]

    def copies():
        return copies_of(info, (own_out,), pieces, pl.ds(3, 1), wo, sems)

    @pl.when(batch == 0)
    def _():
        start_all(copies())

    chunks = Chunks(info, bounds, rows, jnp.exp(par[5:6, :]))
    boost = chunks.split(jnp.exp(par[6:7, :]))

    def emit(at, i, before_num, before_den, ek, x):
        inverse = 1.0 / (before_den + boost[i] * ek)
        line_inverse[i, at, :] = inverse
        line_wkv[i, at, :] = (before_num + boost[i] * x) * inverse

    forward_scan(info, states, batch, chunks, exp_key, value, ends, span, ranks, emit)

    def pack(row, n, owned, carry):
        at = pl.ds(row, n)
        out = ([], [], [], [])
        for i in range(chunks.tiles):
            w, sig = line_wkv[i, at, :], gate[0, i, at, :]
            g = w * sig
            out[0].append(g)
            out[1].append(sig * line_inverse[i, at, :])
            out[2].append(g * (1.0 - sig))
            out[3].append(w)
        for ref, tiles in zip((gated, by_num, by_recept, wkv), out):
            ref[0, at, :] = join(tiles).astype(BF)
        return carry

    slabs(span, pack, 0)

    @pl.when(batch == 0)
    def _():
        wait_all(copies())

    middle[0] = nn(gated[0], wo[0])
    gain, bias = par[7:8, :], par[8:9, :]
    mean, scale = stats.at[0, 0], stats.at[0, 1]

    def residual(row, n, owned, carry):
        at = pl.ds(row, n)
        mid = middle[0, at, :] + tokens[0, at, :].astype(F32)
        middle[0, at, :] = mid
        mean[at, :] = lanes(mid)
        return carry

    slabs(span, residual, 0)
    mean[...] = row_mean(mean, width)

    def spread(row, n, owned, carry):
        at = pl.ds(row, n)
        x = middle[0, at, :] - wide(mean[at, :], width)
        scale[at, :] = lanes(x * x)
        return carry

    slabs(span, spread, 0)
    scale[...] = lax.rsqrt(row_mean(scale, width) + EPS)

    def body(row, n, owned, carry):
        at = pl.ds(row, n)
        normed = (middle[0, at, :] - wide(mean[at, :], width)) * wide(scale[at, :], width)
        second = normed * gain + bias
        keep = keep_flag(positions(info, row, n), bounds, width)
        shifted = down(second, carry) * keep
        diff = second - shifted
        ffn_in[0, at, :] = (shifted + diff * par[9:10, :]).astype(BF)
        ffn_gate_in[0, at, :] = (shifted + diff * par[10:11, :]).astype(BF)
        change[0, at, :] = diff.astype(BF)
        return second[n - 1 : n]

    slabs(span, body, jnp.zeros((1, width), F32))
    keep_whole(batch, wo, kept, sems.at[PER])


def hidden_kernel(info, ffn_in, own_key, *refs):
    pieces = refs[0:4]
    hidden, kept, wk, sems = refs[4:]
    width = ffn_in.shape[2]
    tiles = wk.shape[0]

    def copies():
        owns = [own_key.at[:, pl.ds(j * width, width)] for j in range(tiles)]
        return copies_of(info, owns, pieces, pl.ds(0, tiles), wk, sems)

    @pl.when(pl.program_id(0) == 0)
    def _():
        start_all(copies())
        wait_all(copies())

    for j in range(tiles):
        relu = jnp.maximum(nn(ffn_in[0], wk[j]), 0.0)
        hidden[0, :, pl.ds(j * width, width)] = (relu * relu).astype(BF)
    keep_whole(pl.program_id(0), wk, kept, sems.at[tiles + PER])


def gate_kernel(
    span, seqs, info, hidden, ffn_gate_in, middle, cotangent, own_value, own_recept, *refs
):
    pieces = refs[0:4]
    mixed, grad_carried, grad_gate, kept, kept_gate, wv, wr, sems = refs[4:]
    batch = pl.program_id(0)
    bounds = bounds_of(info, batch, seqs)
    rows, width = middle.shape[1:]

    def copies():
        return (
            copies_of(info, (own_recept,), pieces, pl.ds(4, 1), wr, sems),
            value_copies(info, own_value, pieces, wv, sems, PER),
        )

    @pl.when(batch == 0)
    def _():
        for c in copies():
            start_all(c)
        wait_all(copies()[0])
    keep_whole(batch, wv, kept, sems.at[2 * PER])
    keep_whole(batch, wr, kept_gate, sems.at[2 * PER + 1])


    @pl.when(batch == 0)
    def _():
        wait_all(copies()[1])

    flat = wv[...].reshape(wv.shape[0] * wv.shape[1], width)
    total = bounds[-1]
    step = rows // 2
    for low in range(0, rows, step):
        gate = nn(ffn_gate_in[0, low : low + step, :], wr[0])
        carried = nn(hidden[0, low : low + step, :], flat)
        for i in range(0, step, PAD):
            row = low + i
            at = pl.ds(row, PAD)
            sig = jax.nn.sigmoid(gate[i : i + PAD])
            car = carried[i : i + PAD]
            live = flag(positions(info, row, PAD) < total, width)
            grad = cotangent[0, at, :].astype(F32) * live
            if PAD <= row < PAD + span:
                mixed[0, 0, row - PAD : row, :] = (middle[0, at, :] + sig * car).astype(BF)
            part = grad * sig
            grad_carried[0, at, :] = part.astype(BF)
            grad_gate[0, at, :] = (part * car * (1.0 - sig)).astype(BF)


def over_own(left, right, span):
    own = pl.ds(PAD, span)
    both = [jnp.concatenate([f[b, own] for b in range(f.shape[0])], axis=0) for f in (left, right)]
    return tn(*both)


def store_sixteen(ref, row, value):
    ref[row : row + 16, :] = value


def value_grad_kernel(span, plan, info, hidden, grad_carried, keep, send, total):
    nz, plain = plan
    d, z, c = place(info, plain)
    width = total.shape[1]
    column = pl.ds(pl.multiple_of((pl.program_id(0) ^ d) * width, width), width)
    block = keep.shape[2]
    total[...] = over_own(hidden.at[:, :, column], grad_carried, span)
    for q in range(nz):
        for ref, core in ((keep, c), (send, 1 - c)):
            row = pl.multiple_of(((z ^ (q if plain else turn(core, q))) * 2 + core) * block, 8)
            ref[0, q] = total[pl.ds(row, block), :].astype(BF)


def gate_back_kernel(span, plan, info, ffn_gate_in, grad_gate, keep, send, total):
    total[...] = over_own(ffn_gate_in, grad_gate, span)
    scatter_rows(info, total, keep, send, plan, store_sixteen)


def inner_kernel(
    span, plan, info, _, __, hidden, grad_carried, ffn_in, key, whole_value, keep, send, grad_inner, grad_in, weights, total, sems
):
    step = pl.program_id(0)
    batches, _, width = grad_in.shape
    tiles = weights.shape[0] // 4
    last = step == tiles - 1

    def value_copy(j):
        block = pl.ds(4 * j, 4)
        return pltpu.make_async_copy(whole_value.at[block], weights.at[block], sems.at[j])

    def key_copy():
        return pltpu.make_async_copy(key, weights, sems.at[tiles])

    @pl.when(step == 0)
    def _():
        for j in range(tiles):
            value_copy(j).start()

    here = pl.multiple_of(step * width, width)
    for j in range(tiles):
        pl.when(step == j)(lambda: value_copy(j).wait())
    value = weights[pl.ds(4 * step, 4)].reshape(4 * weights.shape[1], width)
    for b in range(batches):
        back = nt(grad_carried[b], value)
        at = pl.ds(here, width)
        square = hidden[b, :, at].astype(F32)
        relu = square * lax.rsqrt(jnp.maximum(square, 1e-30))
        grad_inner[b, :, at] = (back * (2.0 * relu)).astype(BF)
    pl.when(last)(lambda: key_copy().start())
    total[...] = over_own(ffn_in, grad_inner.at[:, :, pl.ds(here, width)], span)
    scatter_rows(info, total, keep, send, plan, store_sixteen)

    @pl.when(last)
    def _():
        key_copy().wait()
        blocks = [weights[4 * j : 4 * j + 4].reshape(4 * weights.shape[1], width) for j in range(tiles)]
        right = jnp.concatenate(blocks, axis=1)
        for b in range(batches):
            grad_in[b] = nt(grad_inner[b], right).astype(BF)


def attend_back_kernel(
    span,
    seqs,
    info,
    grad_gate,
    grad_in,
    change,
    middle,
    stats,
    cotangent,
    by_num,
    by_recept,
    wkv,
    par,
    wo,
    wr,
    *refs,
):
    (grad_middle, grad_att, grad_recept, grad_num, grad_den, ends, state, sums, acc, held, back_gate, part_a, part_b) = refs
    batch = pl.program_id(0)
    bounds = bounds_of(info, batch, seqs)
    rows, width = middle.shape[1:]

    @pl.when(batch == 0)
    def _():
        acc[...] = jnp.zeros_like(acc)

    gain = par[7:8, :]
    mu, nu = par[9:10, :], par[10:11, :]
    total = bounds[-1]

    back_gate[...] = nt(grad_gate[0], wr[0])
    mean, scale = stats.at[0, 0], stats.at[0, 1]

    def normed_of(at):
        return (middle[0, at, :] - wide(mean[at, :], width)) * wide(scale[at, :], width)

    def gather(row, n, owned, carry):
        at = pl.ds(row, n)
        a, b = grad_in[0, at, :].astype(F32), back_gate[at, :]
        keep = keep_flag(positions(info, row, n), bounds, width)
        normed = normed_of(at)
        direct = a * mu + b * nu
        moved = (a + b - direct) * keep
        second = direct + up(moved, carry)
        if owned:
            diff = change[0, at, :].astype(F32)
            acc[0] += fold(second * normed)
            acc[1] += fold(second)
            acc[2] += fold(a * diff)
            acc[3] += fold(b * diff)
        inner = second * gain
        held[at, :] = inner
        part_a[at, :] = lanes(inner)
        part_b[at, :] = lanes(inner * normed)
        return moved[0:1]

    slabs(span, gather, jnp.zeros((1, width), F32), reverse=True)
    part_a[...] = row_mean(part_a, width)
    part_b[...] = row_mean(part_b, width)


    def apply(row, n, owned, carry):
        at = pl.ds(row, n)
        back = wide(scale[at, :], width) * (
            held[at, :] - wide(part_a[at, :], width) - normed_of(at) * wide(part_b[at, :], width)
        )
        live = flag(positions(info, row, n) < total, width)
        grad = cotangent[0, at, :].astype(F32) * live + back
        grad_middle[0, at, :] = grad
        grad_att[0, at, :] = grad.astype(BF)
        return carry

    cotangent = cotangent.ready()
    slabs(span, apply, 0)

    held[...] = nt(grad_att[0], wo[0])
    speed = jnp.exp(par[5:6, :])
    chunks = Chunks(info, bounds, rows, speed)
    size = chunks.size


    def point(row, n, owned, carry):
        at = pl.ds(row, n)
        back = held[at, :]
        num = back * by_num[0, at, :].astype(F32)
        den = num * wkv[0, at, :].astype(F32)
        for i in range(chunks.tiles):
            grad_num[0, i, at, :] = tile(num, i)
            grad_den[0, i, at, :] = -tile(den, i)
        grad_recept[0, at, :] = (back * by_recept[0, at, :].astype(F32)).astype(BF)
        return carry

    by_num, by_recept, wkv = by_num.ready(), by_recept.ready(), wkv.ready()
    slabs(span, point, 0)

    def step(j, carry, cut=False):
        nums, dens = carry
        at = chunks.at(j)
        keep = chunks.keep(j, 1)
        num_out, den_out = [], []
        for i in range(chunks.tiles):
            gn, gd = grad_num[0, i, at, :], grad_den[0, i, at, :]
            if cut:
                gn, gd = jnp.where(chunks.row8 == 7, 0.0, gn), jnp.where(chunks.row8 == 7, 0.0, gd)
            factor = chunks.rate[i] * keep
            num_out.append(factor * nums[i] + gn)
            den_out.append(factor * dens[i] + gd)
        return tuple(num_out), tuple(den_out)

    zero = tuple(jnp.zeros((8, 128), F32) for _ in range(chunks.tiles))
    after = PAD + span + 1 - 7 * size
    carry = (zero, zero)
    for j in reversed(range(after, size)):
        carry = step(j, carry, cut=True)
    carry = steps_of(PAD + 1, after, step, carry, reverse=True)
    inside = [join(c)[0:1] for c in carry]
    carry = steps_of(0, PAD + 1, step, carry, reverse=True, unroll=size)
    whole_ends = [join(c) for c in carry]
    out = []
    for k in range(2):
        ends[0, k] = whole_ends[k]
        line = whole_ends[k][7:8]
        for s in range(6, 0, -1):
            line = whole_ends[k][s : s + 1] + chunks.decay(s * size, (s + 1) * size, size) * line
        out.append(inside[k] + chunks.decay(PAD + 1, size, size - PAD - 1) * line)
    write_state(state, batch, *out)

    @pl.when(batch == pl.num_programs(0) - 1)
    def _():
        sums[...] = jnp.zeros_like(sums)
        for i in range(4):
            sums[i : i + 1, :] = jnp.sum(acc[i], axis=0, keepdims=True)


def recept_kernel(span, plan, info, gated, grad_att, mix_recept, grad_recept, keep, send, total):
    def grad(left, right):
        total[...] = over_own(left, right, span)
        scatter_rows(info, total, keep, send, plan, store_sixteen)

    pl.when(pl.program_id(0) == 0)(lambda: grad(gated, grad_att))
    pl.when(pl.program_id(0) == 1)(lambda: grad(mix_recept, grad_recept))


def again_kernel(span, seqs, ranks, parts, info, exp_key, value, ends, grad_recept, par, whole_a, *refs):
    states, (num_prev, den_prev, back_recept, wr, sems) = refs[:parts], refs[parts:]
    batch = pl.program_id(0)
    bounds = bounds_of(info, batch, seqs)
    chunks = Chunks(info, bounds, grad_recept.shape[1], jnp.exp(par[5:6, :]))

    def copy():
        return pltpu.make_async_copy(whole_a.at[2], wr, sems.at[0])

    pl.when(batch == 0)(lambda: copy().start())

    def emit(at, i, before_num, before_den, ek, x):
        num_prev[0, i, at, :] = before_num
        den_prev[0, i, at, :] = before_den

    forward_scan(info, states, batch, chunks, exp_key, value, ends, span, ranks, emit)
    pl.when(batch == 0)(lambda: copy().wait())
    back_recept[0] = nt(grad_recept[0], wr[...]).astype(BF)


def recur_back_kernel(
    span,
    seqs,
    ranks,
    parts,
    plan,
    info,
    grad_num,
    grad_den,
    exp_key,
    value,
    num_prev,
    den_prev,
    ends,
    mix_key,
    mix_value,
    par,
    *refs,
):
    states, refs = refs[:parts], refs[parts:]
    grad_key, grad_value, keep, send, sums, line_key, line_value, total, acc = refs
    batch = pl.program_id(0)
    bounds = bounds_of(info, batch, seqs)
    rows, width = mix_key.shape[1:]

    @pl.when(batch == 0)
    def _():
        acc[...] = jnp.zeros_like(acc)

    speed = jnp.exp(par[5:6, :])
    chunks = Chunks(info, bounds, rows, speed)
    size = chunks.size
    boost = chunks.split(jnp.exp(par[6:7, :]))
    entering = incoming(info, states, batch, bounds, speed, span, ranks, True)
    after = PAD + span + 1 - 7 * size
    begin = []
    for k in range(2):
        lines = [jnp.zeros((1, width), F32)]
        lines.append(ends[0, k, 7:8, :] + chunks.decay(7 * size, 7 * size + after, after) * entering[k])
        for s in range(6, 0, -1):
            lines.append(ends[0, k, s : s + 1, :] + chunks.decay(s * size, (s + 1) * size, size) * lines[-1])
        begin.append(jnp.concatenate(lines[::-1], axis=0))
    zero = tuple(jnp.zeros((8, 128), F32) for _ in range(chunks.tiles))
    carry = tuple(tuple(tile(b, i) for i in range(chunks.tiles)) for b in begin) + (zero, zero)

    def step(j, carry, insert=None, mask=None):
        nums, dens, bonuses, decays = carry
        at = chunks.at(j)
        keep_next = chunks.keep(j, 1)
        outs = ([], [], [], [])
        for i in range(chunks.tiles):
            gn, ek, v = grad_num[0, i, at, :], exp_key[0, i, at, :], value[0, i, at, :]
            gd = grad_den[0, i, at, :]
            after_num = keep_next * nums[i]
            after_den = keep_next * dens[i]
            bek = boost[i] * ek
            bonus = bek * (v * gn + gd)
            line_key[i, at, :] = bonus + ek * (v * after_num + after_den)
            line_value[i, at, :] = bek * gn + ek * after_num
            decay = num_prev[0, i, at, :] * after_num + den_prev[0, i, at, :] * after_den
            if mask is not None:
                bonus = jnp.where(mask, bonus, 0.0)
                decay = jnp.where(mask, decay, 0.0)
            if insert is not None:
                gn = jnp.where(chunks.row8 == 7, insert[0][i], gn)
                gd = jnp.where(chunks.row8 == 7, insert[1][i], gd)
            outs[0].append(chunks.rate[i] * after_num + gn)
            outs[1].append(chunks.rate[i] * after_den + gd)
            outs[2].append(bonuses[i] + bonus)
            outs[3].append(decays[i] + decay)
        return tuple(tuple(o) for o in outs)

    none = [[0.0] * chunks.tiles] * 2
    upper = chunks.row8 < 7
    for j in reversed(range(after + 1, size)):
        carry = step(j, carry, none, upper)
    carry = step(after, carry, [chunks.split(e) for e in entering], upper)
    edge = PAD + span - 7 * size
    for j in reversed(range(edge, after)):
        carry = step(j, carry, None, upper)
    carry = steps_of(PAD, edge, step, carry, reverse=True)
    lower = chunks.row8 > 0
    carry = steps_of(0, PAD, lambda j, c: step(j, c, None, lower), carry, reverse=True)
    acc[0] += join(carry[2])
    acc[1] += join(carry[3])

    def pack(row, n, owned, carry):
        at = pl.ds(row, n)
        grad_key[batch, at, :] = join([line_key[i, at, :] for i in range(chunks.tiles)]).astype(BF)
        grad_value[batch, at, :] = join([line_value[i, at, :] for i in range(chunks.tiles)]).astype(BF)
        return carry

    slabs(span, pack, 0)
    mix_key.ready(), mix_value.ready()

    @pl.when(batch == pl.num_programs(0) - 1)
    def _():
        sums[...] = jnp.zeros_like(sums)
        for i in range(2):
            sums[i : i + 1, :] = jnp.sum(acc[i], axis=0, keepdims=True)
        for left, right, low in ((mix_key, grad_key, 0), (mix_value, grad_value, width)):
            total[...] = over_own(left.buffer, right, span)

            def write(ref, row, value):
                ref[row : row + 16, low : low + width] = value

            scatter_rows(info, total, keep, send, plan, write)


def first_back_kernel(
    span,
    seqs,
    plan,
    info,
    grad_key,
    grad_value,
    back_recept,
    tokens,
    stats,
    change,
    sums,
    sums_back,
    par,
    whole_a,
    *refs,
):
    inners, part_ref, keep, send, weights, back_key, back_value, acc, turned, sems = refs
    part_a, part_b = part_ref.at[0, 0], part_ref.at[0, 1]
    batch = pl.program_id(0)
    bounds = bounds_of(info, batch, seqs)
    width = tokens.shape[2]

    def copies():
        return [pltpu.make_async_copy(whole_a.at[pl.ds(0, 2)], weights, sems.at[0])]

    @pl.when(batch == 0)
    def _():
        start_all(copies())
        acc[...] = jnp.zeros_like(acc)
        wait_all(copies())

    back_key[...] = nt(grad_key[0], weights[0])
    back_value[...] = nt(grad_value[0], weights[1])
    gain = par[0:1, :]
    mixes = (par[2:3, :], par[3:4, :], par[4:5, :])
    tokens, stats, change = tokens.ready(), stats.ready(), change.ready()
    mean, scale = stats.at[0, 0], stats.at[0, 1]

    def normed_of(at):
        return (tokens[0, at, :].astype(F32) - wide(mean[at, :], width)) * wide(scale[at, :], width)

    def gather(row, n, owned, carry):
        at = pl.ds(row, n)
        parts = (back_key[at, :], back_value[at, :], back_recept[0, at, :].astype(F32))
        keep = keep_flag(positions(info, row, n), bounds, width)
        direct = sum(g * mu for g, mu in zip(parts, mixes))
        moved = (parts[0] + parts[1] + parts[2] - direct) * keep
        if owned:
            normed = normed_of(at)
            first = direct + up(moved, carry)
            diff = change[0, at, :].astype(F32)
            acc[2] += fold(first * normed)
            acc[3] += fold(first)
            for i in range(3):
                acc[4 + i] += fold(parts[i] * diff)
            inner = first * gain
            inners[0, at, :] = inner
            part_a[at, :] = lanes(inner)
            part_b[at, :] = lanes(inner * normed)
        return moved[0:1]

    slabs(span, gather, jnp.zeros((1, width), F32), reverse=True)
    part_a[...] = row_mean(part_a, width)
    part_b[...] = row_mean(part_b, width)

    @pl.when(batch == pl.num_programs(0) - 1)
    def _():
        def final(i):
            return jnp.sum(acc[i], axis=0, keepdims=True)

        speed = jnp.exp(par[5:6, :])
        decay = sums_back[1:2, :] * jnp.exp(-speed) * -speed
        columns = [final(i) for i in (2, 3, 4, 5, 6)] + [decay, sums_back[0:1, :]]
        columns += [sums[i : i + 1, :] for i in range(4)]
        stacked = jnp.concatenate(columns + [jnp.zeros((128 - len(columns), width), F32)], axis=0)
        turned[...] = stacked.T
        scatter_rows(info, turned, keep, send, plan, store_sixteen)


def tokens_grad_kernel(span, info, inners, parts, tokens, stats, grad_middle, tokens_grad):
    width = inners.shape[2]
    mean, scale = stats.at[0, 0], stats.at[0, 1]
    part_a, part_b = parts.at[0, 0], parts.at[0, 1]

    def apply(row, n, owned, carry):
        if owned:
            at = pl.ds(row, n)
            rate = wide(scale[at, :], width)
            normed = (tokens[0, at, :].astype(F32) - wide(mean[at, :], width)) * rate
            back = rate * (inners[0, at, :] - wide(part_a[at, :], width) - normed * wide(part_b[at, :], width))
            tokens_grad[0, 0, pl.ds(row - PAD, n), :] = grad_middle[0, at, :] + back
        return carry

    slabs(span, apply, 0)


def swap(x, kind):
    devices, size = lax.axis_size("dp"), lax.axis_size("seq")
    if kind == "next":
        return lax.ppermute(x, "seq", [(i, i + 1) for i in range(size - 1)])
    if kind == "last":
        return lax.ppermute(x, "seq", [(i + 1, i) for i in range(size - 1)])
    if isinstance(kind, int):
        return lax.ppermute(x, "seq", [(i, i ^ kind) for i in range(size)])
    masks = {"xy": ((1, 0), (2, 0)), "yx": ((2, 0), (1, 0)), "over": ((3, 0), (3, 0)), "near": ((0, 2), (0, 4)), "far": ((0, 4), (0, 2))}
    pairs = []
    for d in range(devices):
        for s in range(size):
            over, along = masks[kind][s % 2]
            pairs.append((d * size + s, (d ^ over) * size + (s ^ along)))
    return lax.ppermute(x, ("dp", "seq"), pairs)


def add(terms):
    return sum(t.astype(F32) for t in terms)


def hold(x, deps):
    return lax.optimization_barrier((x,) + tuple(deps))[0] if deps else x


def launch(deps, *items):
    items = [item for item in items if item.sends()]
    sends = [s for item in items for s in item.sends()]
    if not sends:
        return list(deps)
    held = lax.optimization_barrier(tuple(s[0] for s in sends) + tuple(deps))
    came = [swap(x, kind) for x, (_, kind) in zip(held, sends)]
    left = list(came)
    for item in items:
        count = len(item.sends())
        item.receive(left[:count])
        left = left[count:]
    return came


class Gather:
    def __init__(self, blocks, core):
        self.core = core
        self.next = [(blocks, "xy")]
        self.stage = 0

    def sends(self):
        return self.next

    def receive(self, came):
        if self.stage == 0:
            self.pieces = came
            half = came[0].shape[1] // 2
            part = lax.dynamic_slice_in_dim(came[0], self.core * half, half, axis=1)
            self.next = [(part, "yx"), (came[0], 1)]
        elif self.stage == 1:
            self.pieces = self.pieces + [came[1], came[0]]
            self.next = [(came[0], 1)]
        else:
            self.pieces = self.pieces + came
            self.next = []
        self.stage += 1


class Table:
    def __init__(self, params):
        self.own = jnp.pad(params.T, ((0, 16 - params.shape[1]), (0, 0)))

    def sends(self):
        return [(self.own, kind) for kind in ("xy", "yx", "over")]

    def receive(self, came):
        d = lax.axis_index("dp")
        first = lax.axis_index("seq") % 2 == 0
        a = [self.own, jnp.where(first, came[0], came[1]), jnp.where(first, came[1], came[0]), came[2]]
        a = [jnp.where(d % 2 == 1, a[i ^ 1], a[i]) for i in range(4)]
        a = [jnp.where(d // 2 == 1, a[i ^ 2], a[i]) for i in range(4)]
        self.whole = jnp.concatenate(a, axis=1).astype(F32)


class States:
    def __init__(self, state):
        self.parts = [state]
        self.mask = 1

    def sends(self):
        return [(self.parts[0], self.mask)] if self.mask < lax.axis_size("seq") else []

    def receive(self, came):
        self.parts = self.parts + came
        self.mask *= 2
        if self.sends():
            self.parts = [jnp.concatenate(self.parts, axis=0)]


class Halo:
    def __init__(self, tokens, cotangent):
        span = tokens.shape[2]
        toks, cots = tokens[:, 0], cotangent[:, 0]
        self.next = [(toks[:, span - 2 :], "next"), (jnp.stack([toks[:, :2], cots[:, :2]]), "last")]

    def sends(self):
        return self.next

    def receive(self, came):
        before, after = came
        blank = jnp.zeros(after.shape[:2] + (PAD - 2,) + after.shape[3:], BF)
        before = jnp.stack([before, jnp.zeros_like(before)])
        self.rows = jnp.concatenate([blank, before, after, blank], axis=2)


class Core:
    def __init__(self, keep, send, plain):
        self.keep, self.send, self.plain = keep, send, plain

    def sends(self):
        return [] if self.plain else [(self.send, 1)]

    def receive(self, came):
        self.terms = [self.keep, came[0]]

    def whole(self):
        full = jnp.stack([self.keep, self.send], axis=1).reshape(-1, self.keep.shape[-1]).astype(F32)
        return lax.psum_scatter(full, ("dp", "seq"), scatter_dimension=0, tiled=True)


class Quarter:
    def __init__(self, *cores):
        self.cores = cores
        self.rows = cores[0].keep.shape[1]
        self.plain = cores[0].plain
        self.came = []

    def value(self, p, rows=slice(None)):
        return jnp.concatenate([add([t[p, rows] for t in c.terms]) for c in self.cores], axis=-1)

    def sends(self):
        if self.plain or len(self.came) == 2:
            return []
        if not self.came:
            return [(self.value(slice(2, 4)).astype(BF), "xy")]
        return [((self.value(1) + self.came[0][1].astype(F32)).astype(BF), "yx")]

    def receive(self, came):
        self.came += came

    def final(self, rows):
        return self.value(0, rows) + self.came[0][0, rows].astype(F32) + self.came[1][rows].astype(F32)


class SmallQuarter(Quarter):
    def sends(self):
        if self.plain or self.came:
            return []
        return [(self.value(p).astype(BF), kind) for p, kind in ((2, "xy"), (1, "yx"), (3, "over"))]

    def final(self, rows):
        return self.value(0, rows) + add([t[rows] for t in self.came])


class Finish:
    def __init__(self, *quarters):
        self.quarters = quarters
        self.plain = quarters[0].plain
        self.block = quarters[0].rows // 4
        self.came = []
        if self.plain:
            self.total = jnp.concatenate([c.whole() for q in quarters for c in q.cores], axis=-1)

    def value(self, low, high):
        rows = slice(low * self.block, high * self.block)
        return jnp.concatenate([q.final(rows) for q in self.quarters], axis=-1)

    def sends(self):
        if self.plain or len(self.came) == 2:
            return []
        if not self.came:
            return [(self.value(2, 4).astype(BF), "near")]
        return [((self.value(1, 2) + self.came[0][self.block :].astype(F32)).astype(BF), "far")]

    def receive(self, came):
        self.came += came
        if len(self.came) == 2:
            self.total = self.value(0, 1) + self.came[0][: self.block].astype(F32) + self.came[1].astype(F32)


ANY = pl.BlockSpec(memory_space=pl.ANY)
SMEM = pl.BlockSpec(memory_space=pltpu.SMEM)


def shape(s, dtype):
    return jax.ShapeDtypeStruct(s, dtype)


BATCH = "batch"
LATE = "late"
HELD = "held"
VMEM = pl.BlockSpec(memory_space=pltpu.VMEM)


def call(name, kernel, grid, ins, outs, scratch, mib, deps=(), aliases=None, prefetch=False):
    ins = [(hold(ins[0][0], deps), ins[0][1])] + ins[1:]
    views = [i for i, (_, spec) in enumerate(ins + outs) if spec is BATCH]
    lates = [i for i, (_, spec) in enumerate(ins) if spec is LATE]
    extra = [pltpu.VMEM(ins[i][0].shape, ins[i][0].dtype) for i in lates]
    if lates:
        extra.append(pltpu.SemaphoreType.DMA((len(lates), grid[0])))

    def run(*refs):
        refs = list(refs)
        if lates:
            held, sems = refs[-len(extra) : -1], refs[-1]
            refs = refs[: -len(extra)]
            for k, i in enumerate(lates):
                refs[i] = Late(refs[i], held[k], sems, k)

            @pl.when(pl.program_id(0) == 0)
            def _():
                for b in range(grid[0]):
                    for i in lates:
                        refs[i].copy(b).start()

        for i in views:
            refs[i] = refs[i].at[pl.ds(pl.program_id(0), 1)]
        kernel(*refs)

    specs = {id(BATCH): VMEM, id(LATE): ANY, id(HELD): ANY}
    held = (LATE, HELD)
    operands = [pltpu.with_memory_space_constraint(a, pltpu.HBM) if any(s is h for h in held) else a for a, s in ins]
    grid_spec = pltpu.PrefetchScalarGridSpec(
        num_scalar_prefetch=1 if prefetch else 0,
        grid=grid,
        in_specs=[specs.get(id(s), s) for _, s in ins[1 if prefetch else 0 :]],
        out_specs=[specs.get(id(s), s) for _, s in outs],
        scratch_shapes=list(scratch) + extra,
    )
    return pl.pallas_call(
        run,
        grid_spec=grid_spec,
        out_shape=[a for a, _ in outs],
        input_output_aliases=aliases or {},
        compiler_params=pltpu.CompilerParams(vmem_limit_bytes=mib * 2**20),
        name=name,
    )(*operands)


def body(
    tokens,
    cotangent,
    lengths,
    att_key,
    att_value,
    att_recept,
    att_out,
    ffn_key,
    ffn_value,
    ffn_recept,
    params,
):
    batches, _, span, width = tokens.shape
    seqs = lengths.shape[2]
    ff = ffn_key.shape[1]
    tiles = ff // width
    ranks = lax.axis_size("seq")
    rows = span + 2 * PAD
    d, s = lax.axis_index("dp"), lax.axis_index("seq")
    core = s % 2
    at = lax.iota(jnp.int32, HEAD + batches * seqs)
    info = jnp.pad(lengths.reshape(batches * seqs), (HEAD, 0))
    for i, number in enumerate((s * span, d, s, core)):
        info = jnp.where(at == i, number, info)
    shard = att_key.shape[0]
    group_a = Gather(jnp.stack([att_key, att_value, att_recept, att_out]), core)
    group_b = Gather(jnp.stack([ffn_key[:, j * width : (j + 1) * width] for j in range(tiles)]), core)
    group_c = Gather(jnp.concatenate([ffn_value.reshape(-1, shard, width), ffn_recept[None]], axis=0), core)
    table = Table(params)

    edge = Halo(tokens, cotangent)
    came = launch((), group_a) + launch([info], edge, table)
    halo = edge.rows
    par = table.whole

    ext = (batches, rows, width)
    ext_f, ext_b = shape(ext, F32), shape(ext, BF)
    line_f = shape((batches, width // 128, rows, 128), F32)
    stats_shape = shape((batches, 2, rows, 128), F32)
    ends_shape = shape((batches, 2, 8, width), F32)
    wide_b = shape((batches, rows, ff), BF)
    square = pltpu.VMEM((1, width, width), BF)
    three = pltpu.VMEM((3, width, width), BF)
    square_f = pltpu.VMEM((width, width), F32)
    block_f = pltpu.VMEM((rows, width), F32)
    block_line = pltpu.VMEM((width // 128, rows, 128), F32)
    part = pltpu.VMEM((rows, 128), F32)

    def sems(n):
        return pltpu.SemaphoreType.DMA((n,))

    def refs(group):
        return [(p, ANY) for p in group.pieces]

    info_in = (info, SMEM)

    deps = came
    came = launch(deps, group_a)
    mix_key, mix_value, mix_recept, change_one, tok_ext, cot_ext, stats_one = call(
        "mix",
        functools.partial(mix_kernel, span, seqs),
        (batches,),
        [
            info_in,
            (tokens, pl.BlockSpec((1,) + tokens.shape[1:], lambda i: (i, 0, 0, 0))),
            (cotangent, pl.BlockSpec((1,) + tokens.shape[1:], lambda i: (i, 0, 0, 0))),
            (halo, pl.BlockSpec((2, 1, 2 * PAD, width), lambda i: (0, i, 0, 0))),
            (par, VMEM),
        ],
        [(ext_b, BATCH)] * 6 + [(stats_shape, BATCH)],
        [block_f],
        13,
        deps,
    )
    came = launch(came + [stats_one], group_a, group_b)
    deps, far = came[:1], came[1:]
    state_shape = shape((2 * batches, width), F32)
    exp_key, value, gate_one, ends, state, whole_a = call(
        "project",
        functools.partial(project_kernel, span, seqs),
        (batches,),
        [info_in]
        + [(a, BATCH) for a in (mix_key, mix_value, mix_recept)]
        + [(par, VMEM), (att_key, ANY), (att_value, ANY), (att_recept, ANY)]
        + refs(group_a),
        [(line_f, BATCH)] * 3
        + [(ends_shape, BATCH), (state_shape, VMEM), (pltpu.HBM((3, width, width), BF), ANY)],
        [three, sems(PER + 3)],
        10,
        deps,
    )
    exchange = States(state)
    came = launch([state], exchange)
    far = launch(far + came, group_b)
    came = launch(came, exchange)
    deps = came + far
    far = launch(deps, group_b)
    after = launch(deps, group_c)
    while exchange.sends():
        came = launch(came, exchange)
    states = exchange.parts
    deps = came + far
    came = after
    gated, by_num, by_recept, wkv, middle, ffn_in, ffn_gate_in, change_two, stats_two, whole_out = call(
        "recur",
        functools.partial(recur_kernel, span, seqs, ranks, len(states)),
        (batches,),
        [info_in]
        + [(a, BATCH) for a in (exp_key, value, gate_one)]
        + [(ends, BATCH), (tok_ext, BATCH)]
        + [(par, VMEM), (att_out, ANY)]
        + [(a, VMEM) for a in states]
        + refs(group_a),
        [
            (a, BATCH)
            for a in (ext_b, ext_b, ext_b, ext_b, ext_f, ext_b, ext_b, ext_b, stats_shape)
        ]
        + [(pltpu.HBM((1, width, width), BF), ANY)],
        [square, block_line, block_line, sems(PER + 1)],
        10,
        deps,
    )
    deps = came + [stats_two]
    came = launch(deps, group_c)
    key_buf = pltpu.VMEM((tiles, width, width), BF)
    own_value = ffn_value.reshape(4, shard, width)
    hidden, whole_key = call(
        "hidden",
        hidden_kernel,
        (batches,),
        [info_in, (ffn_in, BATCH), (ffn_key, ANY)] + refs(group_b),
        [(wide_b, BATCH), (pltpu.HBM((tiles, width, width), BF), ANY)],
        [key_buf, sems(tiles + PER + 1)],
        11,
        deps,
    )
    came = launch(came + [hidden], group_c)
    mixed_shape = shape((batches, 1, span, width), BF)
    value_buf = pltpu.VMEM((4 * tiles, shard, width), BF)
    mixed, grad_carried, grad_gate, whole_value, whole_gate = call(
        "gate",
        functools.partial(gate_kernel, span, seqs),
        (batches,),
        [info_in]
        + [(a, BATCH) for a in (hidden, ffn_gate_in, middle, cot_ext)]
        + [(own_value, ANY), (ffn_recept, ANY)]
        + refs(group_c),
        [(mixed_shape, BATCH)]
        + [(ext_b, BATCH)] * 2
        + [(pltpu.HBM(value_buf.shape, BF), ANY), (pltpu.HBM((1, width, width), BF), ANY)],
        [value_buf, square, sems(2 * PER + 2)],
        17,
        came,
    )

    plain = ranks != 8 or (width // (4 * ranks)) % 8 != 0
    nz = 1 if plain else 4
    plan = (nz, plain)

    def core_of(keep, send):
        return Core(*(a.reshape(4, -1, a.shape[-1]) for a in (keep, send)), plain)

    big = pltpu.HBM((4, nz, ff // (8 * nz), width), BF)
    big_kept = shape(big.shape, BF)

    def place_of(other):
        def index(i, info):
            core = (info[3] + other) % 2
            return (i if plain else turn(core, i), 0, 0, 0)

        return pl.BlockSpec((1,) + big.shape[1:], index)

    keep_v, send_v = call(
        "value_grad",
        functools.partial(value_grad_kernel, span, plan),
        (4,),
        [info_in, (hidden, VMEM), (grad_carried, VMEM)],
        [(big_kept, place_of(0)), (big, place_of(1))],
        [square_f],
        10,
        prefetch=True,
    )
    core_value = core_of(keep_v, send_v)
    deps = [keep_v]
    came = launch(deps, core_value)
    wide_half = pltpu.HBM((width // 2, ff + width), BF)
    wide_kept = shape(wide_half.shape, BF)
    keep_k, send_k = call(
        "gate_back",
        functools.partial(gate_back_kernel, span, plan),
        (1,),
        [info_in, (ffn_gate_in, VMEM), (grad_gate, VMEM)],
        [(a, pl.BlockSpec((width // 2, width), lambda i: (0, tiles))) for a in (wide_kept, wide_half)],
        [square_f],
        10,
        deps,
    )
    deps = came + [keep_k]
    sum_value = Quarter(core_value)
    came = launch(deps, sum_value)
    out_tile = pl.BlockSpec((width // 2, width), lambda i: (0, i))
    keep_k, send_k, _, grad_in = call(
        "inner",
        functools.partial(inner_kernel, span, plan),
        (tiles,),
        [
            info_in,
            (keep_k, ANY),
            (send_k, HELD),
            (hidden, VMEM),
            (grad_carried, VMEM),
            (ffn_in, VMEM),
            (whole_key.reshape(value_buf.shape), HELD),
            (whole_value, HELD),
        ],
        [(wide_kept, out_tile), (wide_half, out_tile)] + [(pltpu.VMEM(wide_b.shape, BF), VMEM), (ext_b, VMEM)],
        [
            value_buf,
            square_f,
            sems(tiles + 1),
        ],
        20,
        deps,
        {1: 0, 2: 1, 3: 2},
    )
    core_key = core_of(keep_k, send_k)
    deps = came + [grad_in]
    came = launch(deps, sum_value, core_key)
    sums_shape = shape((8, width), F32)
    grad_middle, grad_att, grad_recept, grad_num, grad_den, ends_back, state_back, sums = call(
        "attend_back",
        functools.partial(attend_back_kernel, span, seqs),
        (batches,),
        [info_in]
        + [
            (a, LATE if a is cot_ext or a is by_num or a is by_recept or a is wkv else BATCH)
            for a in (
                grad_gate,
                grad_in,
                change_two,
                middle,
                stats_two,
                cot_ext,
                by_num,
                by_recept,
                wkv,
            )
        ]
        + [(par, VMEM), (whole_out, VMEM), (whole_gate, VMEM)],
        [(a, BATCH) for a in (ext_f, ext_b, ext_b, pltpu.VMEM(line_f.shape, F32), pltpu.VMEM(line_f.shape, F32))]
        + [(ends_shape, BATCH)]
        + [(state_shape, VMEM), (sums_shape, VMEM)],
        [pltpu.VMEM((4, 8, width), F32), block_f, block_f, part, part],
        16,
        deps,
    )
    exchange = States(state_back)
    sum_key = Quarter(core_key)
    all_value = Finish(sum_value)
    came = launch(came + [state_back], exchange)
    deps = came
    came = launch(came, exchange, sum_key)
    came, far = came[:1], came[1:]
    two = pltpu.HBM((width // 2, 2 * width), BF)
    two_kept = shape(two.shape, BF)
    keep_o, send_o = call(
        "recept",
        functools.partial(recept_kernel, span, plan),
        (2,),
        [info_in] + [(a, VMEM) for a in (gated, grad_att, mix_recept, grad_recept)],
        [(a, pl.BlockSpec((width // 2, width), lambda i: (0, i))) for a in (two_kept, two)],
        [square_f],
        10,
        deps,
    )
    core_out = core_of(keep_o, send_o)
    deps = came + [keep_o]
    came = launch(deps, exchange)
    num_prev, den_prev, back_recept = call(
        "again",
        functools.partial(again_kernel, span, seqs, ranks, len(states)),
        (batches,),
        [info_in]
        + [(a, BATCH) for a in (exp_key, value, ends, grad_recept)]
        + [(par, VMEM), (whole_a, HELD)]
        + [(a, VMEM) for a in states],
        [(line_f, BATCH)] * 2 + [(ext_b, BATCH)],
        [pltpu.VMEM((width, width), BF), sems(1)],
        8,
        deps,
    )
    while exchange.sends():
        came = launch(came, exchange)
    states_back = exchange.parts
    deps = came + far + [back_recept]
    came = launch(deps, all_value, sum_key, core_out)
    grad_key, grad_value, keep_l, send_l, sums_back = call(
        "recur_back",
        functools.partial(recur_back_kernel, span, seqs, ranks, len(states_back), plan),
        (batches,),
        [info_in]
        + [
            (a, LATE if a is mix_key or a is mix_value else BATCH)
            for a in (
                grad_num,
                grad_den,
                exp_key,
                value,
                num_prev,
                den_prev,
                ends_back,
                mix_key,
                mix_value,
            )
        ]
        + [(par, VMEM)]
        + [(a, VMEM) for a in states_back],
        [(ext_b, VMEM)] * 2 + [(two_kept, VMEM), (two, VMEM)] + [(sums_shape, VMEM)],
        [block_line, block_line, square_f, pltpu.VMEM((2, 8, width), F32)],
        18,
        deps,
    )
    core_last = core_of(keep_l, send_l)
    deps = launch(came + [sums_back], core_last)
    all_key = Finish(sum_key)
    sum_last = Quarter(core_last, core_out)
    came = launch(deps, all_key, sum_last, all_value)
    grad_shape = shape((batches, 1, span, width), F32)
    half_table = shape((width // 2, 128), BF)
    inners, parts, keep_p, send_p = call(
        "first_back",
        functools.partial(first_back_kernel, span, seqs, plan),
        (batches,),
        [info_in]
        + [(a, BATCH) for a in (grad_key, grad_value, back_recept)]
        + [(a, LATE) for a in (tok_ext, stats_one, change_one)]
        + [(sums, VMEM), (sums_back, VMEM), (par, VMEM)]
        + [(whole_a, HELD)],
        [(ext_f, BATCH), (stats_shape, BATCH)] + [(half_table, VMEM)] * 2,
        [
            pltpu.VMEM((2, width, width), BF),
            block_f,
            block_f,
            pltpu.VMEM((7, 8, width), F32),
            pltpu.VMEM((width, 128), F32),
            sems(1),
        ],
        18,
        deps,
    )
    core_table = core_of(keep_p, send_p)
    deps = launch(came + [keep_p], core_table)
    sum_table = SmallQuarter(core_table)
    came = launch(deps, sum_last, sum_table, all_key)
    (tokens_grad,) = call(
        "tokens_grad",
        functools.partial(tokens_grad_kernel, span),
        (batches,),
        [info_in] + [(a, BATCH) for a in (inners, parts, tok_ext, stats_one, grad_middle)],
        [(grad_shape, BATCH)],
        [],
        7,
        deps,
    )
    all_last = Finish(sum_last, sum_table)
    came = launch(came + [tokens_grad], all_last)
    launch(came, all_last)
    key, last = all_key.total, all_last.total
    return (
        mixed,
        tokens_grad,
        last[:, :width],
        last[:, width : 2 * width],
        last[:, 3 * width : 4 * width],
        last[:, 2 * width : 3 * width],
        key[:, :ff],
        all_value.total,
        key[:, ff:],
        last[:, 4 * width : 4 * width + params.shape[1]],
    )


def solution(mesh):
    split = P(("dp", "seq"), None)
    rows = P("dp", None)
    stream = P(None, "dp", "seq", None)
    return jax.shard_map(
        body,
        mesh=mesh,
        in_specs=(stream, stream, P(None, "dp", None)) + (rows,) * 8,
        out_specs=(stream, stream) + (split,) * 8,
        check_vma=False,
    )
```

```python
import functools

import jax
import jax.numpy as jnp
from jax import lax
from jax.experimental import pallas as pl
from jax.experimental.pallas import tpu as pltpu
from jax.sharding import PartitionSpec as P

EPS = 1e-05
BF = jnp.bfloat16
F32 = jnp.float32
PAD = 16
FAR = 1 << 30
PER = 5
HEAD = 4


def bounds_of(info, batch, seqs):
    ends = [jnp.int32(0)]
    for i in range(seqs):
        ends.append(ends[-1] + info[HEAD + batch * seqs + i])
    return ends


def positions(info, row, count):
    return lax.broadcasted_iota(jnp.int32, (count, 128), 0) + (row - PAD + info[0])


def since_start(pos, bounds):
    best = jnp.full(pos.shape, FAR, jnp.int32)
    for b in bounds:
        best = jnp.where(pos >= b, jnp.minimum(best, pos - b), best)
    return best


def until_start(pos, bounds):
    best = jnp.full(pos.shape, FAR, jnp.int32)
    for b in bounds:
        best = jnp.where(pos < b, jnp.minimum(best, b - pos), best)
    return best


def wide(mask, width):
    return jnp.concatenate([mask] * (width // 128), axis=1)


def flag(cond, width):
    return wide(jnp.where(cond, 1.0, 0.0).astype(F32), width)


def keep_flag(pos, bounds, width):
    hit = pos == bounds[0]
    for b in bounds[1:]:
        hit = hit | (pos == b)
    return wide(jnp.where(hit, 0.0, 1.0).astype(F32), width)


def rows_of(count, width):
    return wide(lax.broadcasted_iota(jnp.int32, (count, 128), 0), width)


def down(x, carry):
    rolled = pltpu.roll(x, 1, 0)
    return jnp.where(rows_of(*x.shape) == 0, carry, rolled)


def up(x, carry):
    n = x.shape[0]
    rolled = pltpu.roll(x, n - 1, 0)
    return jnp.where(rows_of(*x.shape) == n - 1, carry, rolled)


def nn(a, b):
    return jnp.dot(a, b, preferred_element_type=F32)


def nt(a, b):
    return lax.dot_general(a, b, (((1,), (1,)), ((), ())), preferred_element_type=F32)


def tn(a, b):
    return lax.dot_general(a, b, (((0,), (0,)), ((), ())), preferred_element_type=F32)


def slabs(span, body, init, reverse=False, unroll=4):
    step = 32
    many = span // step

    def one(i, carry):
        at = many - 1 - i if reverse else i
        return body(pl.multiple_of(PAD + at * step, PAD), step, True, carry)

    first, last = (PAD + span, 0) if reverse else (0, PAD + span)
    carry = body(first, PAD, False, init)
    carry = lax.fori_loop(0, many, one, carry, unroll=unroll)
    return body(last, PAD, False, carry)


def lanes(x):
    return sum(x[:, i : i + 128] for i in range(0, x.shape[1], 128))


def tile(x, i):
    return x[:, i * 128 : (i + 1) * 128]


def row_mean(ref, width):
    total = jnp.sum(ref[...], axis=1, keepdims=True) * (1.0 / width)
    return jnp.broadcast_to(total, ref.shape)


def steps_of(low, high, body, carry, reverse=False, unroll=4):
    def one(i, carry):
        return body(high - 1 - i if reverse else low + i, carry)

    count = high - low
    while count % unroll:
        unroll -= 1
    return lax.fori_loop(0, count, one, carry, unroll=unroll)


def fold(x):
    n, c = x.shape
    return jnp.sum(x.reshape(n // 8, 8, c), axis=0)


def no_start(bounds, low, high):
    hit = jnp.int32(0)
    for b in bounds:
        hit = hit | jnp.where((b > low) & (b <= high), 1, 0)
    return jnp.where(hit == 0, 1.0, 0.0).astype(F32)


def incoming(info, states, batch, bounds, speed, span, ranks, reverse):
    me, base = info[2], info[0]
    num = jnp.zeros(speed.shape, F32)
    den = jnp.zeros(speed.shape, F32)
    for k in range(1, ranks):
        other = me ^ k
        if reverse:
            gap = other - me - 1
            clear = no_start(bounds, base + span + 1, other * span + 1)
        else:
            gap = me - 1 - other
            clear = no_start(bounds, (other + 1) * span - 2, base - 2)
        use = jnp.where(gap >= 0, clear, 0.0).astype(F32)
        weight = jnp.exp(-speed * (jnp.maximum(gap, 0) * span).astype(F32)) * use
        per = sum(r.shape[0] for r in states) // ranks
        many = states[0].shape[0] // per
        at = (k % many) * per + 2 * batch
        num += weight * states[k // many][pl.ds(at, 1), :]
        den += weight * states[k // many][pl.ds(at + 1, 1), :]
    return num, den


def start_all(copies):
    for c in copies:
        c.start()


def wait_all(copies):
    for c in copies:
        c.wait()


def copies_of(info, owns, pieces, blocks, target, sems, at=0):
    d, c = info[1], info[3]
    shard = owns[0].shape[0]
    half = shard // 2
    out = []
    for k, own in enumerate(owns):
        out.append(pltpu.make_async_copy(own, target.at[k, pl.ds(pl.multiple_of(d * shard, 16), shard)], sems.at[at]))
        at += 1
    places = ((d ^ (1 + c)) * shard, (d ^ (2 - c)) * shard, (d ^ 3) * shard + c * half, (d ^ 3) * shard + (1 - c) * half)
    for row, ref in zip(places, pieces):
        source = ref.at[blocks]
        place = target.at[:, pl.ds(pl.multiple_of(row, 16), source.shape[1])]
        out.append(pltpu.make_async_copy(source, place, sems.at[at]))
        at += 1
    return out


def value_copies(info, own, pieces, target, sems, at=0):
    d, c = info[1], info[3]
    half = target.shape[1] // 2
    out = [pltpu.make_async_copy(own, target.at[pl.ds(4 * d, 4)], sems.at[at])]
    places = ((d ^ (1 + c), 0), (d ^ (2 - c), 0), (d ^ 3, c * half), (d ^ 3, (1 - c) * half))
    for (block, row), ref in zip(places, pieces):
        at += 1
        place = target.at[pl.ds(4 * block, 4), pl.ds(pl.multiple_of(row, 16), ref.shape[1])]
        out.append(pltpu.make_async_copy(ref.at[pl.ds(0, 4)], place, sems.at[at]))
    return out


def place(info, plain):
    if plain:
        return 0, 0, 0
    return info[1], info[2] // 2, info[3]


def turn(core, i):
    return core * i + (1 - core) * (((i & 1) << 1) | (i >> 1))


def scatter_rows(info, src, keep, send, plan, write):
    nz, plain = plan
    d, z, c = place(info, plain)
    block = src.shape[0] // (8 * nz)
    per = 4 * nz * block // 16
    groups = block // 8
    for ref, core in ((keep, c), (send, 1 - c)):
        for slab in range(per):
            parts = []
            for g in (2 * slab, 2 * slab + 1):
                i = g % groups
                q = (g // groups) % nz
                p = g // (groups * nz)
                if not plain:
                    p, q = turn(core, p), turn(core, q)
                row = ((d ^ p) * nz + (z ^ q)) * (2 * block) + core * block + i * 8
                parts.append(src[pl.ds(pl.multiple_of(row, 8), 8), :])
            write(ref, slab * 16, jnp.concatenate(parts, axis=0).astype(BF))


def keep_whole(batch, buffer, target, sem):
    def copy():
        return pltpu.make_async_copy(buffer, target, sem)

    pl.when(batch == 0)(lambda: copy().start())
    pl.when(batch == pl.num_programs(0) - 1)(lambda: copy().wait())


class Late:
    def __init__(self, source, buffer, sems, index):
        self.source, self.buffer, self.sems, self.index = source, buffer, sems, index
        self.shape = (1,) + tuple(buffer.shape[1:])

    def copy(self, b):
        return pltpu.make_async_copy(self.source.at[b], self.buffer.at[b], self.sems.at[self.index, b])

    def ready(self):
        b = pl.program_id(0)
        self.copy(b).wait()
        return self.buffer.at[pl.ds(b, 1)]


def mix_kernel(
    span, seqs, info, tokens, cotangent, halo, par, mix_key, mix_value, mix_recept, change, tok_ext, cot_ext, stats, held
):
    batch = pl.program_id(0)
    bounds = bounds_of(info, batch, seqs)
    gain, bias = par[0:1, :], par[1:2, :]
    mixes = (par[2:3, :], par[3:4, :], par[4:5, :])
    width = tokens.shape[3]
    mean, scale = stats.at[0, 0], stats.at[0, 1]

    def load(row, n, owned, carry):
        at = pl.ds(row, n)
        if owned:
            x, g = tokens[0, 0, pl.ds(row - PAD, n), :], cotangent[0, 0, pl.ds(row - PAD, n), :]
        else:
            low = 0 if row == 0 else PAD
            x, g = halo[0, 0, low : low + PAD, :], halo[1, 0, low : low + PAD, :]
        tok_ext[0, at, :] = x
        cot_ext[0, at, :] = g
        x = x.astype(F32)
        held[at, :] = x
        mean[at, :] = lanes(x)
        return carry

    slabs(span, load, 0)
    mean[...] = row_mean(mean, width)

    def spread(row, n, owned, carry):
        at = pl.ds(row, n)
        x = held[at, :] - wide(mean[at, :], width)
        scale[at, :] = lanes(x * x)
        return carry

    slabs(span, spread, 0)
    scale[...] = lax.rsqrt(row_mean(scale, width) + EPS)

    def body(row, n, owned, carry):
        at = pl.ds(row, n)
        normed = (held[at, :] - wide(mean[at, :], width)) * wide(scale[at, :], width)
        first = normed * gain + bias
        keep = keep_flag(positions(info, row, n), bounds, width)
        shifted = down(first, carry) * keep
        diff = first - shifted
        for mu, ref in zip(mixes, (mix_key, mix_value, mix_recept)):
            ref[0, at, :] = (shifted + diff * mu).astype(BF)
        change[0, at, :] = diff.astype(BF)
        return first[n - 1 : n]

    slabs(span, body, jnp.zeros((1, width), F32))


class Chunks:
    def __init__(self, info, bounds, rows, speed):
        self.size = rows // 8
        self.bounds = bounds
        self.base = info[0] - PAD
        self.row8 = lax.broadcasted_iota(jnp.int32, (8, 128), 0)
        self.start = self.row8 * self.size + self.base
        self.speed = speed
        self.tiles = speed.shape[1] // 128
        self.rate = self.split(jnp.exp(-speed))

    def split(self, row):
        return [jnp.broadcast_to(tile(row, i), (8, 128)) for i in range(self.tiles)]

    def at(self, j):
        return pl.ds(j, 8, stride=self.size)

    def keep(self, j, ahead=0):
        pos = self.start + (j + ahead)
        hit = pos == self.bounds[0]
        for b in self.bounds[1:]:
            hit = hit | (pos == b)
        return jnp.where(hit, 0.0, 1.0).astype(F32)

    def decay(self, low, high, count):
        clear = no_start(self.bounds, self.base + low, self.base + high)
        return jnp.exp(-self.speed * float(count)) * clear


def join(tiles):
    return jnp.concatenate(tiles, axis=1)


def write_state(state, batch, num, den):
    for i in range(state.shape[0] // 2):

        @pl.when(batch == i)
        def _():
            state[2 * i : 2 * i + 1, :] = num
            state[2 * i + 1 : 2 * i + 2, :] = den


def project_kernel(
    span, seqs, info, mix_key, mix_value, mix_recept, par, own_key, own_value, own_recept, *refs
):
    pieces = refs[0:4]
    exp_key, value, gate, ends, state, kept, weights, sems = refs[4:]
    batch = pl.program_id(0)
    bounds = bounds_of(info, batch, seqs)
    rows, width = mix_key.shape[1:]

    def copies():
        return copies_of(info, (own_key, own_value, own_recept), pieces, pl.ds(0, 3), weights, sems)

    @pl.when(batch == 0)
    def _():
        start_all(copies())
        wait_all(copies())

    acts = (jnp.exp, lambda x: x, jax.nn.sigmoid)
    for k, (left, ref, act) in enumerate(zip((mix_key, mix_value, mix_recept), (exp_key, value, gate), acts)):
        part = act(nn(left[0], weights[k]))
        for i in range(width // 128):
            ref[0, i] = tile(part, i)

    speed = jnp.exp(par[5:6, :])
    chunks = Chunks(info, bounds, rows, speed)
    size = chunks.size

    def step(j, carry, cut=False):
        nums, dens = carry
        at = chunks.at(j)
        keep = chunks.keep(j)
        num_out, den_out = [], []
        for i in range(chunks.tiles):
            ek = exp_key[0, i, at, :]
            if cut:
                ek = jnp.where(chunks.row8 == 0, 0.0, ek)
            factor = chunks.rate[i] * keep
            num_out.append(factor * nums[i] + ek * value[0, i, at, :])
            den_out.append(factor * dens[i] + ek)
        return tuple(num_out), tuple(den_out)

    zero = tuple(jnp.zeros((8, 128), F32) for _ in range(chunks.tiles))
    last = PAD + span - 2 - 7 * size
    carry = (zero, zero)
    for j in range(PAD - 1):
        carry = step(j, carry, cut=True)
    carry = steps_of(PAD - 1, last + 1, step, carry)
    inside = [join(c)[7:8] for c in carry]
    carry = steps_of(last + 1, size, step, carry, unroll=size)
    whole_ends = [join(c) for c in carry]
    out = []
    for k in range(2):
        ends[0, k] = whole_ends[k]
        total = whole_ends[k][0:1]
        for s in range(1, 7):
            total = whole_ends[k][s : s + 1] + chunks.decay(s * size - 1, (s + 1) * size - 1, size) * total
        out.append(inside[k] + chunks.decay(7 * size - 1, 7 * size + last, last + 1) * total)
    write_state(state, batch, *out)
    keep_whole(batch, weights, kept, sems.at[PER + 2])


def forward_scan(info, states, batch, chunks, exp_key, value, ends, span, ranks, emit):
    size, width = chunks.size, chunks.speed.shape[1]
    entering = incoming(info, states, batch, chunks.bounds, chunks.speed, span, ranks, False)
    begin = []
    for k in range(2):
        lines = [jnp.zeros((1, width), F32)]
        lines.append(ends[0, k, 0:1, :] + chunks.decay(PAD - 2, size - 1, size - PAD + 1) * entering[k])
        for s in range(1, 7):
            lines.append(ends[0, k, s : s + 1, :] + chunks.decay(s * size - 1, (s + 1) * size - 1, size) * lines[-1])
        begin.append(jnp.concatenate(lines, axis=0))
    carry = tuple(tuple(tile(b, i) for i in range(chunks.tiles)) for b in begin)

    def step(j, carry, insert=None):
        nums, dens = carry
        at = chunks.at(j)
        keep = chunks.keep(j)
        num_out, den_out = [], []
        for i in range(chunks.tiles):
            ek, v = exp_key[0, i, at, :], value[0, i, at, :]
            before_num = keep * nums[i]
            before_den = keep * dens[i]
            x, y = ek * v, ek
            emit(at, i, before_num, before_den, ek, x)
            if insert is not None:
                x = jnp.where(chunks.row8 == 0, insert[0][i], x)
                y = jnp.where(chunks.row8 == 0, insert[1][i], y)
            num_out.append(chunks.rate[i] * before_num + x)
            den_out.append(chunks.rate[i] * before_den + y)
        return tuple(num_out), tuple(den_out)

    none = [[0.0] * chunks.tiles] * 2
    for j in range(PAD - 2):
        carry = step(j, carry, none)
    carry = step(PAD - 2, carry, [chunks.split(e) for e in entering])
    steps_of(PAD - 1, size, step, carry)


def recur_kernel(span, seqs, ranks, parts, info, exp_key, value, gate, ends, tokens, par, own_out, *refs):
    states, refs = refs[:parts], refs[parts:]
    pieces = refs[0:4]
    (
        gated,
        by_num,
        by_recept,
        wkv,
        middle,
        ffn_in,
        ffn_gate_in,
        change,
        stats,
        kept,
        wo,
        line_wkv,
        line_inverse,
        sems,
    ) = refs[4:]
    batch = pl.program_id(0)
    bounds = bounds_of(info, batch, seqs)
    rows, width = tokens.shape[1:]

    def copies():
        return copies_of(info, (own_out,), pieces, pl.ds(3, 1), wo, sems)

    @pl.when(batch == 0)
    def _():
        start_all(copies())

    chunks = Chunks(info, bounds, rows, jnp.exp(par[5:6, :]))
    boost = chunks.split(jnp.exp(par[6:7, :]))

    def emit(at, i, before_num, before_den, ek, x):
        inverse = 1.0 / (before_den + boost[i] * ek)
        line_inverse[i, at, :] = inverse
        line_wkv[i, at, :] = (before_num + boost[i] * x) * inverse

    forward_scan(info, states, batch, chunks, exp_key, value, ends, span, ranks, emit)

    def pack(row, n, owned, carry):
        at = pl.ds(row, n)
        out = ([], [], [], [])
        for i in range(chunks.tiles):
            w, sig = line_wkv[i, at, :], gate[0, i, at, :]
            g = w * sig
            out[0].append(g)
            out[1].append(sig * line_inverse[i, at, :])
            out[2].append(g * (1.0 - sig))
            out[3].append(w)
        for ref, tiles in zip((gated, by_num, by_recept, wkv), out):
            ref[0, at, :] = join(tiles).astype(ref.dtype)
        return carry

    slabs(span, pack, 0)

    @pl.when(batch == 0)
    def _():
        wait_all(copies())

    middle[0] = nn(gated[0], wo[0])
    gain, bias = par[7:8, :], par[8:9, :]
    mean, scale = stats.at[0, 0], stats.at[0, 1]

    def residual(row, n, owned, carry):
        at = pl.ds(row, n)
        mid = middle[0, at, :] + tokens[0, at, :].astype(F32)
        middle[0, at, :] = mid
        mean[at, :] = lanes(mid)
        return carry

    slabs(span, residual, 0)
    mean[...] = row_mean(mean, width)

    def spread(row, n, owned, carry):
        at = pl.ds(row, n)
        x = middle[0, at, :] - wide(mean[at, :], width)
        scale[at, :] = lanes(x * x)
        return carry

    slabs(span, spread, 0)
    scale[...] = lax.rsqrt(row_mean(scale, width) + EPS)

    def body(row, n, owned, carry):
        at = pl.ds(row, n)
        normed = (middle[0, at, :] - wide(mean[at, :], width)) * wide(scale[at, :], width)
        second = normed * gain + bias
        keep = keep_flag(positions(info, row, n), bounds, width)
        shifted = down(second, carry) * keep
        diff = second - shifted
        ffn_in[0, at, :] = (shifted + diff * par[9:10, :]).astype(BF)
        ffn_gate_in[0, at, :] = (shifted + diff * par[10:11, :]).astype(BF)
        change[0, at, :] = diff.astype(BF)
        return second[n - 1 : n]

    slabs(span, body, jnp.zeros((1, width), F32))
    keep_whole(batch, wo, kept, sems.at[PER])


def hidden_kernel(info, ffn_in, own_key, *refs):
    pieces = refs[0:4]
    hidden, kept, wk, sems = refs[4:]
    width = ffn_in.shape[2]
    tiles = wk.shape[0]

    def copies():
        owns = [own_key.at[:, pl.ds(j * width, width)] for j in range(tiles)]
        return copies_of(info, owns, pieces, pl.ds(0, tiles), wk, sems)

    @pl.when(pl.program_id(0) == 0)
    def _():
        start_all(copies())
        wait_all(copies())

    for j in range(tiles):
        relu = jnp.maximum(nn(ffn_in[0], wk[j]), 0.0)
        hidden[0, :, pl.ds(j * width, width)] = (relu * relu).astype(BF)
    keep_whole(pl.program_id(0), wk, kept, sems.at[tiles + PER])


def gate_kernel(
    span, seqs, info, hidden, ffn_gate_in, middle, cotangent, own_value, own_recept, *refs
):
    pieces = refs[0:4]
    mixed, grad_carried, grad_gate, kept, kept_gate, wv, wr, sems = refs[4:]
    batch = pl.program_id(0)
    bounds = bounds_of(info, batch, seqs)
    rows, width = middle.shape[1:]

    def copies():
        return (
            copies_of(info, (own_recept,), pieces, pl.ds(4, 1), wr, sems),
            value_copies(info, own_value, pieces, wv, sems, PER),
        )

    @pl.when(batch == 0)
    def _():
        for c in copies():
            start_all(c)
        wait_all(copies()[0])
    keep_whole(batch, wv, kept, sems.at[2 * PER])
    keep_whole(batch, wr, kept_gate, sems.at[2 * PER + 1])


    @pl.when(batch == 0)
    def _():
        wait_all(copies()[1])

    flat = wv[...].reshape(wv.shape[0] * wv.shape[1], width)
    total = bounds[-1]
    step = rows // 2
    for low in range(0, rows, step):
        gate = nn(ffn_gate_in[0, low : low + step, :], wr[0])
        carried = nn(hidden[0, low : low + step, :], flat)
        for i in range(0, step, PAD):
            row = low + i
            at = pl.ds(row, PAD)
            sig = jax.nn.sigmoid(gate[i : i + PAD])
            car = carried[i : i + PAD]
            live = flag(positions(info, row, PAD) < total, width)
            grad = cotangent[0, at, :].astype(F32) * live
            if PAD <= row < PAD + span:
                mixed[0, 0, row - PAD : row, :] = (middle[0, at, :] + sig * car).astype(BF)
            part = grad * sig
            grad_carried[0, at, :] = part.astype(BF)
            grad_gate[0, at, :] = (part * car * (1.0 - sig)).astype(BF)


def over_own(left, right, span):
    own = pl.ds(PAD, span)
    both = [jnp.concatenate([f[b, own] for b in range(f.shape[0])], axis=0) for f in (left, right)]
    return tn(*both)


def store_sixteen(ref, row, value):
    ref[row : row + 16, :] = value


def value_grad_kernel(span, plan, info, hidden, grad_carried, keep, send, total):
    nz, plain = plan
    d, z, c = place(info, plain)
    width = total.shape[1]
    column = pl.ds(pl.multiple_of((pl.program_id(0) ^ d) * width, width), width)
    block = keep.shape[2]
    total[...] = over_own(hidden.at[:, :, column], grad_carried, span)
    for q in range(nz):
        for ref, core in ((keep, c), (send, 1 - c)):
            row = pl.multiple_of(((z ^ (q if plain else turn(core, q))) * 2 + core) * block, 8)
            ref[0, q] = total[pl.ds(row, block), :].astype(BF)


def gate_back_kernel(span, plan, info, ffn_gate_in, grad_gate, keep, send, total):
    total[...] = over_own(ffn_gate_in, grad_gate, span)
    scatter_rows(info, total, keep, send, plan, store_sixteen)


def inner_kernel(
    span, plan, info, hidden, grad_carried, ffn_in, key, whole_value, keep, send, grad_inner, grad_in, weights, total, sems
):
    step = pl.program_id(0)
    batches, _, width = grad_in.shape
    tiles = weights.shape[0] // 4
    last = step == tiles - 1

    def value_copy(j):
        block = pl.ds(4 * j, 4)
        return pltpu.make_async_copy(whole_value.at[block], weights.at[block], sems.at[j])

    def key_copy():
        return pltpu.make_async_copy(key, weights, sems.at[tiles])

    @pl.when(step == 0)
    def _():
        for j in range(tiles):
            value_copy(j).start()

    here = pl.multiple_of(step * width, width)
    for j in range(tiles):
        pl.when(step == j)(lambda: value_copy(j).wait())
    value = weights[pl.ds(4 * step, 4)].reshape(4 * weights.shape[1], width)
    for b in range(batches):
        back = nt(grad_carried[b], value)
        at = pl.ds(here, width)
        square = hidden[b, :, at].astype(F32)
        relu = square * lax.rsqrt(jnp.maximum(square, 1e-30))
        grad_inner[b, :, at] = (back * (2.0 * relu)).astype(BF)
    pl.when(last)(lambda: key_copy().start())
    total[...] = over_own(ffn_in, grad_inner.at[:, :, pl.ds(here, width)], span)
    scatter_rows(info, total, keep, send, plan, store_sixteen)

    @pl.when(last)
    def _():
        key_copy().wait()
        blocks = [weights[4 * j : 4 * j + 4].reshape(4 * weights.shape[1], width) for j in range(tiles)]
        right = jnp.concatenate(blocks, axis=1)
        for b in range(batches):
            grad_in[b] = nt(grad_inner[b], right).astype(BF)


def attend_back_kernel(
    span,
    seqs,
    info,
    grad_gate,
    grad_in,
    change,
    middle,
    stats,
    cotangent,
    by_num,
    by_recept,
    wkv,
    par,
    wo,
    wr,
    *refs,
):
    (grad_middle, grad_att, grad_recept, grad_num, grad_den, ends, state, sums, acc, held, back_gate, part_a, part_b) = refs
    batch = pl.program_id(0)
    bounds = bounds_of(info, batch, seqs)
    rows, width = middle.shape[1:]

    @pl.when(batch == 0)
    def _():
        acc[...] = jnp.zeros_like(acc)

    gain = par[7:8, :]
    mu, nu = par[9:10, :], par[10:11, :]
    total = bounds[-1]

    back_gate[...] = nt(grad_gate[0], wr[0])
    mean, scale = stats.at[0, 0], stats.at[0, 1]

    def normed_of(at):
        return (middle[0, at, :] - wide(mean[at, :], width)) * wide(scale[at, :], width)

    def gather(row, n, owned, carry):
        at = pl.ds(row, n)
        a, b = grad_in[0, at, :].astype(F32), back_gate[at, :]
        keep = keep_flag(positions(info, row, n), bounds, width)
        normed = normed_of(at)
        direct = a * mu + b * nu
        moved = (a + b - direct) * keep
        second = direct + up(moved, carry)
        if owned:
            diff = change[0, at, :].astype(F32)
            acc[0] += fold(second * normed)
            acc[1] += fold(second)
            acc[2] += fold(a * diff)
            acc[3] += fold(b * diff)
        inner = second * gain
        held[at, :] = inner
        part_a[at, :] = lanes(inner)
        part_b[at, :] = lanes(inner * normed)
        return moved[0:1]

    slabs(span, gather, jnp.zeros((1, width), F32), reverse=True)
    part_a[...] = row_mean(part_a, width)
    part_b[...] = row_mean(part_b, width)


    def apply(row, n, owned, carry):
        at = pl.ds(row, n)
        back = wide(scale[at, :], width) * (
            held[at, :] - wide(part_a[at, :], width) - normed_of(at) * wide(part_b[at, :], width)
        )
        live = flag(positions(info, row, n) < total, width)
        grad = cotangent[0, at, :].astype(F32) * live + back
        grad_middle[0, at, :] = grad
        grad_att[0, at, :] = grad.astype(BF)
        return carry

    cotangent = cotangent.ready()
    slabs(span, apply, 0)

    held[...] = nt(grad_att[0], wo[0])
    speed = jnp.exp(par[5:6, :])
    chunks = Chunks(info, bounds, rows, speed)
    size = chunks.size


    def point(row, n, owned, carry):
        at = pl.ds(row, n)
        back = held[at, :]
        num = back * by_num[0, at, :].astype(F32)
        den = num * wkv[0, at, :]
        for i in range(chunks.tiles):
            grad_num[0, i, at, :] = tile(num, i)
            grad_den[0, i, at, :] = -tile(den, i)
        grad_recept[0, at, :] = (back * by_recept[0, at, :].astype(F32)).astype(BF)
        return carry

    by_num, by_recept, wkv = by_num.ready(), by_recept.ready(), wkv.ready()
    slabs(span, point, 0)

    def step(j, carry, cut=False):
        nums, dens = carry
        at = chunks.at(j)
        keep = chunks.keep(j, 1)
        num_out, den_out = [], []
        for i in range(chunks.tiles):
            gn, gd = grad_num[0, i, at, :], grad_den[0, i, at, :]
            if cut:
                gn, gd = jnp.where(chunks.row8 == 7, 0.0, gn), jnp.where(chunks.row8 == 7, 0.0, gd)
            factor = chunks.rate[i] * keep
            num_out.append(factor * nums[i] + gn)
            den_out.append(factor * dens[i] + gd)
        return tuple(num_out), tuple(den_out)

    zero = tuple(jnp.zeros((8, 128), F32) for _ in range(chunks.tiles))
    after = PAD + span + 1 - 7 * size
    carry = (zero, zero)
    for j in reversed(range(after, size)):
        carry = step(j, carry, cut=True)
    carry = steps_of(PAD + 1, after, step, carry, reverse=True)
    inside = [join(c)[0:1] for c in carry]
    carry = steps_of(0, PAD + 1, step, carry, reverse=True, unroll=size)
    whole_ends = [join(c) for c in carry]
    out = []
    for k in range(2):
        ends[0, k] = whole_ends[k]
        line = whole_ends[k][7:8]
        for s in range(6, 0, -1):
            line = whole_ends[k][s : s + 1] + chunks.decay(s * size, (s + 1) * size, size) * line
        out.append(inside[k] + chunks.decay(PAD + 1, size, size - PAD - 1) * line)
    write_state(state, batch, *out)

    @pl.when(batch == pl.num_programs(0) - 1)
    def _():
        sums[...] = jnp.zeros_like(sums)
        for i in range(4):
            sums[i : i + 1, :] = jnp.sum(acc[i], axis=0, keepdims=True)


def recept_kernel(span, plan, info, gated, grad_att, mix_recept, grad_recept, keep, send, total):
    def grad(left, right):
        total[...] = over_own(left, right, span)
        scatter_rows(info, total, keep, send, plan, store_sixteen)

    pl.when(pl.program_id(0) == 0)(lambda: grad(gated, grad_att))
    pl.when(pl.program_id(0) == 1)(lambda: grad(mix_recept, grad_recept))


def again_kernel(span, seqs, ranks, parts, info, exp_key, value, ends, grad_recept, par, whole_a, *refs):
    states, (num_prev, den_prev, back_recept, wr, sems) = refs[:parts], refs[parts:]
    batch = pl.program_id(0)
    bounds = bounds_of(info, batch, seqs)
    chunks = Chunks(info, bounds, grad_recept.shape[1], jnp.exp(par[5:6, :]))

    def copy():
        return pltpu.make_async_copy(whole_a.at[2], wr, sems.at[0])

    pl.when(batch == 0)(lambda: copy().start())

    def emit(at, i, before_num, before_den, ek, x):
        num_prev[0, i, at, :] = before_num
        den_prev[0, i, at, :] = before_den

    forward_scan(info, states, batch, chunks, exp_key, value, ends, span, ranks, emit)
    pl.when(batch == 0)(lambda: copy().wait())
    back_recept[0] = nt(grad_recept[0], wr[...]).astype(BF)


def recur_back_kernel(
    span,
    seqs,
    ranks,
    parts,
    plan,
    info,
    grad_num,
    grad_den,
    exp_key,
    value,
    num_prev,
    den_prev,
    ends,
    mix_key,
    mix_value,
    par,
    *refs,
):
    states, refs = refs[:parts], refs[parts:]
    grad_key, grad_value, keep, send, sums, line_key, line_value, total, acc = refs
    batch = pl.program_id(0)
    bounds = bounds_of(info, batch, seqs)
    rows, width = mix_key.shape[1:]

    @pl.when(batch == 0)
    def _():
        acc[...] = jnp.zeros_like(acc)

    speed = jnp.exp(par[5:6, :])
    chunks = Chunks(info, bounds, rows, speed)
    size = chunks.size
    boost = chunks.split(jnp.exp(par[6:7, :]))
    entering = incoming(info, states, batch, bounds, speed, span, ranks, True)
    after = PAD + span + 1 - 7 * size
    begin = []
    for k in range(2):
        lines = [jnp.zeros((1, width), F32)]
        lines.append(ends[0, k, 7:8, :] + chunks.decay(7 * size, 7 * size + after, after) * entering[k])
        for s in range(6, 0, -1):
            lines.append(ends[0, k, s : s + 1, :] + chunks.decay(s * size, (s + 1) * size, size) * lines[-1])
        begin.append(jnp.concatenate(lines[::-1], axis=0))
    zero = tuple(jnp.zeros((8, 128), F32) for _ in range(chunks.tiles))
    carry = tuple(tuple(tile(b, i) for i in range(chunks.tiles)) for b in begin) + (zero, zero)

    def step(j, carry, insert=None, mask=None):
        nums, dens, bonuses, decays = carry
        at = chunks.at(j)
        keep_next = chunks.keep(j, 1)
        outs = ([], [], [], [])
        for i in range(chunks.tiles):
            gn, ek, v = grad_num[0, i, at, :], exp_key[0, i, at, :], value[0, i, at, :]
            gd = grad_den[0, i, at, :]
            after_num = keep_next * nums[i]
            after_den = keep_next * dens[i]
            bek = boost[i] * ek
            bonus = bek * (v * gn + gd)
            line_key[i, at, :] = bonus + ek * (v * after_num + after_den)
            line_value[i, at, :] = bek * gn + ek * after_num
            decay = num_prev[0, i, at, :] * after_num + den_prev[0, i, at, :] * after_den
            if mask is not None:
                bonus = jnp.where(mask, bonus, 0.0)
                decay = jnp.where(mask, decay, 0.0)
            if insert is not None:
                gn = jnp.where(chunks.row8 == 7, insert[0][i], gn)
                gd = jnp.where(chunks.row8 == 7, insert[1][i], gd)
            outs[0].append(chunks.rate[i] * after_num + gn)
            outs[1].append(chunks.rate[i] * after_den + gd)
            outs[2].append(bonuses[i] + bonus)
            outs[3].append(decays[i] + decay)
        return tuple(tuple(o) for o in outs)

    none = [[0.0] * chunks.tiles] * 2
    upper = chunks.row8 < 7
    for j in reversed(range(after + 1, size)):
        carry = step(j, carry, none, upper)
    carry = step(after, carry, [chunks.split(e) for e in entering], upper)
    edge = PAD + span - 7 * size
    for j in reversed(range(edge, after)):
        carry = step(j, carry, None, upper)
    carry = steps_of(PAD, edge, step, carry, reverse=True)
    lower = chunks.row8 > 0
    carry = steps_of(0, PAD, lambda j, c: step(j, c, None, lower), carry, reverse=True)
    acc[0] += join(carry[2])
    acc[1] += join(carry[3])

    def pack(row, n, owned, carry):
        at = pl.ds(row, n)
        grad_key[batch, at, :] = join([line_key[i, at, :] for i in range(chunks.tiles)]).astype(BF)
        grad_value[batch, at, :] = join([line_value[i, at, :] for i in range(chunks.tiles)]).astype(BF)
        return carry

    slabs(span, pack, 0)
    mix_key.ready(), mix_value.ready()

    @pl.when(batch == pl.num_programs(0) - 1)
    def _():
        sums[...] = jnp.zeros_like(sums)
        for i in range(2):
            sums[i : i + 1, :] = jnp.sum(acc[i], axis=0, keepdims=True)
        for left, right, low in ((mix_key, grad_key, 0), (mix_value, grad_value, width)):
            total[...] = over_own(left.buffer, right, span)

            def write(ref, row, value):
                ref[row : row + 16, low : low + width] = value

            scatter_rows(info, total, keep, send, plan, write)


def first_back_kernel(
    span,
    seqs,
    plan,
    info,
    grad_key,
    grad_value,
    back_recept,
    tokens,
    stats,
    change,
    sums,
    sums_back,
    par,
    whole_a,
    *refs,
):
    inners, part_ref, keep, send, weights, back_key, back_value, acc, turned, sems = refs
    part_a, part_b = part_ref.at[0, 0], part_ref.at[0, 1]
    batch = pl.program_id(0)
    bounds = bounds_of(info, batch, seqs)
    width = tokens.shape[2]

    def copies():
        return [pltpu.make_async_copy(whole_a.at[pl.ds(0, 2)], weights, sems.at[0])]

    @pl.when(batch == 0)
    def _():
        start_all(copies())
        acc[...] = jnp.zeros_like(acc)
        wait_all(copies())

    back_key[...] = nt(grad_key[0], weights[0])
    back_value[...] = nt(grad_value[0], weights[1])
    gain = par[0:1, :]
    mixes = (par[2:3, :], par[3:4, :], par[4:5, :])
    tokens, stats, change = tokens.ready(), stats.ready(), change.ready()
    mean, scale = stats.at[0, 0], stats.at[0, 1]

    def normed_of(at):
        return (tokens[0, at, :].astype(F32) - wide(mean[at, :], width)) * wide(scale[at, :], width)

    def gather(row, n, owned, carry):
        at = pl.ds(row, n)
        parts = (back_key[at, :], back_value[at, :], back_recept[0, at, :].astype(F32))
        keep = keep_flag(positions(info, row, n), bounds, width)
        direct = sum(g * mu for g, mu in zip(parts, mixes))
        moved = (parts[0] + parts[1] + parts[2] - direct) * keep
        if owned:
            normed = normed_of(at)
            first = direct + up(moved, carry)
            diff = change[0, at, :].astype(F32)
            acc[2] += fold(first * normed)
            acc[3] += fold(first)
            for i in range(3):
                acc[4 + i] += fold(parts[i] * diff)
            inner = first * gain
            inners[0, at, :] = inner
            part_a[at, :] = lanes(inner)
            part_b[at, :] = lanes(inner * normed)
        return moved[0:1]

    slabs(span, gather, jnp.zeros((1, width), F32), reverse=True)
    part_a[...] = row_mean(part_a, width)
    part_b[...] = row_mean(part_b, width)

    @pl.when(batch == pl.num_programs(0) - 1)
    def _():
        def final(i):
            return jnp.sum(acc[i], axis=0, keepdims=True)

        speed = jnp.exp(par[5:6, :])
        decay = sums_back[1:2, :] * jnp.exp(-speed) * -speed
        columns = [final(i) for i in (2, 3, 4, 5, 6)] + [decay, sums_back[0:1, :]]
        columns += [sums[i : i + 1, :] for i in range(4)]
        stacked = jnp.concatenate(columns + [jnp.zeros((128 - len(columns), width), F32)], axis=0)
        turned[...] = stacked.T
        scatter_rows(info, turned, keep, send, plan, store_sixteen)


def tokens_grad_kernel(span, info, inners, parts, tokens, stats, grad_middle, tokens_grad):
    width = inners.shape[2]
    mean, scale = stats.at[0, 0], stats.at[0, 1]
    part_a, part_b = parts.at[0, 0], parts.at[0, 1]

    def apply(row, n, owned, carry):
        if owned:
            at = pl.ds(row, n)
            rate = wide(scale[at, :], width)
            normed = (tokens[0, at, :].astype(F32) - wide(mean[at, :], width)) * rate
            back = rate * (inners[0, at, :] - wide(part_a[at, :], width) - normed * wide(part_b[at, :], width))
            tokens_grad[0, 0, pl.ds(row - PAD, n), :] = grad_middle[0, at, :] + back
        return carry

    slabs(span, apply, 0)


def swap(x, kind):
    devices, size = lax.axis_size("dp"), lax.axis_size("seq")
    if kind == "next":
        return lax.ppermute(x, "seq", [(i, i + 1) for i in range(size - 1)])
    if kind == "last":
        return lax.ppermute(x, "seq", [(i + 1, i) for i in range(size - 1)])
    if isinstance(kind, int):
        return lax.ppermute(x, "seq", [(i, i ^ kind) for i in range(size)])
    masks = {"xy": ((1, 0), (2, 0)), "yx": ((2, 0), (1, 0)), "over": ((3, 0), (3, 0)), "near": ((0, 2), (0, 4)), "far": ((0, 4), (0, 2))}
    pairs = []
    for d in range(devices):
        for s in range(size):
            over, along = masks[kind][s % 2]
            pairs.append((d * size + s, (d ^ over) * size + (s ^ along)))
    return lax.ppermute(x, ("dp", "seq"), pairs)


def add(terms):
    return sum(t.astype(F32) for t in terms)


def hold(x, deps):
    return lax.optimization_barrier((x,) + tuple(deps))[0] if deps else x


def launch(deps, *items):
    items = [item for item in items if item.sends()]
    sends = [s for item in items for s in item.sends()]
    if not sends:
        return list(deps)
    held = lax.optimization_barrier(tuple(s[0] for s in sends) + tuple(deps))
    came = [swap(x, kind) for x, (_, kind) in zip(held, sends)]
    left = list(came)
    for item in items:
        count = len(item.sends())
        item.receive(left[:count])
        left = left[count:]
    return came


class Gather:
    def __init__(self, blocks, core):
        self.core = core
        self.next = [(blocks, "xy")]
        self.stage = 0

    def sends(self):
        return self.next

    def receive(self, came):
        if self.stage == 0:
            self.pieces = came
            half = came[0].shape[1] // 2
            part = lax.dynamic_slice_in_dim(came[0], self.core * half, half, axis=1)
            self.next = [(part, "yx"), (came[0], 1)]
        elif self.stage == 1:
            self.pieces = self.pieces + [came[1], came[0]]
            self.next = [(came[0], 1)]
        else:
            self.pieces = self.pieces + came
            self.next = []
        self.stage += 1


class Table:
    def __init__(self, params, kinds):
        self.own = jnp.pad(params.T, ((0, 16 - params.shape[1]), (0, 0)))
        self.kinds = kinds

    def sends(self):
        return [(self.own, kind) for kind in self.kinds]

    def receive(self, came):
        self.came = came

    def whole(self, last):
        d = lax.axis_index("dp")
        first = lax.axis_index("seq") % 2 == 0
        a, b = self.came
        a = [self.own, jnp.where(first, a, b), jnp.where(first, b, a)] + last.came
        a = [jnp.where(d % 2 == 1, a[i ^ 1], a[i]) for i in range(4)]
        a = [jnp.where(d // 2 == 1, a[i ^ 2], a[i]) for i in range(4)]
        return jnp.concatenate(a, axis=1).astype(F32)


class States:
    def __init__(self, state):
        self.parts = [state]
        self.mask = 1

    def sends(self):
        return [(self.parts[0], self.mask)] if self.mask < lax.axis_size("seq") else []

    def receive(self, came):
        self.parts = self.parts + came
        self.mask *= 2
        if self.sends():
            self.parts = [jnp.concatenate(self.parts, axis=0)]


class Halo:
    def __init__(self, tokens, cotangent):
        span = tokens.shape[2]
        toks, cots = tokens[:, 0], cotangent[:, 0]
        self.next = [(toks[:, span - 2 :], "next"), (jnp.stack([toks[:, :2], cots[:, :2]]), "last")]

    def sends(self):
        return self.next

    def receive(self, came):
        before, after = came
        blank = jnp.zeros(after.shape[:2] + (PAD - 2,) + after.shape[3:], BF)
        before = jnp.stack([before, jnp.zeros_like(before)])
        self.rows = jnp.concatenate([blank, before, after, blank], axis=2)


class Core:
    def __init__(self, keep, send, plain):
        self.keep, self.send, self.plain = keep, send, plain

    def sends(self):
        return [] if self.plain else [(self.send, 1)]

    def receive(self, came):
        self.terms = [self.keep, came[0]]

    def whole(self):
        full = jnp.stack([self.keep, self.send], axis=1).reshape(-1, self.keep.shape[-1]).astype(F32)
        return lax.psum_scatter(full, ("dp", "seq"), scatter_dimension=0, tiled=True)


class Quarter:
    def __init__(self, *cores):
        self.cores = cores
        self.rows = cores[0].keep.shape[1]
        self.plain = cores[0].plain
        self.came = []

    def value(self, p, rows=slice(None)):
        return jnp.concatenate([add([t[p, rows] for t in c.terms]) for c in self.cores], axis=-1)

    def sends(self):
        if self.plain or len(self.came) == 2:
            return []
        if not self.came:
            return [(self.value(slice(2, 4)).astype(BF), "xy")]
        return [((self.value(1) + self.came[0][1].astype(F32)).astype(BF), "yx")]

    def receive(self, came):
        self.came += came

    def final(self, low, high):
        rows = slice(low * self.rows // 4, high * self.rows // 4)
        return self.value(0, rows) + self.came[0][0, rows].astype(F32) + self.came[1][rows].astype(F32)

    def second(self, came):
        return came[came.shape[0] // 2 :]


class TallQuarter(Quarter):
    def value(self, p, rows=slice(None)):
        return jnp.concatenate([add([t[p] for t in c.terms]) for c in self.cores], axis=-2)

    def final(self, low, high):
        out, base = [], 0
        for c in self.cores:
            count = c.keep.shape[1]
            rows = slice(low * count // 4, high * count // 4)
            near = slice(base + rows.start, base + rows.stop)
            came = self.came[0][0, near].astype(F32) + self.came[1][near].astype(F32)
            out.append(add([t[0, rows] for t in c.terms]) + came)
            base += count
        return jnp.concatenate(out, axis=0)

    def second(self, came):
        out, base = [], 0
        for c in self.cores:
            count = c.keep.shape[1] // 4
            out.append(came[base + count : base + 2 * count])
            base += 2 * count
        return jnp.concatenate(out, axis=0)

    def first(self, came):
        out, base = [], 0
        for c in self.cores:
            count = c.keep.shape[1] // 4
            out.append(came[base : base + count])
            base += 2 * count
        return jnp.concatenate(out, axis=0)


class SmallQuarter(Quarter):
    def sends(self):
        if self.plain or self.came:
            return []
        return [(self.value(p).astype(BF), kind) for p, kind in ((2, "xy"), (1, "yx"), (3, "over"))]

    def final(self, low, high):
        rows = slice(low * self.rows // 4, high * self.rows // 4)
        return self.value(0, rows) + add([t[rows] for t in self.came])


class Finish:
    def __init__(self, *quarters):
        self.quarters = quarters
        self.plain = quarters[0].plain
        self.came = []
        if self.plain:
            axis = -2 if isinstance(quarters[0], TallQuarter) else -1
            self.total = jnp.concatenate([c.whole() for q in quarters for c in q.cores], axis=axis)

    def value(self, low, high):
        return jnp.concatenate([q.final(low, high) for q in self.quarters], axis=-1)

    def sends(self):
        if self.plain or len(self.came) == 2:
            return []
        if not self.came:
            return [(self.value(2, 4).astype(BF), "near")]
        part = self.quarters[0].second(self.came[0])
        return [((self.value(1, 2) + part.astype(F32)).astype(BF), "far")]

    def receive(self, came):
        self.came += came
        if len(self.came) == 2:
            near = self.came[0]
            first = self.quarters[0]
            near = first.first(near) if isinstance(first, TallQuarter) else near[: near.shape[0] // 2]
            self.total = self.value(0, 1) + near.astype(F32) + self.came[1].astype(F32)


ANY = pl.BlockSpec(memory_space=pl.ANY)
SMEM = pl.BlockSpec(memory_space=pltpu.SMEM)


def shape(s, dtype):
    return jax.ShapeDtypeStruct(s, dtype)


BATCH = "batch"
LATE = "late"
HELD = "held"
VMEM = pl.BlockSpec(memory_space=pltpu.VMEM)


def call(name, kernel, grid, ins, outs, scratch, mib, deps=(), aliases=None, prefetch=False):
    ins = [(hold(ins[0][0], deps), ins[0][1])] + ins[1:]
    views = [i for i, (_, spec) in enumerate(ins + outs) if spec is BATCH]
    lates = [i for i, (_, spec) in enumerate(ins) if spec is LATE]
    extra = [pltpu.VMEM(ins[i][0].shape, ins[i][0].dtype) for i in lates]
    if lates:
        extra.append(pltpu.SemaphoreType.DMA((len(lates), grid[0])))

    def run(*refs):
        refs = list(refs)
        if lates:
            held, sems = refs[-len(extra) : -1], refs[-1]
            refs = refs[: -len(extra)]
            for k, i in enumerate(lates):
                refs[i] = Late(refs[i], held[k], sems, k)

            @pl.when(pl.program_id(0) == 0)
            def _():
                for b in range(grid[0]):
                    for i in lates:
                        refs[i].copy(b).start()

        for i in views:
            refs[i] = refs[i].at[pl.ds(pl.program_id(0), 1)]
        kernel(*refs)

    specs = {id(BATCH): VMEM, id(LATE): ANY, id(HELD): ANY}
    held = (LATE, HELD)
    operands = [pltpu.with_memory_space_constraint(a, pltpu.HBM) if any(s is h for h in held) else a for a, s in ins]
    grid_spec = pltpu.PrefetchScalarGridSpec(
        num_scalar_prefetch=1 if prefetch else 0,
        grid=grid,
        in_specs=[specs.get(id(s), s) for _, s in ins[1 if prefetch else 0 :]],
        out_specs=[specs.get(id(s), s) for _, s in outs],
        scratch_shapes=list(scratch) + extra,
    )
    return pl.pallas_call(
        run,
        grid_spec=grid_spec,
        out_shape=[a for a, _ in outs],
        input_output_aliases=aliases or {},
        compiler_params=pltpu.CompilerParams(vmem_limit_bytes=mib * 2**20),
        name=name,
    )(*operands)


def body(
    tokens,
    cotangent,
    lengths,
    att_key,
    att_value,
    att_recept,
    att_out,
    ffn_key,
    ffn_value,
    ffn_recept,
    params,
):
    batches, _, span, width = tokens.shape
    seqs = lengths.shape[2]
    ff = ffn_key.shape[1]
    tiles = ff // width
    ranks = lax.axis_size("seq")
    rows = span + 2 * PAD
    d, s = lax.axis_index("dp"), lax.axis_index("seq")
    core = s % 2
    at = lax.iota(jnp.int32, HEAD + batches * seqs)
    info = jnp.pad(lengths.reshape(batches * seqs), (HEAD, 0))
    for i, number in enumerate((s * span, d, s, core)):
        info = jnp.where(at == i, number, info)
    shard = att_key.shape[0]
    group_a = Gather(jnp.stack([att_key, att_value, att_recept, att_out]), core)
    group_b = Gather(jnp.stack([ffn_key[:, j * width : (j + 1) * width] for j in range(tiles)]), core)
    group_c = Gather(jnp.concatenate([ffn_value.reshape(-1, shard, width), ffn_recept[None]], axis=0), core)
    table, last_table = Table(params, ("xy", "yx")), Table(params, ("over",))

    edge = Halo(tokens, cotangent)
    came = launch((), group_a) + launch([info], edge, table)
    over = launch([info], last_table)
    halo = edge.rows
    par = table.whole(last_table)

    ext = (batches, rows, width)
    ext_f, ext_b = shape(ext, F32), shape(ext, BF)
    line_f = shape((batches, width // 128, rows, 128), F32)
    stats_shape = shape((batches, 2, rows, 128), F32)
    ends_shape = shape((batches, 2, 8, width), F32)
    wide_b = shape((batches, rows, ff), BF)
    square = pltpu.VMEM((1, width, width), BF)
    three = pltpu.VMEM((3, width, width), BF)
    square_f = pltpu.VMEM((width, width), F32)
    block_f = pltpu.VMEM((rows, width), F32)
    block_line = pltpu.VMEM((width // 128, rows, 128), F32)
    part = pltpu.VMEM((rows, 128), F32)

    def sems(n):
        return pltpu.SemaphoreType.DMA((n,))

    def refs(group):
        return [(p, ANY) for p in group.pieces]

    info_in = (info, SMEM)

    deps = launch(came, group_a)
    far = launch(deps + over, group_b)
    near = launch(deps, group_a)
    mix_key, mix_value, mix_recept, change_one, tok_ext, cot_ext, stats_one = call(
        "mix",
        functools.partial(mix_kernel, span, seqs),
        (batches,),
        [
            info_in,
            (tokens, pl.BlockSpec((1,) + tokens.shape[1:], lambda i: (i, 0, 0, 0))),
            (cotangent, pl.BlockSpec((1,) + tokens.shape[1:], lambda i: (i, 0, 0, 0))),
            (halo, pl.BlockSpec((2, 1, 2 * PAD, width), lambda i: (0, i, 0, 0))),
            (par, VMEM),
        ],
        [(ext_b, BATCH)] * 6 + [(stats_shape, BATCH)],
        [block_f],
        13,
        deps,
    )
    deps = near
    state_shape = shape((2 * batches, width), F32)
    exp_key, value, gate_one, ends, state, whole_a = call(
        "project",
        functools.partial(project_kernel, span, seqs),
        (batches,),
        [info_in]
        + [(a, BATCH) for a in (mix_key, mix_value, mix_recept)]
        + [(par, VMEM), (att_key, ANY), (att_value, ANY), (att_recept, ANY)]
        + refs(group_a),
        [(line_f, BATCH)] * 3
        + [(ends_shape, BATCH), (state_shape, VMEM), (pltpu.HBM((3, width, width), BF), ANY)],
        [three, sems(PER + 3)],
        10,
        deps,
    )
    exchange = States(state)
    came = launch([state], exchange)
    far = launch(far + came, group_b)
    came = launch(came, exchange)
    deps = came + far
    far = launch(deps, group_b)
    after = launch(deps, group_c)
    while exchange.sends():
        came = launch(came, exchange)
    states = exchange.parts
    deps = came + far
    came = after
    gated, by_num, by_recept, wkv, middle, ffn_in, ffn_gate_in, change_two, stats_two, whole_out = call(
        "recur",
        functools.partial(recur_kernel, span, seqs, ranks, len(states)),
        (batches,),
        [info_in]
        + [(a, BATCH) for a in (exp_key, value, gate_one)]
        + [(ends, BATCH), (tok_ext, BATCH)]
        + [(par, VMEM), (att_out, ANY)]
        + [(a, VMEM) for a in states]
        + refs(group_a),
        [
            (a, BATCH)
            for a in (ext_b, ext_b, ext_b, ext_f, ext_f, ext_b, ext_b, ext_b, stats_shape)
        ]
        + [(pltpu.HBM((1, width, width), BF), ANY)],
        [square, block_line, block_line, sems(PER + 1)],
        10,
        deps,
    )
    deps = came + [stats_two]
    came = launch(deps, group_c)
    key_buf = pltpu.VMEM((tiles, width, width), BF)
    own_value = ffn_value.reshape(4, shard, width)
    hidden, whole_key = call(
        "hidden",
        hidden_kernel,
        (batches,),
        [info_in, (ffn_in, BATCH), (ffn_key, ANY)] + refs(group_b),
        [(wide_b, BATCH), (pltpu.HBM((tiles, width, width), BF), ANY)],
        [key_buf, sems(tiles + PER + 1)],
        11,
        deps,
    )
    came = launch(came + [hidden], group_c)
    mixed_shape = shape((batches, 1, span, width), BF)
    value_buf = pltpu.VMEM((4 * tiles, shard, width), BF)
    mixed, grad_carried, grad_gate, whole_value, whole_gate = call(
        "gate",
        functools.partial(gate_kernel, span, seqs),
        (batches,),
        [info_in]
        + [(a, BATCH) for a in (hidden, ffn_gate_in, middle, cot_ext)]
        + [(own_value, ANY), (ffn_recept, ANY)]
        + refs(group_c),
        [(mixed_shape, BATCH)]
        + [(ext_b, BATCH)] * 2
        + [(pltpu.HBM(value_buf.shape, BF), ANY), (pltpu.HBM((1, width, width), BF), ANY)],
        [value_buf, square, sems(2 * PER + 2)],
        17,
        came,
    )

    plain = ranks != 8 or (width // (4 * ranks)) % 8 != 0
    nz = 1 if plain else 4
    plan = (nz, plain)

    def core_of(keep, send):
        return Core(*(a.reshape(4, -1, a.shape[-1]) for a in (keep, send)), plain)

    big = pltpu.HBM((4, nz, ff // (8 * nz), width), BF)
    big_kept = shape(big.shape, BF)

    def place_of(other):
        def index(i, info):
            core = (info[3] + other) % 2
            return (i if plain else turn(core, i), 0, 0, 0)

        return pl.BlockSpec((1,) + big.shape[1:], index)

    keep_v, send_v = call(
        "value_grad",
        functools.partial(value_grad_kernel, span, plan),
        (4,),
        [info_in, (hidden, VMEM), (grad_carried, VMEM)],
        [(big_kept, place_of(0)), (big, place_of(1))],
        [square_f],
        10,
        prefetch=True,
    )
    core_value = core_of(keep_v, send_v)
    deps = [keep_v]
    came = launch(deps, core_value)
    wide_half = pltpu.HBM((width // 2, ff), BF)
    wide_kept = shape(wide_half.shape, BF)
    one = pltpu.HBM((width // 2, width), BF)
    one_kept = shape(one.shape, BF)
    keep_g, send_g = call(
        "gate_back",
        functools.partial(gate_back_kernel, span, plan),
        (1,),
        [info_in, (ffn_gate_in, VMEM), (grad_gate, VMEM)],
        [(one_kept, VMEM), (one, VMEM)],
        [square_f],
        10,
        deps,
    )
    core_gate = core_of(keep_g, send_g)
    deps = came + launch([keep_g], core_gate)
    sum_value = TallQuarter(core_value, core_gate)
    came = launch(deps, sum_value)
    out_tile = pl.BlockSpec((width // 2, width), lambda i: (0, i))
    keep_k, send_k, _, grad_in = call(
        "inner",
        functools.partial(inner_kernel, span, plan),
        (tiles,),
        [
            info_in,
            (hidden, VMEM),
            (grad_carried, VMEM),
            (ffn_in, VMEM),
            (whole_key.reshape(value_buf.shape), HELD),
            (whole_value, HELD),
        ],
        [(wide_kept, out_tile), (wide_half, out_tile)] + [(pltpu.VMEM(wide_b.shape, BF), VMEM), (ext_b, VMEM)],
        [
            value_buf,
            square_f,
            sems(tiles + 1),
        ],
        20,
        deps,
        {1: 2},
    )
    core_key = core_of(keep_k, send_k)
    deps = came + [grad_in]
    came = launch(deps, sum_value, core_key)
    sums_shape = shape((8, width), F32)
    grad_middle, grad_att, grad_recept, grad_num, grad_den, ends_back, state_back, sums = call(
        "attend_back",
        functools.partial(attend_back_kernel, span, seqs),
        (batches,),
        [info_in]
        + [
            (a, LATE if a is cot_ext or a is by_num or a is by_recept or a is wkv else BATCH)
            for a in (
                grad_gate,
                grad_in,
                change_two,
                middle,
                stats_two,
                cot_ext,
                by_num,
                by_recept,
                wkv,
            )
        ]
        + [(par, VMEM), (whole_out, VMEM), (whole_gate, VMEM)],
        [(a, BATCH) for a in (ext_f, ext_b, ext_b, pltpu.VMEM(line_f.shape, F32), pltpu.VMEM(line_f.shape, F32))]
        + [(ends_shape, BATCH)]
        + [(state_shape, VMEM), (sums_shape, VMEM)],
        [pltpu.VMEM((4, 8, width), F32), block_f, block_f, part, part],
        18,
        deps,
    )
    exchange = States(state_back)
    sum_key = Quarter(core_key)
    all_value = Finish(sum_value)
    came = launch(came + [state_back], exchange)
    deps = came
    came = launch(came, exchange, sum_key)
    came, far = came[:1], came[1:]
    two = pltpu.HBM((width // 2, 2 * width), BF)
    two_kept = shape(two.shape, BF)
    keep_o, send_o = call(
        "recept",
        functools.partial(recept_kernel, span, plan),
        (2,),
        [info_in] + [(a, VMEM) for a in (gated, grad_att, mix_recept, grad_recept)],
        [(a, pl.BlockSpec((width // 2, width), lambda i: (0, i))) for a in (two_kept, two)],
        [square_f],
        10,
        deps,
    )
    core_out = core_of(keep_o, send_o)
    deps = came + [keep_o]
    came = launch(deps, exchange)
    num_prev, den_prev, back_recept = call(
        "again",
        functools.partial(again_kernel, span, seqs, ranks, len(states)),
        (batches,),
        [info_in]
        + [(a, BATCH) for a in (exp_key, value, ends, grad_recept)]
        + [(par, VMEM), (whole_a, HELD)]
        + [(a, VMEM) for a in states],
        [(line_f, BATCH)] * 2 + [(ext_b, BATCH)],
        [pltpu.VMEM((width, width), BF), sems(1)],
        8,
        deps,
    )
    while exchange.sends():
        came = launch(came, exchange)
    states_back = exchange.parts
    deps = came + far + [back_recept]
    came = launch(deps, all_value, sum_key, core_out)
    grad_key, grad_value, keep_l, send_l, sums_back = call(
        "recur_back",
        functools.partial(recur_back_kernel, span, seqs, ranks, len(states_back), plan),
        (batches,),
        [info_in]
        + [
            (a, LATE if a is mix_key or a is mix_value else BATCH)
            for a in (
                grad_num,
                grad_den,
                exp_key,
                value,
                num_prev,
                den_prev,
                ends_back,
                mix_key,
                mix_value,
            )
        ]
        + [(par, VMEM)]
        + [(a, VMEM) for a in states_back],
        [(ext_b, VMEM)] * 2 + [(two_kept, VMEM), (two, VMEM)] + [(sums_shape, VMEM)],
        [block_line, block_line, square_f, pltpu.VMEM((2, 8, width), F32)],
        18,
        deps,
    )
    core_last = core_of(keep_l, send_l)
    deps = launch(came + [sums_back], core_last)
    all_key = Finish(sum_key)
    sum_last = Quarter(core_last, core_out)
    came = launch(deps, all_key, sum_last, all_value)
    grad_shape = shape((batches, 1, span, width), F32)
    half_table = shape((width // 2, 128), BF)
    inners, parts, keep_p, send_p = call(
        "first_back",
        functools.partial(first_back_kernel, span, seqs, plan),
        (batches,),
        [info_in]
        + [(a, BATCH) for a in (grad_key, grad_value, back_recept)]
        + [(a, LATE) for a in (tok_ext, stats_one, change_one)]
        + [(sums, VMEM), (sums_back, VMEM), (par, VMEM)]
        + [(whole_a, HELD)],
        [(ext_f, BATCH), (stats_shape, BATCH)] + [(half_table, VMEM)] * 2,
        [
            pltpu.VMEM((2, width, width), BF),
            block_f,
            block_f,
            pltpu.VMEM((7, 8, width), F32),
            pltpu.VMEM((width, 128), F32),
            sems(1),
        ],
        18,
        deps,
    )
    core_table = core_of(keep_p, send_p)
    deps = launch(came + [keep_p], core_table)
    sum_table = SmallQuarter(core_table)
    came = launch(deps, sum_last, sum_table, all_key)
    (tokens_grad,) = call(
        "tokens_grad",
        functools.partial(tokens_grad_kernel, span),
        (batches,),
        [info_in] + [(a, BATCH) for a in (inners, parts, tok_ext, stats_one, grad_middle)],
        [(grad_shape, BATCH)],
        [],
        7,
        deps,
    )
    all_last = Finish(sum_last, sum_table)
    came = launch(came + [tokens_grad], all_last)
    launch(came, all_last)
    key, last = all_key.total, all_last.total
    cut = ff // (4 * ranks)
    return (
        mixed,
        tokens_grad,
        last[:, :width],
        last[:, width : 2 * width],
        last[:, 3 * width : 4 * width],
        last[:, 2 * width : 3 * width],
        key,
        all_value.total[:cut],
        all_value.total[cut:],
        last[:, 4 * width : 4 * width + params.shape[1]],
    )


def solution(mesh):
    split = P(("dp", "seq"), None)
    rows = P("dp", None)
    stream = P(None, "dp", "seq", None)
    return jax.shard_map(
        body,
        mesh=mesh,
        in_specs=(stream, stream, P(None, "dp", None)) + (rows,) * 8,
        out_specs=(stream, stream) + (split,) * 8,
        check_vma=False,
    )
```

```python
import functools

import jax
import jax.numpy as jnp
from jax import lax
from jax.experimental import pallas as pl
from jax.experimental.pallas import tpu as pltpu
from jax.sharding import PartitionSpec as P

EPS = 1e-05
BF = jnp.bfloat16
F32 = jnp.float32
PAD = 16
FAR = 1 << 30
PER = 5
HEAD = 4


def bounds_of(info, batch, seqs):
    ends = [jnp.int32(0)]
    for i in range(seqs):
        ends.append(ends[-1] + info[HEAD + batch * seqs + i])
    return ends


def positions(info, row, count):
    return lax.broadcasted_iota(jnp.int32, (count, 128), 0) + (row - PAD + info[0])


def since_start(pos, bounds):
    best = jnp.full(pos.shape, FAR, jnp.int32)
    for b in bounds:
        best = jnp.where(pos >= b, jnp.minimum(best, pos - b), best)
    return best


def until_start(pos, bounds):
    best = jnp.full(pos.shape, FAR, jnp.int32)
    for b in bounds:
        best = jnp.where(pos < b, jnp.minimum(best, b - pos), best)
    return best


def wide(mask, width):
    return jnp.concatenate([mask] * (width // 128), axis=1)


def flag(cond, width):
    return wide(jnp.where(cond, 1.0, 0.0).astype(F32), width)


def keep_flag(pos, bounds, width):
    hit = pos == bounds[0]
    for b in bounds[1:]:
        hit = hit | (pos == b)
    return wide(jnp.where(hit, 0.0, 1.0).astype(F32), width)


def rows_of(count, width):
    return wide(lax.broadcasted_iota(jnp.int32, (count, 128), 0), width)


def down(x, carry):
    rolled = pltpu.roll(x, 1, 0)
    return jnp.where(rows_of(*x.shape) == 0, carry, rolled)


def up(x, carry):
    n = x.shape[0]
    rolled = pltpu.roll(x, n - 1, 0)
    return jnp.where(rows_of(*x.shape) == n - 1, carry, rolled)


def nn(a, b):
    return jnp.dot(a, b, preferred_element_type=F32)


def nt(a, b):
    return lax.dot_general(a, b, (((1,), (1,)), ((), ())), preferred_element_type=F32)


def tn(a, b):
    return lax.dot_general(a, b, (((0,), (0,)), ((), ())), preferred_element_type=F32)


def slabs(span, body, init, reverse=False, unroll=4):
    step = 32
    many = span // step

    def one(i, carry):
        at = many - 1 - i if reverse else i
        return body(pl.multiple_of(PAD + at * step, PAD), step, True, carry)

    first, last = (PAD + span, 0) if reverse else (0, PAD + span)
    carry = body(first, PAD, False, init)
    carry = lax.fori_loop(0, many, one, carry, unroll=unroll)
    return body(last, PAD, False, carry)


def lanes(x):
    return sum(x[:, i : i + 128] for i in range(0, x.shape[1], 128))


def tile(x, i):
    return x[:, i * 128 : (i + 1) * 128]


def row_mean(ref, width):
    total = jnp.sum(ref[...], axis=1, keepdims=True) * (1.0 / width)
    return jnp.broadcast_to(total, ref.shape)


def steps_of(low, high, body, carry, reverse=False, unroll=4):
    def one(i, carry):
        return body(high - 1 - i if reverse else low + i, carry)

    count = high - low
    while count % unroll:
        unroll -= 1
    return lax.fori_loop(0, count, one, carry, unroll=unroll)


def fold(x):
    n, c = x.shape
    return jnp.sum(x.reshape(n // 8, 8, c), axis=0)


def no_start(bounds, low, high):
    hit = jnp.int32(0)
    for b in bounds:
        hit = hit | jnp.where((b > low) & (b <= high), 1, 0)
    return jnp.where(hit == 0, 1.0, 0.0).astype(F32)


def incoming(info, states, batch, bounds, speed, span, ranks, reverse):
    me, base = info[2], info[0]
    num = jnp.zeros(speed.shape, F32)
    den = jnp.zeros(speed.shape, F32)
    for k in range(1, ranks):
        other = me ^ k
        if reverse:
            gap = other - me - 1
            clear = no_start(bounds, base + span + 1, other * span + 1)
        else:
            gap = me - 1 - other
            clear = no_start(bounds, (other + 1) * span - 2, base - 2)
        use = jnp.where(gap >= 0, clear, 0.0).astype(F32)
        weight = jnp.exp(-speed * (jnp.maximum(gap, 0) * span).astype(F32)) * use
        per = sum(r.shape[0] for r in states) // ranks
        many = states[0].shape[0] // per
        at = (k % many) * per + 2 * batch
        num += weight * states[k // many][pl.ds(at, 1), :]
        den += weight * states[k // many][pl.ds(at + 1, 1), :]
    return num, den


def start_all(copies):
    for c in copies:
        c.start()


def wait_all(copies):
    for c in copies:
        c.wait()


def copies_of(info, owns, pieces, blocks, target, sems, at=0):
    d, c = info[1], info[3]
    shard = owns[0].shape[0]
    half = shard // 2
    out = []
    for k, own in enumerate(owns):
        out.append(pltpu.make_async_copy(own, target.at[k, pl.ds(pl.multiple_of(d * shard, 16), shard)], sems.at[at]))
        at += 1
    places = ((d ^ (1 + c)) * shard, (d ^ (2 - c)) * shard, (d ^ 3) * shard + c * half, (d ^ 3) * shard + (1 - c) * half)
    for row, ref in zip(places, pieces):
        source = ref.at[blocks]
        place = target.at[:, pl.ds(pl.multiple_of(row, 16), source.shape[1])]
        out.append(pltpu.make_async_copy(source, place, sems.at[at]))
        at += 1
    return out


def value_copies(info, own, pieces, target, sems, at=0):
    d, c = info[1], info[3]
    half = target.shape[1] // 2
    out = [pltpu.make_async_copy(own, target.at[pl.ds(4 * d, 4)], sems.at[at])]
    places = ((d ^ (1 + c), 0), (d ^ (2 - c), 0), (d ^ 3, c * half), (d ^ 3, (1 - c) * half))
    for (block, row), ref in zip(places, pieces):
        at += 1
        place = target.at[pl.ds(4 * block, 4), pl.ds(pl.multiple_of(row, 16), ref.shape[1])]
        out.append(pltpu.make_async_copy(ref.at[pl.ds(0, 4)], place, sems.at[at]))
    return out


def place(info, plain):
    if plain:
        return 0, 0, 0
    return info[1], info[2] // 2, info[3]


def turn(core, i):
    return core * i + (1 - core) * (((i & 1) << 1) | (i >> 1))


def scatter_rows(info, src, keep, send, plan, write):
    nz, plain = plan
    d, z, c = place(info, plain)
    block = src.shape[0] // (8 * nz)
    per = 4 * nz * block // 16
    groups = block // 8
    for ref, core in ((keep, c), (send, 1 - c)):
        for slab in range(per):
            parts = []
            for g in (2 * slab, 2 * slab + 1):
                i = g % groups
                q = (g // groups) % nz
                p = g // (groups * nz)
                if not plain:
                    p, q = turn(core, p), turn(core, q)
                row = ((d ^ p) * nz + (z ^ q)) * (2 * block) + core * block + i * 8
                parts.append(src[pl.ds(pl.multiple_of(row, 8), 8), :])
            write(ref, slab * 16, jnp.concatenate(parts, axis=0).astype(BF))


def keep_whole(batch, buffer, target, sem):
    def copy():
        return pltpu.make_async_copy(buffer, target, sem)

    pl.when(batch == 0)(lambda: copy().start())
    pl.when(batch == pl.num_programs(0) - 1)(lambda: copy().wait())


class Late:
    def __init__(self, source, buffer, sems, index):
        self.source, self.buffer, self.sems, self.index = source, buffer, sems, index
        self.shape = (1,) + tuple(buffer.shape[1:])

    def copy(self, b):
        return pltpu.make_async_copy(self.source.at[b], self.buffer.at[b], self.sems.at[self.index, b])

    def ready(self):
        b = pl.program_id(0)
        self.copy(b).wait()
        return self.buffer.at[pl.ds(b, 1)]


def mix_kernel(
    span, seqs, info, tokens, cotangent, halo, par, mix_key, mix_value, mix_recept, change, tok_ext, cot_ext, stats, held
):
    batch = pl.program_id(0)
    bounds = bounds_of(info, batch, seqs)
    gain, bias = par[0:1, :], par[1:2, :]
    mixes = (par[2:3, :], par[3:4, :], par[4:5, :])
    width = tokens.shape[3]
    mean, scale = stats.at[0, 0], stats.at[0, 1]

    def load(row, n, owned, carry):
        at = pl.ds(row, n)
        if owned:
            x, g = tokens[0, 0, pl.ds(row - PAD, n), :], cotangent[0, 0, pl.ds(row - PAD, n), :]
        else:
            low = 0 if row == 0 else PAD
            x, g = halo[0, 0, low : low + PAD, :], halo[1, 0, low : low + PAD, :]
        tok_ext[0, at, :] = x
        cot_ext[0, at, :] = g
        x = x.astype(F32)
        held[at, :] = x
        mean[at, :] = lanes(x)
        return carry

    slabs(span, load, 0)
    mean[...] = row_mean(mean, width)

    def spread(row, n, owned, carry):
        at = pl.ds(row, n)
        x = held[at, :] - wide(mean[at, :], width)
        scale[at, :] = lanes(x * x)
        return carry

    slabs(span, spread, 0)
    scale[...] = lax.rsqrt(row_mean(scale, width) + EPS)

    def body(row, n, owned, carry):
        at = pl.ds(row, n)
        normed = (held[at, :] - wide(mean[at, :], width)) * wide(scale[at, :], width)
        first = normed * gain + bias
        keep = keep_flag(positions(info, row, n), bounds, width)
        shifted = down(first, carry) * keep
        diff = first - shifted
        for mu, ref in zip(mixes, (mix_key, mix_value, mix_recept)):
            ref[0, at, :] = (shifted + diff * mu).astype(BF)
        change[0, at, :] = diff.astype(BF)
        return first[n - 1 : n]

    slabs(span, body, jnp.zeros((1, width), F32))


class Chunks:
    def __init__(self, info, bounds, rows, speed):
        self.size = rows // 8
        self.bounds = bounds
        self.base = info[0] - PAD
        self.row8 = lax.broadcasted_iota(jnp.int32, (8, 128), 0)
        self.start = self.row8 * self.size + self.base
        self.speed = speed
        self.tiles = speed.shape[1] // 128
        self.rate = self.split(jnp.exp(-speed))

    def split(self, row):
        return [jnp.broadcast_to(tile(row, i), (8, 128)) for i in range(self.tiles)]

    def at(self, j):
        return pl.ds(j, 8, stride=self.size)

    def keep(self, j, ahead=0):
        pos = self.start + (j + ahead)
        hit = pos == self.bounds[0]
        for b in self.bounds[1:]:
            hit = hit | (pos == b)
        return jnp.where(hit, 0.0, 1.0).astype(F32)

    def decay(self, low, high, count):
        clear = no_start(self.bounds, self.base + low, self.base + high)
        return jnp.exp(-self.speed * float(count)) * clear


def join(tiles):
    return jnp.concatenate(tiles, axis=1)


def write_state(state, batch, num, den):
    for i in range(state.shape[0] // 2):

        @pl.when(batch == i)
        def _():
            state[2 * i : 2 * i + 1, :] = num
            state[2 * i + 1 : 2 * i + 2, :] = den


def project_kernel(
    span, seqs, info, mix_key, mix_value, mix_recept, par, own_key, own_value, own_recept, *refs
):
    pieces = refs[0:4]
    exp_key, value, gate, ends, state, kept, weights, sems = refs[4:]
    batch = pl.program_id(0)
    bounds = bounds_of(info, batch, seqs)
    rows, width = mix_key.shape[1:]

    def copies():
        return copies_of(info, (own_key, own_value, own_recept), pieces, pl.ds(0, 3), weights, sems)

    @pl.when(batch == 0)
    def _():
        start_all(copies())
        wait_all(copies())

    acts = (jnp.exp, lambda x: x, jax.nn.sigmoid)
    for k, (left, ref, act) in enumerate(zip((mix_key, mix_value, mix_recept), (exp_key, value, gate), acts)):
        part = act(nn(left[0], weights[k]))
        for i in range(width // 128):
            ref[0, i] = tile(part, i)

    speed = jnp.exp(par[5:6, :])
    chunks = Chunks(info, bounds, rows, speed)
    size = chunks.size

    def step(j, carry, cut=False):
        nums, dens = carry
        at = chunks.at(j)
        keep = chunks.keep(j)
        num_out, den_out = [], []
        for i in range(chunks.tiles):
            ek = exp_key[0, i, at, :]
            if cut:
                ek = jnp.where(chunks.row8 == 0, 0.0, ek)
            factor = chunks.rate[i] * keep
            num_out.append(factor * nums[i] + ek * value[0, i, at, :])
            den_out.append(factor * dens[i] + ek)
        return tuple(num_out), tuple(den_out)

    zero = tuple(jnp.zeros((8, 128), F32) for _ in range(chunks.tiles))
    last = PAD + span - 2 - 7 * size
    carry = (zero, zero)
    for j in range(PAD - 1):
        carry = step(j, carry, cut=True)
    carry = steps_of(PAD - 1, last + 1, step, carry)
    inside = [join(c)[7:8] for c in carry]
    carry = steps_of(last + 1, size, step, carry, unroll=size)
    whole_ends = [join(c) for c in carry]
    out = []
    for k in range(2):
        ends[0, k] = whole_ends[k]
        total = whole_ends[k][0:1]
        for s in range(1, 7):
            total = whole_ends[k][s : s + 1] + chunks.decay(s * size - 1, (s + 1) * size - 1, size) * total
        out.append(inside[k] + chunks.decay(7 * size - 1, 7 * size + last, last + 1) * total)
    write_state(state, batch, *out)
    keep_whole(batch, weights, kept, sems.at[PER + 2])


def forward_scan(info, states, batch, chunks, exp_key, value, ends, span, ranks, emit):
    size, width = chunks.size, chunks.speed.shape[1]
    entering = incoming(info, states, batch, chunks.bounds, chunks.speed, span, ranks, False)
    begin = []
    for k in range(2):
        lines = [jnp.zeros((1, width), F32)]
        lines.append(ends[0, k, 0:1, :] + chunks.decay(PAD - 2, size - 1, size - PAD + 1) * entering[k])
        for s in range(1, 7):
            lines.append(ends[0, k, s : s + 1, :] + chunks.decay(s * size - 1, (s + 1) * size - 1, size) * lines[-1])
        begin.append(jnp.concatenate(lines, axis=0))
    carry = tuple(tuple(tile(b, i) for i in range(chunks.tiles)) for b in begin)

    def step(j, carry, insert=None):
        nums, dens = carry
        at = chunks.at(j)
        keep = chunks.keep(j)
        num_out, den_out = [], []
        for i in range(chunks.tiles):
            ek, v = exp_key[0, i, at, :], value[0, i, at, :]
            before_num = keep * nums[i]
            before_den = keep * dens[i]
            x, y = ek * v, ek
            emit(at, i, before_num, before_den, ek, x)
            if insert is not None:
                x = jnp.where(chunks.row8 == 0, insert[0][i], x)
                y = jnp.where(chunks.row8 == 0, insert[1][i], y)
            num_out.append(chunks.rate[i] * before_num + x)
            den_out.append(chunks.rate[i] * before_den + y)
        return tuple(num_out), tuple(den_out)

    none = [[0.0] * chunks.tiles] * 2
    for j in range(PAD - 2):
        carry = step(j, carry, none)
    carry = step(PAD - 2, carry, [chunks.split(e) for e in entering])
    steps_of(PAD - 1, size, step, carry)


def recur_kernel(span, seqs, ranks, parts, info, exp_key, value, gate, ends, tokens, par, own_out, *refs):
    states, refs = refs[:parts], refs[parts:]
    pieces = refs[0:4]
    (
        gated,
        by_num,
        by_recept,
        wkv,
        middle,
        ffn_in,
        ffn_gate_in,
        change,
        stats,
        kept,
        wo,
        line_wkv,
        line_inverse,
        sems,
    ) = refs[4:]
    batch = pl.program_id(0)
    bounds = bounds_of(info, batch, seqs)
    rows, width = tokens.shape[1:]

    def copies():
        return copies_of(info, (own_out,), pieces, pl.ds(3, 1), wo, sems)

    @pl.when(batch == 0)
    def _():
        start_all(copies())

    chunks = Chunks(info, bounds, rows, jnp.exp(par[5:6, :]))
    boost = chunks.split(jnp.exp(par[6:7, :]))

    def emit(at, i, before_num, before_den, ek, x):
        inverse = 1.0 / (before_den + boost[i] * ek)
        line_inverse[i, at, :] = inverse
        line_wkv[i, at, :] = (before_num + boost[i] * x) * inverse

    forward_scan(info, states, batch, chunks, exp_key, value, ends, span, ranks, emit)

    def pack(row, n, owned, carry):
        at = pl.ds(row, n)
        out = ([], [], [], [])
        for i in range(chunks.tiles):
            w, sig = line_wkv[i, at, :], gate[0, i, at, :]
            g = w * sig
            out[0].append(g)
            out[1].append(sig * line_inverse[i, at, :])
            out[2].append(g * (1.0 - sig))
            out[3].append(w)
        for ref, tiles in zip((gated, by_num, by_recept, wkv), out):
            ref[0, at, :] = join(tiles).astype(ref.dtype)
        return carry

    slabs(span, pack, 0)

    @pl.when(batch == 0)
    def _():
        wait_all(copies())

    middle[0] = nn(gated[0], wo[0])
    gain, bias = par[7:8, :], par[8:9, :]
    mean, scale = stats.at[0, 0], stats.at[0, 1]

    def residual(row, n, owned, carry):
        at = pl.ds(row, n)
        mid = middle[0, at, :] + tokens[0, at, :].astype(F32)
        middle[0, at, :] = mid
        mean[at, :] = lanes(mid)
        return carry

    slabs(span, residual, 0)
    mean[...] = row_mean(mean, width)

    def spread(row, n, owned, carry):
        at = pl.ds(row, n)
        x = middle[0, at, :] - wide(mean[at, :], width)
        scale[at, :] = lanes(x * x)
        return carry

    slabs(span, spread, 0)
    scale[...] = lax.rsqrt(row_mean(scale, width) + EPS)

    def body(row, n, owned, carry):
        at = pl.ds(row, n)
        normed = (middle[0, at, :] - wide(mean[at, :], width)) * wide(scale[at, :], width)
        second = normed * gain + bias
        keep = keep_flag(positions(info, row, n), bounds, width)
        shifted = down(second, carry) * keep
        diff = second - shifted
        ffn_in[0, at, :] = (shifted + diff * par[9:10, :]).astype(BF)
        ffn_gate_in[0, at, :] = (shifted + diff * par[10:11, :]).astype(BF)
        change[0, at, :] = diff.astype(BF)
        return second[n - 1 : n]

    slabs(span, body, jnp.zeros((1, width), F32))
    keep_whole(batch, wo, kept, sems.at[PER])


def hidden_kernel(info, ffn_in, own_key, *refs):
    pieces = refs[0:4]
    hidden, kept, wk, sems = refs[4:]
    width = ffn_in.shape[2]
    tiles = wk.shape[0]

    def copies():
        owns = [own_key.at[:, pl.ds(j * width, width)] for j in range(tiles)]
        return copies_of(info, owns, pieces, pl.ds(0, tiles), wk, sems)

    @pl.when(pl.program_id(0) == 0)
    def _():
        start_all(copies())
        wait_all(copies())

    for j in range(tiles):
        relu = jnp.maximum(nn(ffn_in[0], wk[j]), 0.0)
        hidden[0, :, pl.ds(j * width, width)] = (relu * relu).astype(BF)
    keep_whole(pl.program_id(0), wk, kept, sems.at[tiles + PER])


def gate_kernel(
    span, seqs, info, hidden, ffn_gate_in, middle, cotangent, own_value, own_recept, *refs
):
    pieces = refs[0:4]
    mixed, grad_carried, grad_gate, kept, kept_gate, wv, wr, sems = refs[4:]
    batch = pl.program_id(0)
    bounds = bounds_of(info, batch, seqs)
    rows, width = middle.shape[1:]

    def copies():
        return (
            copies_of(info, (own_recept,), pieces, pl.ds(4, 1), wr, sems),
            value_copies(info, own_value, pieces, wv, sems, PER),
        )

    @pl.when(batch == 0)
    def _():
        for c in copies():
            start_all(c)
        wait_all(copies()[0])

    step = rows // 2
    gates = [nn(ffn_gate_in[0, low : low + step, :], wr[0]) for low in range(0, rows, step)]

    @pl.when(batch == 0)
    def _():
        wait_all(copies()[1])

    keep_whole(batch, wv, kept, sems.at[2 * PER])
    keep_whole(batch, wr, kept_gate, sems.at[2 * PER + 1])
    flat = wv[...].reshape(wv.shape[0] * wv.shape[1], width)
    total = bounds[-1]
    for low in range(0, rows, step):
        gate = gates[low // step]
        carried = nn(hidden[0, low : low + step, :], flat)
        for i in range(0, step, PAD):
            row = low + i
            at = pl.ds(row, PAD)
            sig = jax.nn.sigmoid(gate[i : i + PAD])
            car = carried[i : i + PAD]
            live = flag(positions(info, row, PAD) < total, width)
            grad = cotangent[0, at, :].astype(F32) * live
            if PAD <= row < PAD + span:
                mixed[0, 0, row - PAD : row, :] = (middle[0, at, :] + sig * car).astype(BF)
            part = grad * sig
            grad_carried[0, at, :] = part.astype(BF)
            grad_gate[0, at, :] = (part * car * (1.0 - sig)).astype(BF)


def over_own(left, right, span):
    own = pl.ds(PAD, span)
    both = [jnp.concatenate([f[b, own] for b in range(f.shape[0])], axis=0) for f in (left, right)]
    return tn(*both)


def store_sixteen(ref, row, value):
    ref[row : row + 16, :] = value


def value_grad_kernel(span, plan, info, hidden, grad_carried, keep, send, total):
    nz, plain = plan
    d, z, c = place(info, plain)
    width = total.shape[1]
    column = pl.ds(pl.multiple_of((pl.program_id(0) ^ d) * width, width), width)
    block = keep.shape[2]
    total[...] = over_own(hidden.at[:, :, column], grad_carried, span)
    for q in range(nz):
        for ref, core in ((keep, c), (send, 1 - c)):
            row = pl.multiple_of(((z ^ (q if plain else turn(core, q))) * 2 + core) * block, 8)
            ref[0, q] = total[pl.ds(row, block), :].astype(BF)


def gate_back_kernel(span, plan, info, ffn_gate_in, grad_gate, keep, send, total):
    total[...] = over_own(ffn_gate_in, grad_gate, span)
    scatter_rows(info, total, keep, send, plan, store_sixteen)


def inner_kernel(
    span, plan, info, hidden, grad_carried, ffn_in, key, whole_value, keep, send, grad_inner, grad_in, weights, total, sems
):
    step = pl.program_id(0)
    batches, _, width = grad_in.shape
    tiles = weights.shape[0] // 4
    last = step == tiles - 1

    def value_copy(j):
        block = pl.ds(4 * j, 4)
        return pltpu.make_async_copy(whole_value.at[block], weights.at[block], sems.at[j])

    def key_copy():
        return pltpu.make_async_copy(key, weights, sems.at[tiles])

    @pl.when(step == 0)
    def _():
        for j in range(tiles):
            value_copy(j).start()

    here = pl.multiple_of(step * width, width)
    for j in range(tiles):
        pl.when(step == j)(lambda: value_copy(j).wait())
    value = weights[pl.ds(4 * step, 4)].reshape(4 * weights.shape[1], width)
    for b in range(batches):
        back = nt(grad_carried[b], value)
        at = pl.ds(here, width)
        square = hidden[b, :, at].astype(F32)
        relu = square * lax.rsqrt(jnp.maximum(square, 1e-30))
        grad_inner[b, :, at] = (back * (2.0 * relu)).astype(BF)
    pl.when(last)(lambda: key_copy().start())
    total[...] = over_own(ffn_in, grad_inner.at[:, :, pl.ds(here, width)], span)
    scatter_rows(info, total, keep, send, plan, store_sixteen)

    @pl.when(last)
    def _():
        key_copy().wait()
        blocks = [weights[4 * j : 4 * j + 4].reshape(4 * weights.shape[1], width) for j in range(tiles)]
        right = jnp.concatenate(blocks, axis=1)
        for b in range(batches):
            grad_in[b] = nt(grad_inner[b], right).astype(BF)


def attend_back_kernel(
    span,
    seqs,
    info,
    grad_gate,
    grad_in,
    change,
    middle,
    stats,
    cotangent,
    by_num,
    by_recept,
    wkv,
    par,
    wo,
    wr,
    *refs,
):
    (grad_middle, grad_att, grad_recept, grad_num, grad_den, ends, state, sums, acc, held, back_gate, part_a, part_b) = refs
    batch = pl.program_id(0)
    bounds = bounds_of(info, batch, seqs)
    rows, width = middle.shape[1:]

    @pl.when(batch == 0)
    def _():
        acc[...] = jnp.zeros_like(acc)

    gain = par[7:8, :]
    mu, nu = par[9:10, :], par[10:11, :]
    total = bounds[-1]

    back_gate[...] = nt(grad_gate[0], wr[0])
    mean, scale = stats.at[0, 0], stats.at[0, 1]

    def normed_of(at):
        return (middle[0, at, :] - wide(mean[at, :], width)) * wide(scale[at, :], width)

    def gather(row, n, owned, carry):
        at = pl.ds(row, n)
        a, b = grad_in[0, at, :].astype(F32), back_gate[at, :]
        keep = keep_flag(positions(info, row, n), bounds, width)
        normed = normed_of(at)
        direct = a * mu + b * nu
        moved = (a + b - direct) * keep
        second = direct + up(moved, carry)
        if owned:
            diff = change[0, at, :].astype(F32)
            acc[0] += fold(second * normed)
            acc[1] += fold(second)
            acc[2] += fold(a * diff)
            acc[3] += fold(b * diff)
        inner = second * gain
        held[at, :] = inner
        part_a[at, :] = lanes(inner)
        part_b[at, :] = lanes(inner * normed)
        return moved[0:1]

    slabs(span, gather, jnp.zeros((1, width), F32), reverse=True)
    part_a[...] = row_mean(part_a, width)
    part_b[...] = row_mean(part_b, width)


    def apply(row, n, owned, carry):
        at = pl.ds(row, n)
        back = wide(scale[at, :], width) * (
            held[at, :] - wide(part_a[at, :], width) - normed_of(at) * wide(part_b[at, :], width)
        )
        live = flag(positions(info, row, n) < total, width)
        grad = cotangent[0, at, :].astype(F32) * live + back
        grad_middle[0, at, :] = grad
        grad_att[0, at, :] = grad.astype(BF)
        return carry

    cotangent = cotangent.ready()
    slabs(span, apply, 0)

    held[...] = nt(grad_att[0], wo[0])
    speed = jnp.exp(par[5:6, :])
    chunks = Chunks(info, bounds, rows, speed)
    size = chunks.size


    def point(row, n, owned, carry):
        at = pl.ds(row, n)
        back = held[at, :]
        num = back * by_num[0, at, :].astype(F32)
        den = num * wkv[0, at, :]
        for i in range(chunks.tiles):
            grad_num[0, i, at, :] = tile(num, i)
            grad_den[0, i, at, :] = -tile(den, i)
        grad_recept[0, at, :] = (back * by_recept[0, at, :].astype(F32)).astype(BF)
        return carry

    by_num, by_recept, wkv = by_num.ready(), by_recept.ready(), wkv.ready()
    slabs(span, point, 0)

    def step(j, carry, cut=False):
        nums, dens = carry
        at = chunks.at(j)
        keep = chunks.keep(j, 1)
        num_out, den_out = [], []
        for i in range(chunks.tiles):
            gn, gd = grad_num[0, i, at, :], grad_den[0, i, at, :]
            if cut:
                gn, gd = jnp.where(chunks.row8 == 7, 0.0, gn), jnp.where(chunks.row8 == 7, 0.0, gd)
            factor = chunks.rate[i] * keep
            num_out.append(factor * nums[i] + gn)
            den_out.append(factor * dens[i] + gd)
        return tuple(num_out), tuple(den_out)

    zero = tuple(jnp.zeros((8, 128), F32) for _ in range(chunks.tiles))
    after = PAD + span + 1 - 7 * size
    carry = (zero, zero)
    for j in reversed(range(after, size)):
        carry = step(j, carry, cut=True)
    carry = steps_of(PAD + 1, after, step, carry, reverse=True)
    inside = [join(c)[0:1] for c in carry]
    carry = steps_of(0, PAD + 1, step, carry, reverse=True, unroll=size)
    whole_ends = [join(c) for c in carry]
    out = []
    for k in range(2):
        ends[0, k] = whole_ends[k]
        line = whole_ends[k][7:8]
        for s in range(6, 0, -1):
            line = whole_ends[k][s : s + 1] + chunks.decay(s * size, (s + 1) * size, size) * line
        out.append(inside[k] + chunks.decay(PAD + 1, size, size - PAD - 1) * line)
    write_state(state, batch, *out)

    @pl.when(batch == pl.num_programs(0) - 1)
    def _():
        sums[...] = jnp.zeros_like(sums)
        for i in range(4):
            sums[i : i + 1, :] = jnp.sum(acc[i], axis=0, keepdims=True)


def recept_kernel(span, plan, info, gated, grad_att, mix_recept, grad_recept, keep, send, total):
    def grad(left, right):
        total[...] = over_own(left, right, span)
        scatter_rows(info, total, keep, send, plan, store_sixteen)

    pl.when(pl.program_id(0) == 0)(lambda: grad(gated, grad_att))
    pl.when(pl.program_id(0) == 1)(lambda: grad(mix_recept, grad_recept))


def again_kernel(span, seqs, ranks, parts, info, exp_key, value, ends, grad_recept, par, whole_a, *refs):
    states, (num_prev, den_prev, back_recept, wr, sems) = refs[:parts], refs[parts:]
    batch = pl.program_id(0)
    bounds = bounds_of(info, batch, seqs)
    chunks = Chunks(info, bounds, grad_recept.shape[1], jnp.exp(par[5:6, :]))

    def copy():
        return pltpu.make_async_copy(whole_a.at[2], wr, sems.at[0])

    pl.when(batch == 0)(lambda: copy().start())

    def emit(at, i, before_num, before_den, ek, x):
        num_prev[0, i, at, :] = before_num
        den_prev[0, i, at, :] = before_den

    forward_scan(info, states, batch, chunks, exp_key, value, ends, span, ranks, emit)
    pl.when(batch == 0)(lambda: copy().wait())
    back_recept[0] = nt(grad_recept[0], wr[...]).astype(BF)


def recur_back_kernel(
    span,
    seqs,
    ranks,
    parts,
    plan,
    info,
    grad_num,
    grad_den,
    exp_key,
    value,
    num_prev,
    den_prev,
    ends,
    mix_key,
    mix_value,
    par,
    *refs,
):
    states, refs = refs[:parts], refs[parts:]
    grad_key, grad_value, keep, send, sums, line_key, line_value, total, acc = refs
    batch = pl.program_id(0)
    bounds = bounds_of(info, batch, seqs)
    rows, width = mix_key.shape[1:]

    @pl.when(batch == 0)
    def _():
        acc[...] = jnp.zeros_like(acc)

    speed = jnp.exp(par[5:6, :])
    chunks = Chunks(info, bounds, rows, speed)
    size = chunks.size
    boost = chunks.split(jnp.exp(par[6:7, :]))
    entering = incoming(info, states, batch, bounds, speed, span, ranks, True)
    after = PAD + span + 1 - 7 * size
    begin = []
    for k in range(2):
        lines = [jnp.zeros((1, width), F32)]
        lines.append(ends[0, k, 7:8, :] + chunks.decay(7 * size, 7 * size + after, after) * entering[k])
        for s in range(6, 0, -1):
            lines.append(ends[0, k, s : s + 1, :] + chunks.decay(s * size, (s + 1) * size, size) * lines[-1])
        begin.append(jnp.concatenate(lines[::-1], axis=0))
    zero = tuple(jnp.zeros((8, 128), F32) for _ in range(chunks.tiles))
    carry = tuple(tuple(tile(b, i) for i in range(chunks.tiles)) for b in begin) + (zero, zero)

    def step(j, carry, insert=None, mask=None):
        nums, dens, bonuses, decays = carry
        at = chunks.at(j)
        keep_next = chunks.keep(j, 1)
        outs = ([], [], [], [])
        for i in range(chunks.tiles):
            gn, ek, v = grad_num[0, i, at, :], exp_key[0, i, at, :], value[0, i, at, :]
            gd = grad_den[0, i, at, :]
            after_num = keep_next * nums[i]
            after_den = keep_next * dens[i]
            bek = boost[i] * ek
            bonus = bek * (v * gn + gd)
            line_key[i, at, :] = bonus + ek * (v * after_num + after_den)
            line_value[i, at, :] = bek * gn + ek * after_num
            decay = num_prev[0, i, at, :] * after_num + den_prev[0, i, at, :] * after_den
            if mask is not None:
                bonus = jnp.where(mask, bonus, 0.0)
                decay = jnp.where(mask, decay, 0.0)
            if insert is not None:
                gn = jnp.where(chunks.row8 == 7, insert[0][i], gn)
                gd = jnp.where(chunks.row8 == 7, insert[1][i], gd)
            outs[0].append(chunks.rate[i] * after_num + gn)
            outs[1].append(chunks.rate[i] * after_den + gd)
            outs[2].append(bonuses[i] + bonus)
            outs[3].append(decays[i] + decay)
        return tuple(tuple(o) for o in outs)

    none = [[0.0] * chunks.tiles] * 2
    upper = chunks.row8 < 7
    for j in reversed(range(after + 1, size)):
        carry = step(j, carry, none, upper)
    carry = step(after, carry, [chunks.split(e) for e in entering], upper)
    edge = PAD + span - 7 * size
    for j in reversed(range(edge, after)):
        carry = step(j, carry, None, upper)
    carry = steps_of(PAD, edge, step, carry, reverse=True)
    lower = chunks.row8 > 0
    carry = steps_of(0, PAD, lambda j, c: step(j, c, None, lower), carry, reverse=True)
    acc[0] += join(carry[2])
    acc[1] += join(carry[3])

    def pack(row, n, owned, carry):
        at = pl.ds(row, n)
        grad_key[batch, at, :] = join([line_key[i, at, :] for i in range(chunks.tiles)]).astype(BF)
        grad_value[batch, at, :] = join([line_value[i, at, :] for i in range(chunks.tiles)]).astype(BF)
        return carry

    slabs(span, pack, 0)
    mix_key.ready(), mix_value.ready()

    @pl.when(batch == pl.num_programs(0) - 1)
    def _():
        sums[...] = jnp.zeros_like(sums)
        for i in range(2):
            sums[i : i + 1, :] = jnp.sum(acc[i], axis=0, keepdims=True)
        for left, right, low in ((mix_key, grad_key, 0), (mix_value, grad_value, width)):
            total[...] = over_own(left.buffer, right, span)

            def write(ref, row, value):
                ref[row : row + 16, low : low + width] = value

            scatter_rows(info, total, keep, send, plan, write)


def first_back_kernel(
    span,
    seqs,
    plan,
    info,
    grad_key,
    grad_value,
    back_recept,
    tokens,
    stats,
    change,
    sums,
    sums_back,
    par,
    whole_a,
    *refs,
):
    inners, part_ref, keep, send, weights, back_key, back_value, acc, turned, sems = refs
    part_a, part_b = part_ref.at[0, 0], part_ref.at[0, 1]
    batch = pl.program_id(0)
    bounds = bounds_of(info, batch, seqs)
    width = tokens.shape[2]

    def copies():
        return [pltpu.make_async_copy(whole_a.at[pl.ds(0, 2)], weights, sems.at[0])]

    @pl.when(batch == 0)
    def _():
        start_all(copies())
        acc[...] = jnp.zeros_like(acc)
        wait_all(copies())

    back_key[...] = nt(grad_key[0], weights[0])
    back_value[...] = nt(grad_value[0], weights[1])
    gain = par[0:1, :]
    mixes = (par[2:3, :], par[3:4, :], par[4:5, :])
    tokens, stats, change = tokens.ready(), stats.ready(), change.ready()
    mean, scale = stats.at[0, 0], stats.at[0, 1]

    def normed_of(at):
        return (tokens[0, at, :].astype(F32) - wide(mean[at, :], width)) * wide(scale[at, :], width)

    def gather(row, n, owned, carry):
        at = pl.ds(row, n)
        parts = (back_key[at, :], back_value[at, :], back_recept[0, at, :].astype(F32))
        keep = keep_flag(positions(info, row, n), bounds, width)
        direct = sum(g * mu for g, mu in zip(parts, mixes))
        moved = (parts[0] + parts[1] + parts[2] - direct) * keep
        if owned:
            normed = normed_of(at)
            first = direct + up(moved, carry)
            diff = change[0, at, :].astype(F32)
            acc[2] += fold(first * normed)
            acc[3] += fold(first)
            for i in range(3):
                acc[4 + i] += fold(parts[i] * diff)
            inner = first * gain
            inners[0, at, :] = inner
            part_a[at, :] = lanes(inner)
            part_b[at, :] = lanes(inner * normed)
        return moved[0:1]

    slabs(span, gather, jnp.zeros((1, width), F32), reverse=True)
    part_a[...] = row_mean(part_a, width)
    part_b[...] = row_mean(part_b, width)

    @pl.when(batch == pl.num_programs(0) - 1)
    def _():
        def final(i):
            return jnp.sum(acc[i], axis=0, keepdims=True)

        speed = jnp.exp(par[5:6, :])
        decay = sums_back[1:2, :] * jnp.exp(-speed) * -speed
        columns = [final(i) for i in (2, 3, 4, 5, 6)] + [decay, sums_back[0:1, :]]
        columns += [sums[i : i + 1, :] for i in range(4)]
        stacked = jnp.concatenate(columns + [jnp.zeros((128 - len(columns), width), F32)], axis=0)
        turned[...] = stacked.T
        scatter_rows(info, turned, keep, send, plan, store_sixteen)


def tokens_grad_kernel(span, info, inners, parts, tokens, stats, grad_middle, tokens_grad):
    width = inners.shape[2]
    mean, scale = stats.at[0, 0], stats.at[0, 1]
    part_a, part_b = parts.at[0, 0], parts.at[0, 1]

    def apply(row, n, owned, carry):
        if owned:
            at = pl.ds(row, n)
            rate = wide(scale[at, :], width)
            normed = (tokens[0, at, :].astype(F32) - wide(mean[at, :], width)) * rate
            back = rate * (inners[0, at, :] - wide(part_a[at, :], width) - normed * wide(part_b[at, :], width))
            tokens_grad[0, 0, pl.ds(row - PAD, n), :] = grad_middle[0, at, :] + back
        return carry

    slabs(span, apply, 0)


def swap(x, kind):
    devices, size = lax.axis_size("dp"), lax.axis_size("seq")
    if kind == "next":
        return lax.ppermute(x, "seq", [(i, i + 1) for i in range(size - 1)])
    if kind == "last":
        return lax.ppermute(x, "seq", [(i + 1, i) for i in range(size - 1)])
    if isinstance(kind, int):
        return lax.ppermute(x, "seq", [(i, i ^ kind) for i in range(size)])
    masks = {"xy": ((1, 0), (2, 0)), "yx": ((2, 0), (1, 0)), "over": ((3, 0), (3, 0)), "near": ((0, 2), (0, 4)), "far": ((0, 4), (0, 2))}
    pairs = []
    for d in range(devices):
        for s in range(size):
            over, along = masks[kind][s % 2]
            pairs.append((d * size + s, (d ^ over) * size + (s ^ along)))
    return lax.ppermute(x, ("dp", "seq"), pairs)


def add(terms):
    return sum(t.astype(F32) for t in terms)


def hold(x, deps):
    return lax.optimization_barrier((x,) + tuple(deps))[0] if deps else x


def launch(deps, *items):
    items = [item for item in items if item.sends()]
    sends = [s for item in items for s in item.sends()]
    if not sends:
        return list(deps)
    held = lax.optimization_barrier(tuple(s[0] for s in sends) + tuple(deps))
    came = [swap(x, kind) for x, (_, kind) in zip(held, sends)]
    left = list(came)
    for item in items:
        count = len(item.sends())
        item.receive(left[:count])
        left = left[count:]
    return came


class Gather:
    def __init__(self, blocks, core):
        self.core = core
        self.next = [(blocks, "xy")]
        self.stage = 0

    def sends(self):
        return self.next

    def receive(self, came):
        if self.stage == 0:
            self.pieces = came
            half = came[0].shape[1] // 2
            part = lax.dynamic_slice_in_dim(came[0], self.core * half, half, axis=1)
            self.next = [(part, "yx"), (came[0], 1)]
        elif self.stage == 1:
            self.pieces = self.pieces + [came[1], came[0]]
            self.next = [(came[0], 1)]
        else:
            self.pieces = self.pieces + came
            self.next = []
        self.stage += 1


class Table:
    def __init__(self, params, kinds):
        self.own = jnp.pad(params.T, ((0, 16 - params.shape[1]), (0, 0)))
        self.kinds = kinds

    def sends(self):
        return [(self.own, kind) for kind in self.kinds]

    def receive(self, came):
        self.came = came

    def whole(self, last):
        d = lax.axis_index("dp")
        first = lax.axis_index("seq") % 2 == 0
        a, b = self.came
        a = [self.own, jnp.where(first, a, b), jnp.where(first, b, a)] + last.came
        a = [jnp.where(d % 2 == 1, a[i ^ 1], a[i]) for i in range(4)]
        a = [jnp.where(d // 2 == 1, a[i ^ 2], a[i]) for i in range(4)]
        return jnp.concatenate(a, axis=1).astype(F32)


class States:
    def __init__(self, state):
        self.parts = [state]
        self.mask = 1

    def sends(self):
        return [(self.parts[0], self.mask)] if self.mask < lax.axis_size("seq") else []

    def receive(self, came):
        self.parts = self.parts + came
        self.mask *= 2
        if self.sends():
            self.parts = [jnp.concatenate(self.parts, axis=0)]


class Halo:
    def __init__(self, tokens, cotangent):
        span = tokens.shape[2]
        toks, cots = tokens[:, 0], cotangent[:, 0]
        self.next = [(toks[:, span - 2 :], "next"), (jnp.stack([toks[:, :2], cots[:, :2]]), "last")]

    def sends(self):
        return self.next

    def receive(self, came):
        before, after = came
        blank = jnp.zeros(after.shape[:2] + (PAD - 2,) + after.shape[3:], BF)
        before = jnp.stack([before, jnp.zeros_like(before)])
        self.rows = jnp.concatenate([blank, before, after, blank], axis=2)


class Core:
    def __init__(self, keep, send, plain):
        self.keep, self.send, self.plain = keep, send, plain

    def sends(self):
        return [] if self.plain else [(self.send, 1)]

    def receive(self, came):
        self.terms = [self.keep, came[0]]

    def whole(self):
        full = jnp.stack([self.keep, self.send], axis=1).reshape(-1, self.keep.shape[-1]).astype(F32)
        return lax.psum_scatter(full, ("dp", "seq"), scatter_dimension=0, tiled=True)


class Quarter:
    def __init__(self, *cores):
        self.cores = cores
        self.rows = cores[0].keep.shape[1]
        self.plain = cores[0].plain
        self.came = []

    def value(self, p, rows=slice(None)):
        return jnp.concatenate([add([t[p, rows] for t in c.terms]) for c in self.cores], axis=-1)

    def sends(self):
        if self.plain or len(self.came) == 2:
            return []
        if not self.came:
            return [(self.value(slice(2, 4)).astype(BF), "xy")]
        return [((self.value(1) + self.came[0][1].astype(F32)).astype(BF), "yx")]

    def receive(self, came):
        self.came += came

    def final(self, low, high):
        rows = slice(low * self.rows // 4, high * self.rows // 4)
        return self.value(0, rows) + self.came[0][0, rows].astype(F32) + self.came[1][rows].astype(F32)

    def second(self, came):
        return came[came.shape[0] // 2 :]


class TallQuarter(Quarter):
    def value(self, p, rows=slice(None)):
        return jnp.concatenate([add([t[p] for t in c.terms]) for c in self.cores], axis=-2)

    def final(self, low, high):
        out, base = [], 0
        for c in self.cores:
            count = c.keep.shape[1]
            rows = slice(low * count // 4, high * count // 4)
            near = slice(base + rows.start, base + rows.stop)
            came = self.came[0][0, near].astype(F32) + self.came[1][near].astype(F32)
            out.append(add([t[0, rows] for t in c.terms]) + came)
            base += count
        return jnp.concatenate(out, axis=0)

    def second(self, came):
        out, base = [], 0
        for c in self.cores:
            count = c.keep.shape[1] // 4
            out.append(came[base + count : base + 2 * count])
            base += 2 * count
        return jnp.concatenate(out, axis=0)

    def first(self, came):
        out, base = [], 0
        for c in self.cores:
            count = c.keep.shape[1] // 4
            out.append(came[base : base + count])
            base += 2 * count
        return jnp.concatenate(out, axis=0)


class SmallQuarter(Quarter):
    def sends(self):
        if self.plain or self.came:
            return []
        return [(self.value(p).astype(BF), kind) for p, kind in ((2, "xy"), (1, "yx"), (3, "over"))]

    def final(self, low, high):
        rows = slice(low * self.rows // 4, high * self.rows // 4)
        return self.value(0, rows) + add([t[rows] for t in self.came])


class Finish:
    def __init__(self, *quarters):
        self.quarters = quarters
        self.plain = quarters[0].plain
        self.came = []
        if self.plain:
            axis = -2 if isinstance(quarters[0], TallQuarter) else -1
            self.total = jnp.concatenate([c.whole() for q in quarters for c in q.cores], axis=axis)

    def value(self, low, high):
        return jnp.concatenate([q.final(low, high) for q in self.quarters], axis=-1)

    def sends(self):
        if self.plain or len(self.came) == 2:
            return []
        if not self.came:
            return [(self.value(2, 4).astype(BF), "near")]
        part = self.quarters[0].second(self.came[0])
        return [((self.value(1, 2) + part.astype(F32)).astype(BF), "far")]

    def receive(self, came):
        self.came += came
        if len(self.came) == 2:
            near = self.came[0]
            first = self.quarters[0]
            near = first.first(near) if isinstance(first, TallQuarter) else near[: near.shape[0] // 2]
            self.total = self.value(0, 1) + near.astype(F32) + self.came[1].astype(F32)


ANY = pl.BlockSpec(memory_space=pl.ANY)
SMEM = pl.BlockSpec(memory_space=pltpu.SMEM)


def shape(s, dtype):
    return jax.ShapeDtypeStruct(s, dtype)


BATCH = "batch"
LATE = "late"
HELD = "held"
VMEM = pl.BlockSpec(memory_space=pltpu.VMEM)


def call(name, kernel, grid, ins, outs, scratch, mib, deps=(), aliases=None, prefetch=False):
    ins = [(hold(ins[0][0], deps), ins[0][1])] + ins[1:]
    views = [i for i, (_, spec) in enumerate(ins + outs) if spec is BATCH]
    lates = [i for i, (_, spec) in enumerate(ins) if spec is LATE]
    extra = [pltpu.VMEM(ins[i][0].shape, ins[i][0].dtype) for i in lates]
    if lates:
        extra.append(pltpu.SemaphoreType.DMA((len(lates), grid[0])))

    def run(*refs):
        refs = list(refs)
        if lates:
            held, sems = refs[-len(extra) : -1], refs[-1]
            refs = refs[: -len(extra)]
            for k, i in enumerate(lates):
                refs[i] = Late(refs[i], held[k], sems, k)

            @pl.when(pl.program_id(0) == 0)
            def _():
                for b in range(grid[0]):
                    for i in lates:
                        refs[i].copy(b).start()

        for i in views:
            refs[i] = refs[i].at[pl.ds(pl.program_id(0), 1)]
        kernel(*refs)

    specs = {id(BATCH): VMEM, id(LATE): ANY, id(HELD): ANY}
    held = (LATE, HELD)
    operands = [pltpu.with_memory_space_constraint(a, pltpu.HBM) if any(s is h for h in held) else a for a, s in ins]
    grid_spec = pltpu.PrefetchScalarGridSpec(
        num_scalar_prefetch=1 if prefetch else 0,
        grid=grid,
        in_specs=[specs.get(id(s), s) for _, s in ins[1 if prefetch else 0 :]],
        out_specs=[specs.get(id(s), s) for _, s in outs],
        scratch_shapes=list(scratch) + extra,
    )
    return pl.pallas_call(
        run,
        grid_spec=grid_spec,
        out_shape=[a for a, _ in outs],
        input_output_aliases=aliases or {},
        compiler_params=pltpu.CompilerParams(vmem_limit_bytes=mib * 2**20),
        name=name,
    )(*operands)


def body(
    tokens,
    cotangent,
    lengths,
    att_key,
    att_value,
    att_recept,
    att_out,
    ffn_key,
    ffn_value,
    ffn_recept,
    params,
):
    batches, _, span, width = tokens.shape
    seqs = lengths.shape[2]
    ff = ffn_key.shape[1]
    tiles = ff // width
    ranks = lax.axis_size("seq")
    rows = span + 2 * PAD
    d, s = lax.axis_index("dp"), lax.axis_index("seq")
    core = s % 2
    at = lax.iota(jnp.int32, HEAD + batches * seqs)
    info = jnp.pad(lengths.reshape(batches * seqs), (HEAD, 0))
    for i, number in enumerate((s * span, d, s, core)):
        info = jnp.where(at == i, number, info)
    shard = att_key.shape[0]
    group_a = Gather(jnp.stack([att_key, att_value, att_recept, att_out]), core)
    group_b = Gather(jnp.stack([ffn_key[:, j * width : (j + 1) * width] for j in range(tiles)]), core)
    group_c = Gather(jnp.concatenate([ffn_value.reshape(-1, shard, width), ffn_recept[None]], axis=0), core)
    table, last_table = Table(params, ("xy", "yx")), Table(params, ("over",))

    edge = Halo(tokens, cotangent)
    came = launch((), group_a) + launch([info], edge, table)
    over = launch([info], last_table)
    halo = edge.rows
    par = table.whole(last_table)

    ext = (batches, rows, width)
    ext_f, ext_b = shape(ext, F32), shape(ext, BF)
    line_f = shape((batches, width // 128, rows, 128), F32)
    stats_shape = shape((batches, 2, rows, 128), F32)
    ends_shape = shape((batches, 2, 8, width), F32)
    wide_b = shape((batches, rows, ff), BF)
    square = pltpu.VMEM((1, width, width), BF)
    three = pltpu.VMEM((3, width, width), BF)
    square_f = pltpu.VMEM((width, width), F32)
    block_f = pltpu.VMEM((rows, width), F32)
    block_line = pltpu.VMEM((width // 128, rows, 128), F32)
    part = pltpu.VMEM((rows, 128), F32)

    def sems(n):
        return pltpu.SemaphoreType.DMA((n,))

    def refs(group):
        return [(p, ANY) for p in group.pieces]

    info_in = (info, SMEM)

    deps = launch(came, group_a)
    far = launch(deps + over, group_b)
    near = launch(deps, group_a)
    mix_key, mix_value, mix_recept, change_one, tok_ext, cot_ext, stats_one = call(
        "mix",
        functools.partial(mix_kernel, span, seqs),
        (batches,),
        [
            info_in,
            (tokens, pl.BlockSpec((1,) + tokens.shape[1:], lambda i: (i, 0, 0, 0))),
            (cotangent, pl.BlockSpec((1,) + tokens.shape[1:], lambda i: (i, 0, 0, 0))),
            (halo, pl.BlockSpec((2, 1, 2 * PAD, width), lambda i: (0, i, 0, 0))),
            (par, VMEM),
        ],
        [(ext_b, BATCH)] * 6 + [(stats_shape, BATCH)],
        [block_f],
        13,
        deps,
    )
    deps = near
    state_shape = shape((2 * batches, width), F32)
    exp_key, value, gate_one, ends, state, whole_a = call(
        "project",
        functools.partial(project_kernel, span, seqs),
        (batches,),
        [info_in]
        + [(a, BATCH) for a in (mix_key, mix_value, mix_recept)]
        + [(par, VMEM), (att_key, ANY), (att_value, ANY), (att_recept, ANY)]
        + refs(group_a),
        [(line_f, BATCH)] * 3
        + [(ends_shape, BATCH), (state_shape, VMEM), (pltpu.HBM((3, width, width), BF), ANY)],
        [three, sems(PER + 3)],
        10,
        deps,
    )
    exchange = States(state)
    came = launch([state], exchange)
    far = launch(far + came, group_b)
    came = launch(came, exchange)
    deps = came + far
    far = launch(deps, group_b)
    after = launch(deps, group_c)
    while exchange.sends():
        came = launch(came, exchange)
    states = exchange.parts
    deps = came + far
    came = after
    gated, by_num, by_recept, wkv, middle, ffn_in, ffn_gate_in, change_two, stats_two, whole_out = call(
        "recur",
        functools.partial(recur_kernel, span, seqs, ranks, len(states)),
        (batches,),
        [info_in]
        + [(a, BATCH) for a in (exp_key, value, gate_one)]
        + [(ends, BATCH), (tok_ext, BATCH)]
        + [(par, VMEM), (att_out, ANY)]
        + [(a, VMEM) for a in states]
        + refs(group_a),
        [
            (a, BATCH)
            for a in (ext_b, ext_b, ext_b, ext_f, ext_f, ext_b, ext_b, ext_b, stats_shape)
        ]
        + [(pltpu.HBM((1, width, width), BF), ANY)],
        [square, block_line, block_line, sems(PER + 1)],
        10,
        deps,
    )
    deps = came + [stats_two]
    came = launch(deps, group_c)
    key_buf = pltpu.VMEM((tiles, width, width), BF)
    own_value = ffn_value.reshape(4, shard, width)
    hidden, whole_key = call(
        "hidden",
        hidden_kernel,
        (batches,),
        [info_in, (ffn_in, BATCH), (ffn_key, ANY)] + refs(group_b),
        [(wide_b, BATCH), (pltpu.HBM((tiles, width, width), BF), ANY)],
        [key_buf, sems(tiles + PER + 1)],
        11,
        deps,
    )
    came = launch(came + [hidden], group_c)
    mixed_shape = shape((batches, 1, span, width), BF)
    value_buf = pltpu.VMEM((4 * tiles, shard, width), BF)
    mixed, grad_carried, grad_gate, whole_value, whole_gate = call(
        "gate",
        functools.partial(gate_kernel, span, seqs),
        (batches,),
        [info_in]
        + [(a, BATCH) for a in (hidden, ffn_gate_in, middle, cot_ext)]
        + [(own_value, ANY), (ffn_recept, ANY)]
        + refs(group_c),
        [(mixed_shape, BATCH)]
        + [(ext_b, BATCH)] * 2
        + [(pltpu.HBM(value_buf.shape, BF), ANY), (pltpu.HBM((1, width, width), BF), ANY)],
        [value_buf, square, sems(2 * PER + 2)],
        19,
        came,
    )

    plain = ranks != 8 or (width // (4 * ranks)) % 8 != 0
    nz = 1 if plain else 4
    plan = (nz, plain)

    def core_of(keep, send):
        return Core(*(a.reshape(4, -1, a.shape[-1]) for a in (keep, send)), plain)

    big = pltpu.HBM((4, nz, ff // (8 * nz), width), BF)
    big_kept = shape(big.shape, BF)

    def place_of(other):
        def index(i, info):
            core = (info[3] + other) % 2
            return (i if plain else turn(core, i), 0, 0, 0)

        return pl.BlockSpec((1,) + big.shape[1:], index)

    keep_v, send_v = call(
        "value_grad",
        functools.partial(value_grad_kernel, span, plan),
        (4,),
        [info_in, (hidden, VMEM), (grad_carried, VMEM)],
        [(big_kept, place_of(0)), (big, place_of(1))],
        [square_f],
        10,
        prefetch=True,
    )
    core_value = core_of(keep_v, send_v)
    deps = [keep_v]
    came = launch(deps, core_value)
    wide_half = pltpu.HBM((width // 2, ff), BF)
    wide_kept = shape(wide_half.shape, BF)
    one = pltpu.HBM((width // 2, width), BF)
    one_kept = shape(one.shape, BF)
    keep_g, send_g = call(
        "gate_back",
        functools.partial(gate_back_kernel, span, plan),
        (1,),
        [info_in, (ffn_gate_in, VMEM), (grad_gate, VMEM)],
        [(one_kept, VMEM), (one, VMEM)],
        [square_f],
        10,
        deps,
    )
    core_gate = core_of(keep_g, send_g)
    deps = came + launch([keep_g], core_gate)
    sum_value = TallQuarter(core_value, core_gate)
    came = launch(deps, sum_value)
    out_tile = pl.BlockSpec((width // 2, width), lambda i: (0, i))
    keep_k, send_k, _, grad_in = call(
        "inner",
        functools.partial(inner_kernel, span, plan),
        (tiles,),
        [
            info_in,
            (hidden, VMEM),
            (grad_carried, VMEM),
            (ffn_in, VMEM),
            (whole_key.reshape(value_buf.shape), HELD),
            (whole_value, HELD),
        ],
        [(wide_kept, out_tile), (wide_half, out_tile)] + [(pltpu.VMEM(wide_b.shape, BF), VMEM), (ext_b, VMEM)],
        [
            value_buf,
            square_f,
            sems(tiles + 1),
        ],
        20,
        deps,
        {1: 2},
    )
    core_key = core_of(keep_k, send_k)
    deps = came + [grad_in]
    came = launch(deps, sum_value, core_key)
    sums_shape = shape((8, width), F32)
    grad_middle, grad_att, grad_recept, grad_num, grad_den, ends_back, state_back, sums = call(
        "attend_back",
        functools.partial(attend_back_kernel, span, seqs),
        (batches,),
        [info_in]
        + [
            (a, LATE if a is cot_ext or a is by_num or a is by_recept or a is wkv else BATCH)
            for a in (
                grad_gate,
                grad_in,
                change_two,
                middle,
                stats_two,
                cot_ext,
                by_num,
                by_recept,
                wkv,
            )
        ]
        + [(par, VMEM), (whole_out, VMEM), (whole_gate, VMEM)],
        [(a, BATCH) for a in (ext_f, ext_b, ext_b, pltpu.VMEM(line_f.shape, F32), pltpu.VMEM(line_f.shape, F32))]
        + [(ends_shape, BATCH)]
        + [(state_shape, VMEM), (sums_shape, VMEM)],
        [pltpu.VMEM((4, 8, width), F32), block_f, block_f, part, part],
        18,
        deps,
    )
    exchange = States(state_back)
    sum_key = Quarter(core_key)
    all_value = Finish(sum_value)
    came = launch(came + [state_back], exchange)
    deps = came
    came = launch(came, exchange, sum_key)
    came, far = came[:1], came[1:]
    two = pltpu.HBM((width // 2, 2 * width), BF)
    two_kept = shape(two.shape, BF)
    keep_o, send_o = call(
        "recept",
        functools.partial(recept_kernel, span, plan),
        (2,),
        [info_in] + [(a, VMEM) for a in (gated, grad_att, mix_recept, grad_recept)],
        [(a, pl.BlockSpec((width // 2, width), lambda i: (0, i))) for a in (two_kept, two)],
        [square_f],
        10,
        deps,
    )
    core_out = core_of(keep_o, send_o)
    deps = came + [keep_o]
    came = launch(deps, exchange)
    num_prev, den_prev, back_recept = call(
        "again",
        functools.partial(again_kernel, span, seqs, ranks, len(states)),
        (batches,),
        [info_in]
        + [(a, BATCH) for a in (exp_key, value, ends, grad_recept)]
        + [(par, VMEM), (whole_a, HELD)]
        + [(a, VMEM) for a in states],
        [(line_f, BATCH)] * 2 + [(ext_b, BATCH)],
        [pltpu.VMEM((width, width), BF), sems(1)],
        8,
        deps,
    )
    while exchange.sends():
        came = launch(came, exchange)
    states_back = exchange.parts
    deps = came + far + [back_recept]
    came = launch(deps, all_value, sum_key, core_out)
    grad_key, grad_value, keep_l, send_l, sums_back = call(
        "recur_back",
        functools.partial(recur_back_kernel, span, seqs, ranks, len(states_back), plan),
        (batches,),
        [info_in]
        + [
            (a, LATE if a is mix_key or a is mix_value else BATCH)
            for a in (
                grad_num,
                grad_den,
                exp_key,
                value,
                num_prev,
                den_prev,
                ends_back,
                mix_key,
                mix_value,
            )
        ]
        + [(par, VMEM)]
        + [(a, VMEM) for a in states_back],
        [(ext_b, VMEM)] * 2 + [(two_kept, VMEM), (two, VMEM)] + [(sums_shape, VMEM)],
        [block_line, block_line, square_f, pltpu.VMEM((2, 8, width), F32)],
        18,
        deps,
    )
    core_last = core_of(keep_l, send_l)
    deps = launch(came + [sums_back], core_last)
    all_key = Finish(sum_key)
    sum_last = Quarter(core_last, core_out)
    came = launch(deps, all_key, sum_last, all_value)
    grad_shape = shape((batches, 1, span, width), F32)
    half_table = shape((width // 2, 128), BF)
    inners, parts, keep_p, send_p = call(
        "first_back",
        functools.partial(first_back_kernel, span, seqs, plan),
        (batches,),
        [info_in]
        + [(a, BATCH) for a in (grad_key, grad_value, back_recept)]
        + [(a, LATE) for a in (tok_ext, stats_one, change_one)]
        + [(sums, VMEM), (sums_back, VMEM), (par, VMEM)]
        + [(whole_a, HELD)],
        [(ext_f, BATCH), (stats_shape, BATCH)] + [(half_table, VMEM)] * 2,
        [
            pltpu.VMEM((2, width, width), BF),
            block_f,
            block_f,
            pltpu.VMEM((7, 8, width), F32),
            pltpu.VMEM((width, 128), F32),
            sems(1),
        ],
        18,
        deps,
    )
    core_table = core_of(keep_p, send_p)
    deps = launch(came + [keep_p], core_table)
    sum_table = SmallQuarter(core_table)
    came = launch(deps, sum_last, sum_table, all_key)
    (tokens_grad,) = call(
        "tokens_grad",
        functools.partial(tokens_grad_kernel, span),
        (batches,),
        [info_in] + [(a, BATCH) for a in (inners, parts, tok_ext, stats_one, grad_middle)],
        [(grad_shape, BATCH)],
        [],
        7,
        deps,
    )
    all_last = Finish(sum_last, sum_table)
    came = launch(came + [tokens_grad], all_last)
    launch(came, all_last)
    key, last = all_key.total, all_last.total
    cut = ff // (4 * ranks)
    return (
        mixed,
        tokens_grad,
        last[:, :width],
        last[:, width : 2 * width],
        last[:, 3 * width : 4 * width],
        last[:, 2 * width : 3 * width],
        key,
        all_value.total[:cut],
        all_value.total[cut:],
        last[:, 4 * width : 4 * width + params.shape[1]],
    )


def solution(mesh):
    split = P(("dp", "seq"), None)
    rows = P("dp", None)
    stream = P(None, "dp", "seq", None)
    return jax.shard_map(
        body,
        mesh=mesh,
        in_specs=(stream, stream, P(None, "dp", None)) + (rows,) * 8,
        out_specs=(stream, stream) + (split,) * 8,
        check_vma=False,
    )
```
